32 devices in a mesh: grp: 2 (over core), lat: 16 (over z, y, x).
Axes of the slice: x: 2, y: 2, z: 4, core: 2. Of those that a mesh axis runs over, the one named last changes fastest.
Arguments:
- spectral_state: bfloat16 [2, 640, 64, 640], P('grp', 'lat'), may hold values from -6 to 6
- cotangent: bfloat16 [2, 640, 64, 640], P('grp', 'lat'), may hold values from -6 to 6
- legendre: bfloat16 [640, 640, 128], P('lat'), as said below
- quadrature: float32 [128], replicated, may hold values from 0.2 to 1
- damping: float32 [32], replicated, may hold values from 0.05 to 20
- physics_in: bfloat16 [512, 32], replicated, may hold values from -1 to 1
- physics_bias: float32 [512], replicated, may hold values from -3 to 3
- physics_out: bfloat16 [32, 512], replicated, may hold values from -0.25 to 0.25
Outputs:
- grad_state: float32 [2, 640, 64, 640], P('grp', 'lat')
- grad_in: float32 [512, 32], replicated
- grad_bias: float32 [512], replicated
- grad_out: float32 [32, 512], replicated
The draws below stay inside these ranges and needn't reach their ends.
Inputs may be any that keep to these rules, and one draw needn't show every extreme that they name: legendre[m, l, p] is zero for every degree l below the wavenumber m, and generally nonzero otherwise.
All inputs are finite; a program needn't handle non-finite values.
Results may differ from the reference program's by a relative error of at most 0.015.
Values may be sent and summed in bfloat16 or wider, within the bound.
No kernel may reach another device: no remote copies, remote signals or barrier semaphores. Data moves between devices by JAX's collectives and lax.ppermute only.
A program may use at most 192 MiB of HBM per device.

```python
import math
import jax
import jax.numpy as jnp
from jax import lax

M = 640
L = 640
NLON = 2560
HID = 512
C = 32
NLAT = 128
ROLLOUTS = 2
N_GRP = 2


def draw_legendre(key, part):
    key = jax.random.fold_in(key, 11)
    values = jax.random.uniform(key, (M, L, NLAT), jnp.float32, -1.7320508, 1.7320508)
    wave = jnp.arange(M, dtype=jnp.int32)[:, None]
    degree = jnp.arange(L, dtype=jnp.int32)[None, :]
    live = (degree >= wave).astype(jnp.float32)
    count = (L - jnp.arange(M, dtype=jnp.int32)).astype(jnp.float32)
    scale = 1.0 / jnp.sqrt(count)
    return (values * live[:, :, None] * scale[:, None, None]).astype(jnp.bfloat16)


def block_scale(rng, extent, split, smallest, top_value):
    loudness = 1.0
    for position, parts in split:
        draws = jax.random.uniform(jax.random.fold_in(jax.random.fold_in(rng, 6), position), (parts,), jnp.float32, smallest / len(split), top_value / len(split))
        loudness = loudness * jnp.repeat(jnp.exp(draws), extent[position] // parts).reshape((-1,) + (1,) * (len(extent) - 1 - position))
    return loudness


def centred(stream_key, extent, width, reach, cuts=(), kind=jnp.bfloat16):
    drawn = width * jax.random.normal(stream_key, extent, jnp.float32)
    if cuts:
        drawn = drawn * block_scale(stream_key, extent, cuts, -0.22, 0.18)
    return jnp.clip(drawn, -reach, reach).astype(kind)


def setup_inputs(seed: int = 0) -> dict:
    keys = jax.random.split(jax.random.key(seed), 9)
    return {
        "spectral_state": centred(keys[0], (ROLLOUTS, M, 2 * C, L), 1.0, 6.0, ((0, 2), (1, 16))),
        "cotangent": centred(keys[1], (ROLLOUTS, M, 2 * C, L), 1.0, 6.0, ((0, 2), (1, 16))),
        "legendre": draw_legendre(jax.random.fold_in(keys[8], 71), 0),
        "quadrature": jnp.clip(jax.random.uniform(keys[3], (NLAT,), jnp.float32, 0.2, 1.0), 0.2, 1.0),
        "damping": jnp.clip(jnp.exp(jax.random.uniform(keys[4], (C,), jnp.float32, math.log(0.05), math.log(20.0))), 0.05, 20.0),
        "physics_in": centred(keys[5], (HID, C), C ** -0.5, 1.0),
        "physics_bias": centred(keys[6], (HID,), 0.5, 3.0, (), jnp.float32),
        "physics_out": centred(keys[7], (C, HID), HID ** -0.5, 0.25),
    }


def implicit_factor(damping):
    degree = jnp.arange(L, dtype=jnp.float32)
    ratio = degree * (degree + 1.0) / (L * (L + 1.0))
    factor = 1.0 / (1.0 + damping[:, None] * ratio[None, :])
    return jnp.concatenate([factor, factor], axis=0)

def to_grid(fourier):
    values = fourier.astype(jnp.float32)
    chans = values.shape[1] // 2
    packed = lax.complex(values[:, :chans, :], values[:, chans:, :])
    padded = jnp.zeros((NLON, chans, values.shape[2]), packed.dtype).at[:M].set(packed)
    grid = jnp.real(jnp.fft.ifft(padded, axis=0)) * (NLON * math.sqrt(2.0 / NLON))
    return jnp.transpose(grid, (1, 2, 0))

def from_grid(grid):
    spectrum = jnp.fft.fft(grid, axis=2)[:, :, :M] * math.sqrt(2.0 / NLON)
    stacked = jnp.concatenate([jnp.real(spectrum), jnp.imag(spectrum)], axis=0)
    return jnp.transpose(stacked, (2, 0, 1))

def column_physics(physics_in, physics_bias, physics_out, inputs, tendency):
    hidden = jnp.dot(physics_in, inputs, preferred_element_type=jnp.float32) + physics_bias[:, None]
    sigma = jax.nn.sigmoid(hidden)
    activated = (hidden * sigma).astype(jnp.bfloat16)
    upstream = jnp.dot(physics_out.T, tendency, preferred_element_type=jnp.float32)
    slope = sigma * (1.0 + hidden * (1.0 - sigma))
    pre_grad = (upstream * slope).astype(jnp.bfloat16)
    grad_out = jnp.dot(tendency, activated.T, preferred_element_type=jnp.float32)
    grad_in = jnp.dot(pre_grad, inputs.T, preferred_element_type=jnp.float32)
    grad_bias = lax.optimization_barrier(jnp.sum(pre_grad.astype(jnp.float32), axis=1))
    grid_grad = jnp.dot(physics_in.T, pre_grad, preferred_element_type=jnp.float32).astype(jnp.bfloat16)
    return (grid_grad, grad_in, grad_bias, grad_out)

def reference(spectral_state, cotangent, legendre, quadrature, damping, physics_in, physics_bias, physics_out):
    factor = implicit_factor(damping)
    table = legendre.astype(jnp.float32)

    def one_rollout(pair):
        spectral, cot_in = pair
        direct = cot_in.astype(jnp.float32) * factor[None]
        cot_tend = direct.astype(jnp.bfloat16)
        fourier_state = jnp.einsum('mkl,mlf->mkf', spectral.astype(jnp.float32), table).astype(jnp.bfloat16)
        fourier_cot = (jnp.einsum('mkl,mlf->mkf', cot_tend.astype(jnp.float32), table) * quadrature[None, None, :]).astype(jnp.bfloat16)
        grid_state = to_grid(fourier_state).astype(jnp.bfloat16)
        grid_tend = to_grid(fourier_cot).astype(jnp.bfloat16)

        def per_row(carry, row):
            grid_row, part_in, part_bias, part_out = column_physics(physics_in, physics_bias, physics_out, row[0], row[1])
            return ((carry[0] + part_in, carry[1] + part_bias, carry[2] + part_out), grid_row)
        start = (jnp.zeros((HID, C), jnp.float32), jnp.zeros((HID,), jnp.float32), jnp.zeros((C, HID), jnp.float32))
        sums, rows = lax.scan(per_row, start, (jnp.transpose(grid_state, (1, 0, 2)), jnp.transpose(grid_tend, (1, 0, 2))))
        grid_grad = jnp.transpose(rows, (1, 0, 2))
        fourier_grad = from_grid(grid_grad.astype(jnp.float32)).astype(jnp.bfloat16)
        grad_state = direct + jnp.einsum('mkf,mlf->mkl', fourier_grad.astype(jnp.float32), table)
        return (grad_state, sums[0], sums[1], sums[2])
    grad_state, grad_in, grad_bias, grad_out = lax.map(one_rollout, (spectral_state, cotangent))
    scale = 1.0 / math.sqrt(N_GRP * NLAT * NLON)
    return (grad_state, lax.optimization_barrier(jnp.sum(grad_in, axis=0)) * scale, lax.optimization_barrier(jnp.sum(grad_bias, axis=0)) * scale, lax.optimization_barrier(jnp.sum(grad_out, axis=0)) * scale)
```

```python
import functools
import math

import jax
import jax.numpy as jnp
import numpy as np
import ml_dtypes
from jax import lax
from jax.experimental import pallas as pl
from jax.experimental.pallas import tpu as pltpu
from jax.sharding import PartitionSpec as P

NLON = 2560
VMEM = 56 * 1024 * 1024
F32 = jnp.float32
BF16 = jnp.bfloat16


def implicit_factor(damping, degrees):
    degree = jnp.arange(degrees, dtype=jnp.float32)
    ratio = degree * (degree + 1.0) / (degrees * (degrees + 1.0))
    factor = 1.0 / (1.0 + damping[:, None] * ratio[None, :])
    return jnp.concatenate([factor, factor], axis=0)


def longitude_table(waves, points):
    phase = np.arange(waves)[:, None] * np.arange(points)[None, :] % points
    angle = phase * (2.0 * math.pi / points)
    scale = math.sqrt(2.0 / points)
    both = np.concatenate([np.cos(angle) * scale, -np.sin(angle) * scale])
    return both.astype(np.float32).astype(ml_dtypes.bfloat16)


def dot(a, b):
    return jnp.dot(a, b, preferred_element_type=F32)


def dot_nt(a, b):
    return lax.dot_general(a, b, (((1,), (1,)), ((), ())), preferred_element_type=F32)


def params(grid_dims=1):
    return pltpu.CompilerParams(
        vmem_limit_bytes=VMEM, dimension_semantics=("arbitrary",) * grid_dims
    )


def steps_of(waves):
    for size in (4, 2, 1):
        if waves % size == 0:
            return size


def forward_kernel(ranks, quarter, spec, cot, leg, factor, quad, out, rows):
    block, width, _ = spec.shape
    chans = width // 2
    lat = leg.shape[2]
    own = rows.shape[0] // lat
    step = pl.program_id(0)
    for i in range(block):
        tend = (cot[i].astype(F32) * factor[...]).astype(BF16)
        stacked = jnp.concatenate(
            [spec[i, :chans], tend[:chans], spec[i, chans:], tend[chans:]], axis=0
        )
        res = dot(stacked, leg[i])
        weight = quad[...]
        res = jnp.concatenate(
            [
                res[:chans],
                res[chans : 2 * chans] * weight,
                res[2 * chans : 3 * chans],
                res[3 * chans :] * weight,
            ],
            axis=0,
        )
        rows[pl.ds(step * block + i, lat, stride=own), :] = res.T

    @pl.when(step == pl.num_programs(0) - 1)
    def _():
        size = quarter * own
        for d in range(ranks):
            for half in range(2):
                start = (half * ranks + d) * size
                out[d, half * size : (half + 1) * size, :] = rows[start : start + size, :].astype(
                    BF16
                )


def forward(spectral, cot, legendre, factor, quad, ranks):
    own, width, degrees = spectral.shape
    lat = legendre.shape[2]
    quarter = lat // ranks // 2
    block = steps_of(own)
    return pl.pallas_call(
        functools.partial(forward_kernel, ranks, quarter),
        grid=(own // block,),
        in_specs=[
            pl.BlockSpec((block, width, degrees), lambda i: (i, 0, 0)),
            pl.BlockSpec((block, width, degrees), lambda i: (i, 0, 0)),
            pl.BlockSpec((block, degrees, lat), lambda i: (i, 0, 0)),
            pl.BlockSpec((width, degrees), lambda i: (0, 0)),
            pl.BlockSpec((1, lat), lambda i: (0, 0)),
        ],
        out_specs=pl.BlockSpec((ranks, 2 * quarter * own, 2 * width), lambda i: (0, 0, 0)),
        out_shape=jax.ShapeDtypeStruct((ranks, 2 * quarter * own, 2 * width), BF16),
        scratch_shapes=[pltpu.VMEM((lat * own, 2 * width), F32)],
        compiler_params=params(),
        name="legendre_forward",
    )(spectral, cot, legendre, factor, quad)


def column_kernel(
    ranks, own, arrived, table, w_in, bias, w_out, out, fourier, cols, weights, w_in_t, acts, grid, modes, sums
):
    hid, chans = w_in.shape
    waves = ranks * own
    lat_rows = arrived.shape[1] // own
    quarter = lat_rows // 2
    size = table.shape[1]
    step = pl.program_id(0)

    @pl.when(step == 0)
    def _():
        for p in range(lat_rows):
            piece = jnp.concatenate(
                [arrived[s, p * own : (p + 1) * own, :] for s in range(ranks)], axis=0
            ).T
            row = 2 * chans * p
            fourier[row : row + 2 * chans, :waves] = piece[: 2 * chans]
            fourier[row : row + 2 * chans, waves:] = piece[2 * chans :]
        cols[2 * chans :, :] = jnp.ones((16, cols.shape[1]), BF16)
        first = bias[...] * 0.5
        high = first.astype(BF16)
        left = first - high.astype(F32)
        mid = left.astype(BF16)
        low = left - mid.astype(F32)
        extra = jnp.concatenate(
            [
                w_out[...].astype(F32) * 0.5,
                high.astype(F32),
                mid.astype(F32),
                low,
                jnp.zeros((13, hid), F32),
            ],
            axis=0,
        ).T.astype(BF16)
        weights[:hid, :] = jnp.concatenate(
            [
                (w_in[...].astype(F32) * 0.5).astype(BF16),
                jnp.zeros((hid, chans), BF16),
                extra[:, chans:],
            ],
            axis=1,
        )
        weights[hid:, :] = jnp.concatenate(
            [jnp.zeros((hid, chans), BF16), extra[:, :chans], jnp.zeros((hid, 16), BF16)], axis=1
        )
        w_in_t[...] = w_in[...].astype(F32).T.astype(BF16)
        modes[...] = jnp.zeros_like(modes)
        sums[...] = jnp.zeros_like(sums)

    values = dot(fourier[...], table[...]).astype(BF16)
    for p in range(lat_rows):
        cols[: 2 * chans, p * size : (p + 1) * size] = values[2 * chans * p : 2 * chans * (p + 1)]
    for p in range(lat_rows):
        here = slice(p * size, (p + 1) * size)
        both = dot(weights[...], cols[:, here])
        half = both[:hid]
        th = jnp.tanh(half)
        rise = 1.0 + th
        act = half * rise
        pre = (both[hid:] * (rise + act * (1.0 - th))).astype(BF16)
        acts[:hid, here] = act.astype(BF16)
        acts[hid:, here] = pre
        grid[chans * p : chans * (p + 1), :] = dot(w_in_t[...], pre).astype(BF16)
    sums[...] += dot_nt(acts[...], cols[...])
    modes[...] += dot_nt(table[...], grid[...])

    @pl.when(step == pl.num_programs(0) - 1)
    def _():
        real = modes[:waves].astype(BF16)
        imag = modes[waves:].astype(BF16)
        span = quarter * chans
        for q in range(quarter):
            a, b = q * chans, (q + 1) * chans
            piece = jnp.concatenate(
                [real[:, a:b], imag[:, a:b], real[:, span + a : span + b], imag[:, span + a : span + b]],
                axis=1,
            )
            for d in range(ranks):
                out[d, q * own : (q + 1) * own, :] = piece[d * own : (d + 1) * own]
        base = quarter * own
        width = 2 * chans
        mixed = jnp.concatenate(
            [sums[hid:, :chans], sums[:hid, chans:width]], axis=1
        )
        main = jnp.concatenate([mixed[: hid // 2], mixed[hid // 2 :]], axis=1)
        main_hi = main.astype(BF16)
        main_lo = (main - main_hi.astype(F32)).astype(BF16)
        total = sums[hid:, width : width + 1]
        total = jnp.concatenate([total[: hid // 2], total[hid // 2 :]], axis=1)
        total_hi = total.astype(BF16)
        total_lo = (total - total_hi.astype(F32)).astype(BF16)
        tail = jnp.concatenate(
            [total_hi, total_lo, jnp.zeros((hid // 2, 2 * width - 4), BF16)], axis=1
        )
        share = hid // 2 // ranks
        for d in range(ranks):
            part = slice(d * share, (d + 1) * share)
            out[d, base : base + share, :] = main_hi[part]
            out[d, base + share : base + 2 * share, :] = main_lo[part]
            out[d, base + 2 * share : base + 3 * share, :] = tail[part]


def columns(arrived, table, w_in, bias, w_out, ranks, own):
    hid, chans = w_in.shape
    lat_rows = arrived.shape[1] // own
    waves = ranks * own
    points = table.shape[1]
    size = 256
    rows_out = lat_rows // 2 * own + 3 * (hid // 2 // ranks)
    whole = lambda *shape: pl.BlockSpec(shape, lambda i: (0,) * len(shape))
    return pl.pallas_call(
        functools.partial(column_kernel, ranks, own),
        grid=(points // size,),
        in_specs=[
            whole(*arrived.shape),
            pl.BlockSpec((2 * waves, size), lambda i: (0, i)),
            whole(hid, chans),
            whole(1, hid),
            whole(chans, hid),
        ],
        out_specs=whole(ranks, rows_out, 4 * chans),
        out_shape=jax.ShapeDtypeStruct((ranks, rows_out, 4 * chans), BF16),
        scratch_shapes=[
            pltpu.VMEM((2 * chans * lat_rows, 2 * waves), BF16),
            pltpu.VMEM((2 * chans + 16, lat_rows * size), BF16),
            pltpu.VMEM((2 * hid, 2 * chans + 16), BF16),
            pltpu.VMEM((chans, hid), BF16),
            pltpu.VMEM((2 * hid, lat_rows * size), BF16),
            pltpu.VMEM((chans * lat_rows, size), BF16),
            pltpu.VMEM((2 * waves, chans * lat_rows), F32),
            pltpu.VMEM((2 * hid, 2 * chans + 16), F32),
        ],
        compiler_params=params(),
        name="column_physics",
    )(arrived, table, w_in, bias, w_out)


def backward_kernel(ranks, quarter, own, arrived, cot, leg, factor, out, rows):
    block, width, _ = cot.shape
    step = pl.program_id(0)
    size = quarter * own

    @pl.when(step == 0)
    def _():
        for s in range(ranks):
            rows[s * size : (s + 1) * size, :] = arrived[s, :size, :].astype(F32)

    for i in range(block):
        mine = rows[pl.ds(step * block + i, ranks * quarter, stride=own), :].T.astype(BF16)
        lhs = jnp.concatenate([mine[:width], mine[width:]], axis=1)
        out[i] = cot[i].astype(F32) * factor[...] + dot_nt(lhs, leg[i])


def backward(arrived, cot, legendre, factor, ranks):
    own, width, degrees = cot.shape
    lat = legendre.shape[2]
    quarter = lat // ranks // 2
    block = steps_of(own)
    return pl.pallas_call(
        functools.partial(backward_kernel, ranks, quarter, own),
        grid=(own // block,),
        in_specs=[
            pl.BlockSpec(arrived.shape, lambda i: (0, 0, 0)),
            pl.BlockSpec((block, width, degrees), lambda i: (i, 0, 0)),
            pl.BlockSpec((block, degrees, lat), lambda i: (i, 0, 0)),
            pl.BlockSpec((width, degrees), lambda i: (0, 0)),
        ],
        out_specs=pl.BlockSpec((block, width, degrees), lambda i: (i, 0, 0)),
        out_shape=jax.ShapeDtypeStruct((own, width, degrees), F32),
        scratch_shapes=[pltpu.VMEM((ranks * quarter * own, 2 * width), F32)],
        compiler_params=params(),
        name="legendre_backward",
    )(arrived, cot, legendre, factor)


def finish_kernel(groups, scale, parts, grad_in, grad_bias, grad_out):
    ranks = parts.shape[0] // groups
    share = parts.shape[1] // 2
    chans = grad_in.shape[1]
    hid = grad_in.shape[0]
    for r in range(ranks):
        total = parts[r]
        for g in range(1, groups):
            total = total + parts[g * ranks + r]
        total = total * scale
        for half in range(2):
            row = half * (hid // 2) + r * share
            lane = 2 * chans * half
            grad_in[row : row + share, :] = total[:share, lane : lane + chans]
            grad_out[row : row + share, :] = total[:share, lane + chans : lane + 2 * chans]
            grad_bias[row : row + share, :] = (
                total[share:, half : half + 1] + total[share:, half + 2 : half + 3]
            )


def finish(parts, hid, chans, groups, scale):
    return pl.pallas_call(
        functools.partial(finish_kernel, groups, scale),
        out_shape=(
            jax.ShapeDtypeStruct((hid, chans), F32),
            jax.ShapeDtypeStruct((hid, 1), F32),
            jax.ShapeDtypeStruct((hid, chans), F32),
        ),
        compiler_params=pltpu.CompilerParams(vmem_limit_bytes=VMEM),
        name="weight_gradients",
    )(parts)


def body(
    spectral_state, cotangent, legendre, quadrature, damping, physics_in, physics_bias, physics_out
):
    spectral = spectral_state[0]
    cot = cotangent[0]
    own, width, degrees = spectral.shape
    chans = width // 2
    hid = physics_in.shape[0]
    ranks = lax.axis_size("lat")
    groups = lax.axis_size("grp")
    lat = legendre.shape[2]
    lat_rows = lat // ranks
    factor = implicit_factor(damping, degrees)
    table = jnp.asarray(longitude_table(own * ranks, NLON))

    sent = forward(spectral, cot, legendre, factor, quadrature[None, :], ranks)
    arrived = lax.all_to_all(sent, "lat", split_axis=0, concat_axis=0, tiled=True)
    back = columns(arrived, table, physics_in, physics_bias[None, :], physics_out, ranks, own)
    returned = lax.all_to_all(back, "lat", split_axis=0, concat_axis=0, tiled=True)

    base = lat_rows // 2 * own
    share = hid // 2 // ranks
    tail = returned[:, base:, :].astype(F32)
    part = jnp.concatenate(
        [
            jnp.sum(tail[:, :share] + tail[:, share : 2 * share], axis=0),
            jnp.sum(tail[:, 2 * share :], axis=0),
        ],
        axis=0,
    )
    spread = jnp.broadcast_to(part[None], (groups * ranks,) + part.shape)
    parts = lax.all_to_all(spread, ("grp", "lat"), split_axis=0, concat_axis=0, tiled=True)
    grad_state = backward(returned, cot, legendre, factor, ranks)
    scale = 1.0 / math.sqrt(groups * lat * NLON)
    grad_in, grad_bias, grad_out = finish(parts, hid, chans, groups, scale)
    return (grad_state[None], grad_in, grad_bias[:, 0], grad_out.T)


def solution(mesh):
    in_specs = (
        P("grp", "lat", None, None),
        P("grp", "lat", None, None),
        P("lat", None, None),
        P(),
        P(),
        P(),
        P(),
        P(),
    )
    out_specs = (P("grp", "lat", None, None), P(), P(), P())
    return jax.shard_map(body, mesh=mesh, in_specs=in_specs, out_specs=out_specs, check_vma=False)
```

```python
import functools
import math

import jax
import jax.numpy as jnp
import numpy as np
import ml_dtypes
from jax import lax
from jax.experimental import pallas as pl
from jax.experimental.pallas import tpu as pltpu
from jax.sharding import PartitionSpec as P

NLON = 2560
MIB = 1024 * 1024
F32 = jnp.float32
BF16 = jnp.bfloat16
PARTS = 2


def longitude_table(waves, points):
    phase = np.arange(waves)[:, None] * np.arange(points)[None, :] % points
    angle = phase * (2.0 * math.pi / points)
    scale = math.sqrt(2.0 / points)
    both = np.concatenate([np.cos(angle) * scale, -np.sin(angle) * scale])
    return both.astype(np.float32).astype(ml_dtypes.bfloat16)


def dot(a, b):
    return jnp.dot(a, b, preferred_element_type=F32)


def dot_nt(a, b):
    return lax.dot_general(a, b, (((1,), (1,)), ((), ())), preferred_element_type=F32)


def params(mib):
    return pltpu.CompilerParams(vmem_limit_bytes=mib * MIB, dimension_semantics=("arbitrary",))


def whole(*shape):
    return pl.BlockSpec(shape, lambda i: (0,) * len(shape))


def block_of(waves):
    return max(size for size in range(1, 9) if waves % size == 0)


def set_factor(factor, damping):
    width, degrees = factor.shape
    chans = width // 2
    lanes = 128
    spread = jnp.broadcast_to(damping[...], (lanes, chans)).T
    for start in range(0, degrees, lanes):
        degree = (lax.broadcasted_iota(jnp.int32, (chans, lanes), 1) + start).astype(F32)
        ratio = degree * (degree + 1.0) / (degrees * (degrees + 1.0))
        piece = 1.0 / (1.0 + spread * ratio)
        factor[:chans, start : start + lanes] = piece
        factor[chans:, start : start + lanes] = piece


def forward_kernel(ranks, spec, cot, leg, damping, quad, *rest):
    outs, (rows, factor) = rest[:PARTS], rest[PARTS:]
    block, width, _ = spec.shape
    chans = width // 2
    lat = leg.shape[2]
    own = rows.shape[0] // lat
    near = lat // ranks // 2 // PARTS
    step = pl.program_id(0)

    @pl.when(step == 0)
    def _():
        set_factor(factor, damping)

    for i in range(block):
        tend = (cot[i].astype(F32) * factor[...]).astype(BF16)
        stacked = jnp.concatenate(
            [spec[i, :chans], tend[:chans], spec[i, chans:], tend[chans:]], axis=0
        )
        res = dot(stacked, leg[i])
        weight = quad[...]
        res = jnp.concatenate(
            [
                res[:chans],
                res[chans : 2 * chans] * weight,
                res[2 * chans : 3 * chans],
                res[3 * chans :] * weight,
            ],
            axis=0,
        )
        rows[pl.ds(step * block + i, lat, stride=own), :] = res.T

    @pl.when(step == pl.num_programs(0) - 1)
    def _():
        size = near * own
        for part in range(PARTS):
            for d in range(ranks):
                for side in range(2):
                    start = ((side * PARTS + part) * ranks + d) * size
                    outs[part][d, side * size : (side + 1) * size, :] = rows[
                        start : start + size, :
                    ].astype(BF16)


def forward(spectral, cot, legendre, damping, quad, ranks):
    own, width, degrees = spectral.shape
    lat = legendre.shape[2]
    block = block_of(own)
    shape = (ranks, lat // ranks // PARTS * own, 2 * width)
    return pl.pallas_call(
        functools.partial(forward_kernel, ranks),
        grid=(own // block,),
        in_specs=[
            pl.BlockSpec((block, width, degrees), lambda i: (i, 0, 0)),
            pl.BlockSpec((block, width, degrees), lambda i: (i, 0, 0)),
            pl.BlockSpec((block, degrees, lat), lambda i: (i, 0, 0)),
            whole(*damping.shape),
            whole(1, lat),
        ],
        out_specs=[whole(*shape)] * PARTS,
        out_shape=[jax.ShapeDtypeStruct(shape, BF16)] * PARTS,
        scratch_shapes=[
            pltpu.VMEM((lat * own, 2 * width), F32),
            pltpu.VMEM((width, degrees), F32),
        ],
        compiler_params=params(60),
        name="legendre_forward",
    )(spectral, cot, legendre, damping, quad)


def column_kernel(ranks, own, last, arrived, table, w_in, bias, w_out, before, out, after, *scratch):
    fourier, cols, weights, acts, grid, modes, sums = scratch
    chans, hid = w_in.shape
    waves = ranks * own
    lat_rows = arrived.shape[1] // own
    near = lat_rows // 2
    size = table.shape[1]
    width = 2 * chans
    step = pl.program_id(0)

    @pl.when(step == 0)
    def _():
        for p in range(lat_rows):
            piece = jnp.concatenate(
                [arrived[s, p * own : (p + 1) * own, :] for s in range(ranks)], axis=0
            ).T
            row = width * p
            fourier[row : row + width, :waves] = piece[:width]
            fourier[row : row + width, waves:] = piece[width:]
        cols[width:, :] = jnp.ones((16, cols.shape[1]), BF16)
        first = bias[...] * 0.5
        high = first.astype(BF16)
        left = first - high.astype(F32)
        mid = left.astype(BF16)
        low = left - mid.astype(F32)
        stack = jnp.concatenate(
            [
                w_in[...].astype(F32) * 0.5,
                w_out[...].astype(F32) * 0.5,
                high.astype(F32),
                mid.astype(F32),
                low,
                jnp.zeros((13, hid), F32),
            ],
            axis=0,
        ).T.astype(BF16)
        lane = lax.broadcasted_iota(jnp.int32, stack.shape, 1)
        is_out = (lane >= chans) & (lane < width)
        nothing = jnp.zeros_like(stack)
        weights[:hid, :] = jnp.where(is_out, nothing, stack)
        weights[hid:, :] = jnp.where(is_out, stack, nothing)
        modes[...] = jnp.zeros_like(modes)
        sums[...] = before[...] if last else jnp.zeros_like(sums)

    values = dot(fourier[...], table[...]).astype(BF16)
    for p in range(lat_rows):
        cols[:width, p * size : (p + 1) * size] = values[width * p : width * (p + 1)]
    for p in range(lat_rows):
        here = slice(p * size, (p + 1) * size)
        both = dot(weights[...], cols[:, here]).astype(BF16)
        half = both[:hid]
        th = jnp.tanh(half)
        rise = 1 + th
        act = half * rise
        pre = both[hid:] * (rise + act * (1 - th))
        acts[:hid, here] = act
        acts[hid:, here] = pre
        grid[chans * p : chans * (p + 1), :] = dot(w_in[...], pre).astype(BF16)
    sums[...] += dot_nt(acts[...], cols[...])
    modes[...] += dot_nt(table[...], grid[...])

    @pl.when(step == pl.num_programs(0) - 1)
    def _():
        real = modes[:waves].astype(BF16)
        imag = modes[waves:].astype(BF16)
        span = near * chans
        for q in range(near):
            a, b = q * chans, (q + 1) * chans
            piece = jnp.concatenate(
                [real[:, a:b], imag[:, a:b], real[:, span + a : span + b], imag[:, span + a : span + b]],
                axis=1,
            )
            for d in range(ranks):
                out[d, q * own : (q + 1) * own, :] = piece[d * own : (d + 1) * own]
        after[...] = sums[...]
        if last:
            base = near * own
            turned = sums[...].T
            main = jnp.concatenate([turned[:chans, hid:], turned[chans:width, :hid]], axis=0)
            main_hi = main.astype(BF16).astype(F32)
            main_lo = main - main_hi
            total = turned[width : width + 1, hid:]
            total_hi = total.astype(BF16).astype(F32)
            total_lo = total - total_hi
            lanes = 4 * chans
            cuts = range(0, hid, lanes)
            tail = jnp.concatenate(
                [piece[:, c : c + lanes] for piece in (total_hi, total_lo) for c in cuts], axis=0
            ).astype(BF16)
            share = width // ranks
            for d in range(ranks):
                rows = [
                    piece[d * share : (d + 1) * share, c : c + lanes]
                    for piece in (main_hi, main_lo)
                    for c in cuts
                ]
                rows = jnp.concatenate(rows, axis=0).astype(BF16)
                size_main = rows.shape[0]
                out[d, base : base + size_main, :] = rows
                out[d, base + size_main : base + size_main + tail.shape[0], :] = tail


def columns(arrived, table, w_in, bias, w_out, before, ranks, own, last):
    chans, hid = w_in.shape
    lat_rows = arrived.shape[1] // own
    waves = ranks * own
    points = table.shape[1]
    size = 256
    rows_out = lat_rows // 2 * own
    lanes = 4 * chans
    if last:
        rows_out += 2 * (hid // lanes) * (2 * chans // ranks) + 2 * (hid // lanes)
    sums = (2 * hid, 2 * chans + 16)
    return pl.pallas_call(
        functools.partial(column_kernel, ranks, own, last),
        grid=(points // size,),
        in_specs=[
            whole(*arrived.shape),
            pl.BlockSpec((2 * waves, size), lambda i: (0, i)),
            whole(chans, hid),
            whole(1, hid),
            whole(chans, hid),
            whole(*before.shape),
        ],
        out_specs=[whole(ranks, rows_out, lanes), whole(*sums)],
        out_shape=[
            jax.ShapeDtypeStruct((ranks, rows_out, lanes), BF16),
            jax.ShapeDtypeStruct(sums, F32),
        ],
        scratch_shapes=[
            pltpu.VMEM((2 * chans * lat_rows, 2 * waves), BF16),
            pltpu.VMEM((2 * chans + 16, lat_rows * size), BF16),
            pltpu.VMEM((2 * hid, 2 * chans + 16), BF16),
            pltpu.VMEM((2 * hid, lat_rows * size), BF16),
            pltpu.VMEM((chans * lat_rows, size), BF16),
            pltpu.VMEM((2 * waves, chans * lat_rows), F32),
            pltpu.VMEM(sums, F32),
        ],
        compiler_params=params(32),
        name="column_physics",
    )(arrived, table, w_in, bias, w_out, before)


def backward_kernel(ranks, near, own, *refs):
    arrived, (cot, leg, damping, out, rows, factor) = refs[:PARTS], refs[PARTS:]
    block, width, _ = cot.shape
    step = pl.program_id(0)
    size = near * own

    @pl.when(step == 0)
    def _():
        set_factor(factor, damping)
        for part in range(PARTS):
            for s in range(ranks):
                row = (part * ranks + s) * size
                rows[row : row + size, :] = arrived[part][s, :size, :].astype(F32)

    for i in range(block):
        mine = rows[pl.ds(step * block + i, PARTS * ranks * near, stride=own), :]
        mine = mine.T.astype(BF16)
        lhs = jnp.concatenate([mine[:width], mine[width:]], axis=1)
        out[i] = cot[i].astype(F32) * factor[...] + dot_nt(lhs, leg[i])


def backward(arrived, cot, legendre, damping, ranks):
    own, width, degrees = cot.shape
    lat = legendre.shape[2]
    near = lat // ranks // 2 // PARTS
    block = block_of(own)
    return pl.pallas_call(
        functools.partial(backward_kernel, ranks, near, own),
        grid=(own // block,),
        in_specs=[whole(*piece.shape) for piece in arrived]
        + [
            pl.BlockSpec((block, width, degrees), lambda i: (i, 0, 0)),
            pl.BlockSpec((block, degrees, lat), lambda i: (i, 0, 0)),
            whole(*damping.shape),
        ],
        out_specs=pl.BlockSpec((block, width, degrees), lambda i: (i, 0, 0)),
        out_shape=jax.ShapeDtypeStruct((own, width, degrees), F32),
        scratch_shapes=[
            pltpu.VMEM((PARTS * ranks * near * own, 2 * width), F32),
            pltpu.VMEM((width, degrees), F32),
        ],
        compiler_params=params(32),
        name="legendre_backward",
    )(*arrived, cot, legendre, damping)


def finish_kernel(groups, scale, parts, grad_in, grad_bias, grad_out):
    ranks = parts.shape[0] // groups
    chans, hid = grad_in.shape
    lanes = parts.shape[2]
    cuts = hid // lanes
    share = 2 * chans // ranks
    for r in range(ranks):
        total = parts[r]
        for g in range(1, groups):
            total = total + parts[g * ranks + r]
        total = total * scale
        row = r * share
        dest, row = (grad_in, row) if row < chans else (grad_out, row - chans)
        for c in range(cuts):
            dest[row : row + share, c * lanes : (c + 1) * lanes] = total[c * share : (c + 1) * share]
        if r == 0:
            for c in range(cuts):
                grad_bias[:, c * lanes : (c + 1) * lanes] = total[cuts * share + c : cuts * share + c + 1]


def finish(parts, hid, chans, groups, scale):
    return pl.pallas_call(
        functools.partial(finish_kernel, groups, scale),
        out_shape=(
            jax.ShapeDtypeStruct((chans, hid), F32),
            jax.ShapeDtypeStruct((1, hid), F32),
            jax.ShapeDtypeStruct((chans, hid), F32),
        ),
        name="weight_gradients",
    )(parts)


def body(
    spectral_state, cotangent, legendre, quadrature, damping, physics_in, physics_bias, physics_out
):
    spectral = spectral_state[0]
    cot = cotangent[0]
    own, width, degrees = spectral.shape
    chans = width // 2
    hid = physics_in.shape[0]
    ranks = lax.axis_size("lat")
    groups = lax.axis_size("grp")
    lat = legendre.shape[2]
    lat_rows = lat // ranks
    table = jnp.asarray(longitude_table(own * ranks, NLON))
    damping = damping[None, :]
    exchange = functools.partial(
        lax.all_to_all, axis_name="lat", split_axis=0, concat_axis=0, tiled=True
    )

    sent = forward(spectral, cot, legendre, damping, quadrature[None, :], ranks)
    arrived = [exchange(piece) for piece in sent]
    sums = jnp.zeros((8, 128), F32)
    returned = []
    for part in range(PARTS):
        back, sums = columns(
            arrived[part],
            table,
            physics_in.T,
            physics_bias[None, :],
            physics_out,
            sums,
            ranks,
            own,
            part == PARTS - 1,
        )
        returned.append(exchange(back))

    base = lat_rows // 2 // PARTS * own
    lanes = 2 * width
    share = (hid // lanes) * (width // ranks)
    tail = hid // lanes
    last = returned[-1][:, base:, :].astype(F32)
    part = jnp.concatenate(
        [
            jnp.sum(last[:, :share] + last[:, share : 2 * share], axis=0),
            jnp.sum(last[:, 2 * share : 2 * share + tail] + last[:, 2 * share + tail :], axis=0),
        ],
        axis=0,
    )
    spread = jnp.broadcast_to(part[None], (groups * ranks,) + part.shape)
    parts = lax.all_to_all(spread, ("grp", "lat"), split_axis=0, concat_axis=0, tiled=True)
    grad_state = backward(returned, cot, legendre, damping, ranks)
    scale = 1.0 / math.sqrt(groups * lat * NLON)
    grad_in, grad_bias, grad_out = finish(parts, hid, chans, groups, scale)
    return (grad_state[None], grad_in.T, grad_bias[0], grad_out)


def solution(mesh):
    in_specs = (
        P("grp", "lat", None, None),
        P("grp", "lat", None, None),
        P("lat", None, None),
        P(),
        P(),
        P(),
        P(),
        P(),
    )
    out_specs = (P("grp", "lat", None, None), P(), P(), P())
    return jax.shard_map(body, mesh=mesh, in_specs=in_specs, out_specs=out_specs, check_vma=False)
```

```python
import functools
import math

import jax
import jax.numpy as jnp
import numpy as np
import ml_dtypes
from jax import lax
from jax.experimental import pallas as pl
from jax.experimental.pallas import tpu as pltpu
from jax.sharding import PartitionSpec as P

NLON = 2560
MIB = 1024 * 1024
F32 = jnp.float32
BF16 = jnp.bfloat16
PARTS = 2


def longitude_table(waves, points):
    phase = np.arange(waves)[:, None] * np.arange(points)[None, :] % points
    angle = phase * (2.0 * math.pi / points)
    scale = math.sqrt(2.0 / points)
    both = np.concatenate([np.cos(angle) * scale, -np.sin(angle) * scale])
    return both.astype(np.float32).astype(ml_dtypes.bfloat16)


def dot(a, b):
    return jnp.dot(a, b, preferred_element_type=F32)


def dot_nt(a, b):
    return lax.dot_general(a, b, (((1,), (1,)), ((), ())), preferred_element_type=F32)


def params(mib):
    return pltpu.CompilerParams(vmem_limit_bytes=mib * MIB, dimension_semantics=("arbitrary",))


def whole(*shape):
    return pl.BlockSpec(shape, lambda i: (0,) * len(shape))


def block_of(waves):
    return max(size for size in range(1, 9) if waves % size == 0)


def set_factor(factor, damping):
    width, degrees = factor.shape
    chans = width // 2
    lanes = 128
    spread = jnp.broadcast_to(damping[...], (lanes, chans)).T
    for start in range(0, degrees, lanes):
        degree = (lax.broadcasted_iota(jnp.int32, (chans, lanes), 1) + start).astype(F32)
        ratio = degree * (degree + 1.0) / (degrees * (degrees + 1.0))
        piece = 1.0 / (1.0 + spread * ratio)
        factor[:chans, start : start + lanes] = piece
        factor[chans:, start : start + lanes] = piece


def forward_kernel(ranks, spec, cot, leg, damping, quad, *rest):
    outs, (rows, factor) = rest[:PARTS], rest[PARTS:]
    block, width, _ = spec.shape
    chans = width // 2
    lat = leg.shape[2]
    own = rows.shape[0] // lat
    near = lat // ranks // 2 // PARTS
    step = pl.program_id(0)

    @pl.when(step == 0)
    def _():
        set_factor(factor, damping)

    group = 2 if block % 2 == 0 else 1
    weight = quad[...]
    for first in range(0, block, group):
        members = range(first, first + group)
        stacked = []
        for i in members:
            tend = (cot[i].astype(F32) * factor[...]).astype(BF16)
            stacked += [spec[i, :chans], tend[:chans], spec[i, chans:], tend[chans:]]
        product = dot(
            jnp.concatenate(stacked, axis=0), jnp.concatenate([leg[i] for i in members], axis=1)
        )
        for k, i in enumerate(members):
            res = product[2 * width * k : 2 * width * (k + 1), lat * k : lat * (k + 1)]
            res = jnp.concatenate(
                [
                    res[:chans],
                    res[chans : 2 * chans] * weight,
                    res[2 * chans : 3 * chans],
                    res[3 * chans :] * weight,
                ],
                axis=0,
            )
            rows[pl.ds(step * block + i, lat, stride=own), :] = res.T

    @pl.when(step == pl.num_programs(0) - 1)
    def _():
        size = near * own
        for part in range(PARTS):
            for d in range(ranks):
                for side in range(2):
                    start = ((side * PARTS + part) * ranks + d) * size
                    outs[part][d, side * size : (side + 1) * size, :] = rows[
                        start : start + size, :
                    ].astype(BF16)


def forward(spectral, cot, legendre, damping, quad, ranks):
    own, width, degrees = spectral.shape
    lat = legendre.shape[2]
    block = block_of(own)
    shape = (ranks, lat // ranks // PARTS * own, 2 * width)
    return pl.pallas_call(
        functools.partial(forward_kernel, ranks),
        grid=(own // block,),
        in_specs=[
            pl.BlockSpec((block, width, degrees), lambda i: (i, 0, 0)),
            pl.BlockSpec((block, width, degrees), lambda i: (i, 0, 0)),
            pl.BlockSpec((block, degrees, lat), lambda i: (i, 0, 0)),
            whole(*damping.shape),
            whole(1, lat),
        ],
        out_specs=[whole(*shape)] * PARTS,
        out_shape=[jax.ShapeDtypeStruct(shape, BF16)] * PARTS,
        scratch_shapes=[
            pltpu.VMEM((lat * own, 2 * width), F32),
            pltpu.VMEM((width, degrees), F32),
        ],
        compiler_params=params(60),
        name="legendre_forward",
    )(spectral, cot, legendre, damping, quad)


def column_kernel(ranks, own, last, arrived, table, w_in, bias, w_out, before, out, after, *scratch):
    fourier, cols, weights, acts, grid, modes, sums = scratch
    chans, hid = w_in.shape
    waves = ranks * own
    lat_rows = arrived.shape[1] // own
    near = lat_rows // 2
    size = table.shape[1]
    width = 2 * chans
    step = pl.program_id(0)

    @pl.when(step == 0)
    def _():
        for p in range(lat_rows):
            piece = jnp.concatenate(
                [arrived[s, p * own : (p + 1) * own, :] for s in range(ranks)], axis=0
            ).T
            row = width * p
            fourier[row : row + width, :waves] = piece[:width]
            fourier[row : row + width, waves:] = piece[width:]
        cols[width:, :] = jnp.ones((16, cols.shape[1]), BF16)
        first = bias[...] * 0.5
        high = first.astype(BF16)
        left = first - high.astype(F32)
        mid = left.astype(BF16)
        low = left - mid.astype(F32)
        stack = jnp.concatenate(
            [
                w_in[...].astype(F32) * 0.5,
                w_out[...].astype(F32) * 0.5,
                high.astype(F32),
                mid.astype(F32),
                low,
                jnp.zeros((13, hid), F32),
            ],
            axis=0,
        ).T.astype(BF16)
        lane = lax.broadcasted_iota(jnp.int32, stack.shape, 1)
        is_out = (lane >= chans) & (lane < width)
        nothing = jnp.zeros_like(stack)
        weights[:hid, :] = jnp.where(is_out, nothing, stack)
        weights[hid:, :] = jnp.where(is_out, stack, nothing)
        modes[...] = jnp.zeros_like(modes)
        sums[...] = before[...].T if last else jnp.zeros_like(sums)

    values = dot(fourier[...], table[...]).astype(BF16)
    for p in range(lat_rows):
        cols[:width, p * size : (p + 1) * size] = values[width * p : width * (p + 1)]
    for p in range(lat_rows):
        here = slice(p * size, (p + 1) * size)
        both = dot(weights[...], cols[:, here]).astype(BF16)
        half = both[:hid]
        th = jnp.tanh(half)
        rise = 1 + th
        act = half * rise
        pre = both[hid:] * (rise + act * (1 - th))
        acts[:hid, here] = act
        acts[hid:, here] = pre
        grid[chans * p : chans * (p + 1), :] = dot(w_in[...], pre).astype(BF16)
    if last:
        sums[...] += dot_nt(cols[...], acts[...])
    else:
        sums[...] += dot_nt(acts[...], cols[...])
    modes[...] += dot_nt(table[...], grid[...])

    @pl.when(step == pl.num_programs(0) - 1)
    def _():
        real = modes[:waves].astype(BF16)
        imag = modes[waves:].astype(BF16)
        span = near * chans
        for q in range(near):
            a, b = q * chans, (q + 1) * chans
            piece = jnp.concatenate(
                [real[:, a:b], imag[:, a:b], real[:, span + a : span + b], imag[:, span + a : span + b]],
                axis=1,
            )
            for d in range(ranks):
                out[d, q * own : (q + 1) * own, :] = piece[d * own : (d + 1) * own]
        if not last:
            after[...] = sums[...]
        else:
            after[...] = jnp.zeros_like(after)
            base = near * own
            turned = sums[...]
            main = jnp.concatenate([turned[:chans, hid:], turned[chans:width, :hid]], axis=0)
            main_hi = main.astype(BF16).astype(F32)
            main_lo = main - main_hi
            total = turned[width : width + 1, hid:]
            total_hi = total.astype(BF16).astype(F32)
            total_lo = total - total_hi
            lanes = 4 * chans
            cuts = range(0, hid, lanes)
            tail = jnp.concatenate(
                [piece[:, c : c + lanes] for piece in (total_hi, total_lo) for c in cuts], axis=0
            ).astype(BF16)
            share = width // ranks
            for d in range(ranks):
                rows = [
                    piece[d * share : (d + 1) * share, c : c + lanes]
                    for piece in (main_hi, main_lo)
                    for c in cuts
                ]
                rows = jnp.concatenate(rows, axis=0).astype(BF16)
                size_main = rows.shape[0]
                out[d, base : base + size_main, :] = rows
                out[d, base + size_main : base + size_main + tail.shape[0], :] = tail


def columns(arrived, table, w_in, bias, w_out, before, ranks, own, last):
    chans, hid = w_in.shape
    lat_rows = arrived.shape[1] // own
    waves = ranks * own
    points = table.shape[1]
    size = 512
    rows_out = lat_rows // 2 * own
    lanes = 4 * chans
    if last:
        rows_out += 2 * (hid // lanes) * (2 * chans // ranks) + 2 * (hid // lanes)
    sums = (2 * chans + 16, 2 * hid) if last else (2 * hid, 2 * chans + 16)
    after = (8, 128) if last else sums
    return pl.pallas_call(
        functools.partial(column_kernel, ranks, own, last),
        grid=(points // size,),
        in_specs=[
            whole(*arrived.shape),
            pl.BlockSpec((2 * waves, size), lambda i: (0, i)),
            whole(chans, hid),
            whole(1, hid),
            whole(chans, hid),
            whole(*before.shape),
        ],
        out_specs=[whole(ranks, rows_out, lanes), whole(*after)],
        out_shape=[
            jax.ShapeDtypeStruct((ranks, rows_out, lanes), BF16),
            jax.ShapeDtypeStruct(after, F32),
        ],
        scratch_shapes=[
            pltpu.VMEM((2 * chans * lat_rows, 2 * waves), BF16),
            pltpu.VMEM((2 * chans + 16, lat_rows * size), BF16),
            pltpu.VMEM((2 * hid, 2 * chans + 16), BF16),
            pltpu.VMEM((2 * hid, lat_rows * size), BF16),
            pltpu.VMEM((chans * lat_rows, size), BF16),
            pltpu.VMEM((2 * waves, chans * lat_rows), F32),
            pltpu.VMEM(sums, F32),
        ],
        compiler_params=params(60),
        name="column_physics",
    )(arrived, table, w_in, bias, w_out, before)


def backward_kernel(ranks, near, own, *refs):
    arrived, (cot, leg, damping, out, rows, factor) = refs[:PARTS], refs[PARTS:]
    block, width, _ = cot.shape
    step = pl.program_id(0)
    size = near * own

    @pl.when(step == 0)
    def _():
        set_factor(factor, damping)
        for part in range(PARTS):
            for s in range(ranks):
                row = (part * ranks + s) * size
                rows[row : row + size, :] = arrived[part][s, :size, :].astype(F32)

    group = 2 if block % 2 == 0 else 1
    for first in range(0, block, group):
        members = range(first, first + group)
        lhs = []
        for k, i in enumerate(members):
            mine = rows[pl.ds(step * block + i, PARTS * ranks * near, stride=own), :]
            mine = mine.T.astype(BF16)
            piece = jnp.concatenate([mine[:width], mine[width:]], axis=1)
            blank = jnp.zeros_like(piece)
            lhs.append(jnp.concatenate([piece if j == k else blank for j in range(group)], axis=1))
        product = dot_nt(
            jnp.concatenate(lhs, axis=0), jnp.concatenate([leg[i] for i in members], axis=1)
        )
        for k, i in enumerate(members):
            out[i] = cot[i].astype(F32) * factor[...] + product[width * k : width * (k + 1)]


def backward(arrived, cot, legendre, damping, ranks):
    own, width, degrees = cot.shape
    lat = legendre.shape[2]
    near = lat // ranks // 2 // PARTS
    block = block_of(own)
    return pl.pallas_call(
        functools.partial(backward_kernel, ranks, near, own),
        grid=(own // block,),
        in_specs=[whole(*piece.shape) for piece in arrived]
        + [
            pl.BlockSpec((block, width, degrees), lambda i: (i, 0, 0)),
            pl.BlockSpec((block, degrees, lat), lambda i: (i, 0, 0)),
            whole(*damping.shape),
        ],
        out_specs=pl.BlockSpec((block, width, degrees), lambda i: (i, 0, 0)),
        out_shape=jax.ShapeDtypeStruct((own, width, degrees), F32),
        scratch_shapes=[
            pltpu.VMEM((PARTS * ranks * near * own, 2 * width), F32),
            pltpu.VMEM((width, degrees), F32),
        ],
        compiler_params=params(60),
        name="legendre_backward",
    )(*arrived, cot, legendre, damping)


def collect_kernel(base, cuts, share, arrived, out):
    total = arrived[0, base:, :].astype(F32)
    for s in range(1, arrived.shape[0]):
        total = total + arrived[s, base:, :].astype(F32)
    main = cuts * share
    part = total[:main] + total[main : 2 * main]
    tail = total[2 * main : 2 * main + cuts] + total[2 * main + cuts :]
    part = jnp.concatenate([part, tail], axis=0)
    for s in range(out.shape[0]):
        out[s] = part


def collect(arrived, base, cuts, share, copies):
    shape = (copies, cuts * share + cuts, arrived.shape[2])
    return pl.pallas_call(
        functools.partial(collect_kernel, base, cuts, share),
        out_shape=jax.ShapeDtypeStruct(shape, F32),
        name="collect_gradients",
    )(arrived)


def finish_kernel(groups, scale, parts, grad_in, grad_bias, grad_out):
    ranks = parts.shape[0] // groups
    chans, hid = grad_in.shape
    lanes = parts.shape[2]
    cuts = hid // lanes
    share = 2 * chans // ranks
    for r in range(ranks):
        total = parts[r]
        for g in range(1, groups):
            total = total + parts[g * ranks + r]
        total = total * scale
        row = r * share
        dest, row = (grad_in, row) if row < chans else (grad_out, row - chans)
        for c in range(cuts):
            dest[row : row + share, c * lanes : (c + 1) * lanes] = total[c * share : (c + 1) * share]
        if r == 0:
            for c in range(cuts):
                grad_bias[:, c * lanes : (c + 1) * lanes] = total[cuts * share + c : cuts * share + c + 1]


def finish(parts, hid, chans, groups, scale):
    return pl.pallas_call(
        functools.partial(finish_kernel, groups, scale),
        out_shape=(
            jax.ShapeDtypeStruct((chans, hid), F32),
            jax.ShapeDtypeStruct((1, hid), F32),
            jax.ShapeDtypeStruct((chans, hid), F32),
        ),
        name="weight_gradients",
    )(parts)


def body(
    spectral_state, cotangent, legendre, quadrature, damping, physics_in, physics_bias, physics_out
):
    spectral = spectral_state[0]
    cot = cotangent[0]
    own, width, degrees = spectral.shape
    chans = width // 2
    hid = physics_in.shape[0]
    ranks = lax.axis_size("lat")
    groups = lax.axis_size("grp")
    lat = legendre.shape[2]
    lat_rows = lat // ranks
    table = jnp.asarray(longitude_table(own * ranks, NLON))
    damping = damping[None, :]
    exchange = functools.partial(
        lax.all_to_all, axis_name="lat", split_axis=0, concat_axis=0, tiled=True
    )

    sent = forward(spectral, cot, legendre, damping, quadrature[None, :], ranks)
    arrived = [exchange(piece) for piece in sent]
    sums = jnp.zeros((8, 128), F32)
    returned = []
    for part in range(PARTS):
        back, sums = columns(
            arrived[part],
            table,
            physics_in.T,
            physics_bias[None, :],
            physics_out,
            sums,
            ranks,
            own,
            part == PARTS - 1,
        )
        if returned:
            back, returned[-1] = lax.optimization_barrier((back, returned[-1]))
        returned.append(exchange(back))

    base = lat_rows // 2 // PARTS * own
    spread = collect(returned[-1], base, hid // (2 * width), width // ranks, groups * ranks)
    parts = lax.all_to_all(spread, ("grp", "lat"), split_axis=0, concat_axis=0, tiled=True)
    grad_state = backward(returned, cot, legendre, damping, ranks)
    scale = 1.0 / math.sqrt(groups * lat * NLON)
    grad_in, grad_bias, grad_out = finish(parts, hid, chans, groups, scale)
    return (grad_state[None], grad_in.T, grad_bias[0], grad_out)


def solution(mesh):
    in_specs = (
        P("grp", "lat", None, None),
        P("grp", "lat", None, None),
        P("lat", None, None),
        P(),
        P(),
        P(),
        P(),
        P(),
    )
    out_specs = (P("grp", "lat", None, None), P(), P(), P())
    return jax.shard_map(body, mesh=mesh, in_specs=in_specs, out_specs=out_specs, check_vma=False)
```

```python
import functools
import math

import jax
import jax.numpy as jnp
import numpy as np
import ml_dtypes
from jax import lax
from jax.experimental import pallas as pl
from jax.experimental.pallas import tpu as pltpu
from jax.sharding import PartitionSpec as P

NLON = 2560
MIB = 1024 * 1024
F32 = jnp.float32
BF16 = jnp.bfloat16
PARTS = 2
SIZE = 512
HBM = pl.BlockSpec(memory_space=pl.ANY)


def longitude_table(waves, points):
    phase = np.arange(waves)[:, None] * np.arange(points)[None, :] % points
    angle = phase * (2.0 * math.pi / points)
    scale = math.sqrt(2.0 / points)
    both = np.concatenate([np.cos(angle) * scale, -np.sin(angle) * scale])
    both = both.astype(np.float32).astype(ml_dtypes.bfloat16)
    return np.ascontiguousarray(both.reshape(2 * waves, -1, SIZE).swapaxes(0, 1))


def dot(a, b):
    return jnp.dot(a, b, preferred_element_type=F32)


def dot_nt(a, b):
    return lax.dot_general(a, b, (((1,), (1,)), ((), ())), preferred_element_type=F32)


def params(mib):
    return pltpu.CompilerParams(vmem_limit_bytes=mib * MIB, dimension_semantics=("arbitrary",))


def whole(*shape):
    return pl.BlockSpec(shape, lambda i: (0,) * len(shape))


def block_of(waves):
    return max(size for size in range(1, 9) if waves % size == 0)


def set_factor(factor, damping):
    width, degrees = factor.shape
    chans = width // 2
    lanes = 128
    spread = jnp.broadcast_to(damping[...], (lanes, chans)).T
    for start in range(0, degrees, lanes):
        degree = (lax.broadcasted_iota(jnp.int32, (chans, lanes), 1) + start).astype(F32)
        ratio = degree * (degree + 1.0) / (degrees * (degrees + 1.0))
        piece = 1.0 / (1.0 + spread * ratio)
        factor[:chans, start : start + lanes] = piece
        factor[chans:, start : start + lanes] = piece


def copies_of(pairs, sems):
    copies = [pltpu.make_async_copy(src, dst, sems.at[k]) for k, (src, dst) in enumerate(pairs)]
    for copy in copies:
        copy.start()
    return copies


def forward_kernel(ranks, block, *refs):
    spec_h, cot_h, leg_h, damping, quad = refs[:5]
    outs = refs[5 : 5 + PARTS]
    spec, cot, leg, rows, factor, sems = refs[5 + PARTS :]
    own, width, _ = spec.shape
    chans = width // 2
    lat = leg.shape[2]
    near = lat // ranks // 2 // PARTS

    def moves(c):
        here = pl.ds(c * block, block)
        return [
            pltpu.make_async_copy(src.at[here], dst.at[here], sems.at[c, k])
            for k, (src, dst) in enumerate(((spec_h, spec), (cot_h, cot), (leg_h, leg)))
        ]

    for c in range(own // block):
        for move in moves(c):
            move.start()
    set_factor(factor, damping)

    def step(c, carry):
        for move in moves(c):
            move.wait()
        weight = quad[...]
        for k in range(block):
            i = c * block + k
            tend = (cot[i].astype(F32) * factor[...]).astype(BF16)
            state = spec[i]
            stacked = jnp.concatenate(
                [state[:chans], tend[:chans], state[chans:], tend[chans:]], axis=0
            )
            res = dot(stacked, leg[i])
            res = jnp.concatenate(
                [
                    res[:chans],
                    res[chans : 2 * chans] * weight,
                    res[2 * chans : 3 * chans],
                    res[3 * chans :] * weight,
                ],
                axis=0,
            )
            rows[pl.ds(i, lat, stride=own), :] = res.T
        return carry

    lax.fori_loop(0, own // block, step, 0)
    size = near * own
    for part in range(PARTS):
        for d in range(ranks):
            for side in range(2):
                start = ((side * PARTS + part) * ranks + d) * size
                outs[part][d, side * size : (side + 1) * size, :] = rows[
                    start : start + size, :
                ].astype(BF16)


def forward(spectral, cot, legendre, damping, quad, ranks):
    own, width, degrees = spectral.shape
    lat = legendre.shape[2]
    block = block_of(own)
    shape = (ranks, lat // ranks // PARTS * own, 2 * width)
    return pl.pallas_call(
        functools.partial(forward_kernel, ranks, block),
        grid=(1,),
        in_specs=[HBM] * 3 + [whole(*damping.shape), whole(1, lat)],
        out_specs=[whole(*shape)] * PARTS,
        out_shape=[jax.ShapeDtypeStruct(shape, BF16)] * PARTS,
        scratch_shapes=[
            pltpu.VMEM(spectral.shape, BF16),
            pltpu.VMEM(cot.shape, BF16),
            pltpu.VMEM(legendre.shape, BF16),
            pltpu.VMEM((lat * own, 2 * width), F32),
            pltpu.VMEM((width, degrees), F32),
            pltpu.SemaphoreType.DMA((own // block, 3)),
        ],
        compiler_params=params(60),
        name="legendre_forward",
    )(spectral, cot, legendre, damping, quad)


def column_kernel(ranks, own, first, last, *refs):
    given = 5 if first else 6
    sources, out = refs[:given], refs[given]
    refs = refs[given + 1 :]
    if not last:
        after, refs = refs[0], refs[1:]
    arrived, table, w_in, bias, w_out, sums, fourier, cols, weights, acts, grid, modes, sems = refs
    chans, hid = w_in.shape
    waves = ranks * own
    lat_rows = arrived.shape[1] // own
    near = lat_rows // 2
    chunks, _, size = table.shape
    width = 2 * chans
    arrived_h, table_h, w_in_h, bias_h, w_out_h = sources[:5]
    pairs = [(arrived_h, arrived), (w_in_h, w_in), (bias_h, bias), (w_out_h, w_out)]
    if not first:
        pairs.append((sources[5], sums))
    small = copies_of(pairs, sems)

    def table_move(c):
        return pltpu.make_async_copy(table_h.at[c], table.at[c], sems.at[5 + c])

    for c in range(chunks):
        table_move(c).start()
    modes[...] = jnp.zeros_like(modes)
    cols[width:, :] = jnp.ones((16, cols.shape[1]), BF16)
    for copy in small:
        copy.wait()
    if first:
        sums[...] = jnp.zeros_like(sums)
    for p in range(lat_rows):
        piece = jnp.concatenate(
            [arrived[s, p * own : (p + 1) * own, :] for s in range(ranks)], axis=0
        ).T
        row = width * p
        fourier[row : row + width, :waves] = piece[:width]
        fourier[row : row + width, waves:] = piece[width:]
    half_bias = bias[...] * 0.5
    high = half_bias.astype(BF16).astype(F32)
    left = half_bias - high
    mid = left.astype(BF16).astype(F32)
    low = left - mid
    stack = jnp.concatenate(
        [
            w_in[...].astype(F32) * 0.5,
            w_out[...].astype(F32) * 0.5,
            high,
            mid,
            low,
            jnp.zeros((13, hid), F32),
        ],
        axis=0,
    ).T.astype(BF16)
    lane = lax.broadcasted_iota(jnp.int32, stack.shape, 1)
    is_out = (lane >= chans) & (lane < width)
    nothing = jnp.zeros_like(stack)
    weights[:hid, :] = jnp.where(is_out, nothing, stack)
    weights[hid:, :] = jnp.where(is_out, stack, nothing)

    def step(c, carry):
        table_move(c).wait()
        values = dot(fourier[...], table[c]).astype(BF16)
        for p in range(lat_rows):
            cols[:width, p * size : (p + 1) * size] = values[width * p : width * (p + 1)]
        for p in range(lat_rows):
            here = slice(p * size, (p + 1) * size)
            both = dot(weights[...], cols[:, here]).astype(BF16)
            half = both[:hid]
            th = jnp.tanh(half)
            rise = 1 + th
            act = half * rise
            pre = both[hid:] * (rise + act * (1 - th))
            acts[:hid, here] = act
            acts[hid:, here] = pre
            grid[chans * p : chans * (p + 1), :] = dot(w_in[...], pre).astype(BF16)
        sums[...] += dot_nt(cols[...], acts[...])
        modes[...] += dot_nt(table[c], grid[...])
        return carry

    lax.fori_loop(0, chunks, step, 0)

    real = modes[:waves].astype(BF16)
    imag = modes[waves:].astype(BF16)
    span = near * chans
    for q in range(near):
        a, b = q * chans, (q + 1) * chans
        piece = jnp.concatenate(
            [real[:, a:b], imag[:, a:b], real[:, span + a : span + b], imag[:, span + a : span + b]],
            axis=1,
        )
        for d in range(ranks):
            out[d, q * own : (q + 1) * own, :] = piece[d * own : (d + 1) * own]
    if not last:
        after[...] = sums[...]
        return
    base = near * own
    main = jnp.concatenate([sums[:chans, hid:], sums[chans:width, :hid]], axis=0)
    total = sums[width : width + 1, hid:]
    lanes = 4 * chans
    cuts = range(0, hid, lanes)
    tail = [total[:, c : c + lanes] for c in cuts]
    share = width // ranks
    for d in range(ranks):
        rows = [main[d * share : (d + 1) * share, c : c + lanes] for c in cuts]
        rows = jnp.concatenate(rows + tail, axis=0).astype(BF16)
        out[d, base : base + rows.shape[0], :] = rows


def columns(arrived, table, w_in, bias, w_out, before, ranks, own, last):
    chans, hid = w_in.shape
    lat_rows = arrived.shape[1] // own
    waves = ranks * own
    chunks, _, size = table.shape
    rows_out = lat_rows // 2 * own
    lanes = 4 * chans
    if last:
        rows_out += (hid // lanes) * (2 * chans // ranks) + hid // lanes
    sums = (2 * chans + 16, 2 * hid)
    out_specs = [whole(ranks, rows_out, lanes)]
    out_shape = [jax.ShapeDtypeStruct((ranks, rows_out, lanes), BF16)]
    if not last:
        out_specs.append(whole(*sums))
        out_shape.append(jax.ShapeDtypeStruct(sums, F32))
    sources = [arrived, table, w_in, bias, w_out] + before
    result = pl.pallas_call(
        functools.partial(column_kernel, ranks, own, not before, last),
        grid=(1,),
        in_specs=[HBM] * len(sources),
        out_specs=out_specs,
        out_shape=out_shape,
        scratch_shapes=[
            pltpu.VMEM(arrived.shape, BF16),
            pltpu.VMEM(table.shape, BF16),
            pltpu.VMEM(w_in.shape, BF16),
            pltpu.VMEM(bias.shape, F32),
            pltpu.VMEM(w_out.shape, BF16),
            pltpu.VMEM(sums, F32),
            pltpu.VMEM((2 * chans * lat_rows, 2 * waves), BF16),
            pltpu.VMEM((2 * chans + 16, lat_rows * size), BF16),
            pltpu.VMEM((2 * hid, 2 * chans + 16), BF16),
            pltpu.VMEM((2 * hid, lat_rows * size), BF16),
            pltpu.VMEM((chans * lat_rows, size), BF16),
            pltpu.VMEM((2 * waves, chans * lat_rows), F32),
            pltpu.SemaphoreType.DMA((5 + chunks,)),
        ],
        compiler_params=params(60),
        name="column_physics",
    )(*sources)
    return result[0], list(result[1:])


def backward_kernel(ranks, near, block, *refs):
    arrived_h, refs = refs[:PARTS], refs[PARTS:]
    cot_h, leg_h, damping, out_h = refs[:4]
    arrived, refs = refs[4 : 4 + PARTS], refs[4 + PARTS :]
    cot, leg, out, rows, factor, in_sems, out_sems, sems = refs
    own, width, _ = cot.shape
    size = near * own
    early = copies_of(zip(arrived_h, arrived), sems)

    def moves(c):
        here = pl.ds(c * block, block)
        return [
            pltpu.make_async_copy(src.at[here], dst.at[here], in_sems.at[c, k])
            for k, (src, dst) in enumerate(((cot_h, cot), (leg_h, leg)))
        ]

    def leave(c):
        here = pl.ds(c * block, block)
        return pltpu.make_async_copy(out.at[here], out_h.at[here], out_sems.at[c])

    for c in range(own // block):
        for move in moves(c):
            move.start()
    set_factor(factor, damping)
    for part in range(PARTS):
        early[part].wait()
        for s in range(ranks):
            row = (part * ranks + s) * size
            rows[row : row + size, :] = arrived[part][s, :size, :].astype(F32)

    def step(c, carry):
        for move in moves(c):
            move.wait()
        for k in range(block):
            i = c * block + k
            mine = rows[pl.ds(i, PARTS * ranks * near, stride=own), :]
            mine = mine.T.astype(BF16)
            lhs = jnp.concatenate([mine[:width], mine[width:]], axis=1)
            out[i] = cot[i].astype(F32) * factor[...] + dot_nt(lhs, leg[i])
        leave(c).start()
        return carry

    lax.fori_loop(0, own // block, step, 0)
    for c in range(own // block):
        leave(c).wait()


def backward(arrived, cot, legendre, damping, ranks):
    own, width, degrees = cot.shape
    lat = legendre.shape[2]
    near = lat // ranks // 2 // PARTS
    block = block_of(own)
    return pl.pallas_call(
        functools.partial(backward_kernel, ranks, near, block),
        grid=(1,),
        in_specs=[HBM] * (PARTS + 2) + [whole(*damping.shape)],
        out_specs=HBM,
        out_shape=jax.ShapeDtypeStruct((own, width, degrees), F32),
        scratch_shapes=[pltpu.VMEM(piece.shape, BF16) for piece in arrived]
        + [
            pltpu.VMEM(cot.shape, BF16),
            pltpu.VMEM(legendre.shape, BF16),
            pltpu.VMEM(cot.shape, F32),
            pltpu.VMEM((PARTS * ranks * near * own, 2 * width), F32),
            pltpu.VMEM((width, degrees), F32),
            pltpu.SemaphoreType.DMA((own // block, 2)),
            pltpu.SemaphoreType.DMA((own // block,)),
            pltpu.SemaphoreType.DMA((PARTS,)),
        ],
        compiler_params=params(60),
        name="legendre_backward",
    )(*arrived, cot, legendre, damping)


def collect_kernel(base, arrived, out):
    total = arrived[0, base:, :].astype(F32)
    for s in range(1, arrived.shape[0]):
        total = total + arrived[s, base:, :].astype(F32)
    for s in range(out.shape[0]):
        out[s] = total


def collect(arrived, base, copies):
    shape = (copies, arrived.shape[1] - base, arrived.shape[2])
    return pl.pallas_call(
        functools.partial(collect_kernel, base),
        grid=(1,),
        in_specs=[whole(*arrived.shape)],
        out_specs=whole(*shape),
        out_shape=jax.ShapeDtypeStruct(shape, F32),
        compiler_params=params(60),
        name="collect_gradients",
    )(arrived)


def finish_kernel(groups, scale, parts, grad_in, grad_bias, grad_out):
    ranks = parts.shape[0] // groups
    chans, hid = grad_in.shape
    lanes = parts.shape[2]
    cuts = hid // lanes
    share = 2 * chans // ranks
    for r in range(ranks):
        total = parts[r]
        for g in range(1, groups):
            total = total + parts[g * ranks + r]
        total = total * scale
        row = r * share
        dest, row = (grad_in, row) if row < chans else (grad_out, row - chans)
        for c in range(cuts):
            dest[row : row + share, c * lanes : (c + 1) * lanes] = total[c * share : (c + 1) * share]
        if r == 0:
            for c in range(cuts):
                grad_bias[:, c * lanes : (c + 1) * lanes] = total[cuts * share + c : cuts * share + c + 1]


def finish(parts, hid, chans, groups, scale):
    return pl.pallas_call(
        functools.partial(finish_kernel, groups, scale),
        grid=(1,),
        in_specs=[whole(*parts.shape)],
        out_specs=(whole(chans, hid), whole(1, hid), whole(chans, hid)),
        out_shape=(
            jax.ShapeDtypeStruct((chans, hid), F32),
            jax.ShapeDtypeStruct((1, hid), F32),
            jax.ShapeDtypeStruct((chans, hid), F32),
        ),
        compiler_params=params(60),
        name="weight_gradients",
    )(parts)


def body(
    spectral_state, cotangent, legendre, quadrature, damping, physics_in, physics_bias, physics_out
):
    spectral = spectral_state[0]
    cot = cotangent[0]
    own, width, degrees = spectral.shape
    chans = width // 2
    hid = physics_in.shape[0]
    ranks = lax.axis_size("lat")
    groups = lax.axis_size("grp")
    lat = legendre.shape[2]
    lat_rows = lat // ranks
    table = jnp.asarray(longitude_table(own * ranks, NLON))
    damping = damping[None, :]
    exchange = functools.partial(
        lax.all_to_all, axis_name="lat", split_axis=0, concat_axis=0, tiled=True
    )

    sent = forward(spectral, cot, legendre, damping, quadrature[None, :], ranks)
    arrived = [exchange(piece) for piece in sent]
    sums = []
    returned = []
    for part in range(PARTS):
        back, sums = columns(
            arrived[part],
            table,
            physics_in.T,
            physics_bias[None, :],
            physics_out,
            sums,
            ranks,
            own,
            part == PARTS - 1,
        )
        if returned:
            back, returned[-1] = lax.optimization_barrier((back, returned[-1]))
        returned.append(exchange(back))

    base = lat_rows // 2 // PARTS * own
    spread = collect(returned[-1], base, groups * ranks)
    parts = lax.all_to_all(spread, ("grp", "lat"), split_axis=0, concat_axis=0, tiled=True)
    grad_state = backward(returned, cot, legendre, damping, ranks)
    scale = 1.0 / math.sqrt(groups * lat * NLON)
    grad_in, grad_bias, grad_out = finish(parts, hid, chans, groups, scale)
    return (grad_state[None], grad_in.T, grad_bias[0], grad_out)


def solution(mesh):
    in_specs = (
        P("grp", "lat", None, None),
        P("grp", "lat", None, None),
        P("lat", None, None),
        P(),
        P(),
        P(),
        P(),
        P(),
    )
    out_specs = (P("grp", "lat", None, None), P(), P(), P())
    return jax.shard_map(body, mesh=mesh, in_specs=in_specs, out_specs=out_specs, check_vma=False)
```

```python
import functools
import math

import jax
import jax.numpy as jnp
import numpy as np
import ml_dtypes
from jax import lax
from jax.experimental import pallas as pl
from jax.experimental.pallas import tpu as pltpu
from jax.sharding import PartitionSpec as P

NLON = 2560
MIB = 1024 * 1024
F32 = jnp.float32
BF16 = jnp.bfloat16
PARTS = 2
SIZE = 512
AHEAD = 2
HBM = pl.BlockSpec(memory_space=pl.ANY)


def longitude_table(waves, points):
    phase = np.arange(waves)[:, None] * np.arange(points)[None, :] % points
    angle = phase * (2.0 * math.pi / points)
    scale = math.sqrt(2.0 / points)
    both = np.concatenate([np.cos(angle) * scale, -np.sin(angle) * scale])
    both = both.astype(np.float32).astype(ml_dtypes.bfloat16)
    return np.ascontiguousarray(both.reshape(2 * waves, -1, SIZE).swapaxes(0, 1))


def dot(a, b):
    return jnp.dot(a, b, preferred_element_type=F32)


def dot_nt(a, b):
    return lax.dot_general(a, b, (((1,), (1,)), ((), ())), preferred_element_type=F32)


def params(mib):
    return pltpu.CompilerParams(vmem_limit_bytes=mib * MIB, dimension_semantics=("arbitrary",))


def whole(*shape):
    return pl.BlockSpec(shape, lambda i: (0,) * len(shape))


def block_of(waves):
    return max(size for size in range(1, 9) if waves % size == 0)


def set_factor(factor, damping):
    width, degrees = factor.shape
    chans = width // 2
    lanes = 128
    spread = jnp.broadcast_to(damping[...], (lanes, chans)).T
    for start in range(0, degrees, lanes):
        degree = (lax.broadcasted_iota(jnp.int32, (chans, lanes), 1) + start).astype(F32)
        ratio = degree * (degree + 1.0) / (degrees * (degrees + 1.0))
        piece = 1.0 / (1.0 + spread * ratio)
        factor[:chans, start : start + lanes] = piece
        factor[chans:, start : start + lanes] = piece


def copies_of(pairs, sems):
    copies = [pltpu.make_async_copy(src, dst, sems.at[k]) for k, (src, dst) in enumerate(pairs)]
    for copy in copies:
        copy.start()
    return copies


def forward_kernel(ranks, block, *refs):
    spec_h, cot_h, leg_h, damping, quad = refs[:5]
    outs = refs[5 : 5 + PARTS]
    spec, cot, leg, rows, factor, sems = refs[5 + PARTS :]
    own, width, _ = spec.shape
    chans = width // 2
    lat = leg.shape[2]
    near = lat // ranks // 2 // PARTS

    def moves(c):
        here = pl.ds(c * block, block)
        return [
            pltpu.make_async_copy(src.at[here], dst.at[here], sems.at[c, k])
            for k, (src, dst) in enumerate(((spec_h, spec), (cot_h, cot), (leg_h, leg)))
        ]

    for c in range(min(AHEAD, own // block)):
        for move in moves(c):
            move.start()
    set_factor(factor, damping)

    def step(c, carry):
        for move in moves(c):
            move.wait()

        @pl.when(c + AHEAD < own // block)
        def _():
            for move in moves(c + AHEAD):
                move.start()

        weight = quad[...]
        for k in range(block):
            i = c * block + k
            tend = (cot[i].astype(F32) * factor[...]).astype(BF16)
            state = spec[i]
            stacked = jnp.concatenate(
                [state[:chans], tend[:chans], state[chans:], tend[chans:]], axis=0
            )
            res = dot(stacked, leg[i])
            res = jnp.concatenate(
                [
                    res[:chans],
                    res[chans : 2 * chans] * weight,
                    res[2 * chans : 3 * chans],
                    res[3 * chans :] * weight,
                ],
                axis=0,
            )
            rows[pl.ds(i, lat, stride=own), :] = res.T
        return carry

    lax.fori_loop(0, own // block, step, 0)
    size = near * own
    for part in range(PARTS):
        for d in range(ranks):
            for side in range(2):
                start = ((side * PARTS + part) * ranks + d) * size
                outs[part][d, side * size : (side + 1) * size, :] = rows[
                    start : start + size, :
                ].astype(BF16)


def forward(spectral, cot, legendre, damping, quad, ranks):
    own, width, degrees = spectral.shape
    lat = legendre.shape[2]
    block = block_of(own)
    shape = (ranks, lat // ranks // PARTS * own, 2 * width)
    return pl.pallas_call(
        functools.partial(forward_kernel, ranks, block),
        grid=(1,),
        in_specs=[HBM] * 3 + [whole(*damping.shape), whole(1, lat)],
        out_specs=[whole(*shape)] * PARTS,
        out_shape=[jax.ShapeDtypeStruct(shape, BF16)] * PARTS,
        scratch_shapes=[
            pltpu.VMEM(spectral.shape, BF16),
            pltpu.VMEM(cot.shape, BF16),
            pltpu.VMEM(legendre.shape, BF16),
            pltpu.VMEM((lat * own, 2 * width), F32),
            pltpu.VMEM((width, degrees), F32),
            pltpu.SemaphoreType.DMA((own // block, 3)),
        ],
        compiler_params=params(60),
        name="legendre_forward",
    )(spectral, cot, legendre, damping, quad)


def column_kernel(ranks, own, first, last, *refs):
    given = 5 if first else 6
    sources, out = refs[:given], refs[given]
    refs = refs[given + 1 :]
    if not last:
        after, refs = refs[0], refs[1:]
    arrived, table, w_in, bias, w_out, sums, fourier, cols, weights, acts, grid, modes, sems = refs
    chans, hid = w_in.shape
    waves = ranks * own
    lat_rows = arrived.shape[1] // own
    near = lat_rows // 2
    chunks, _, size = table.shape
    width = 2 * chans
    unit = hid if last else 64
    arrived_h, table_h, w_in_h, bias_h, w_out_h = sources[:5]
    pairs = [(arrived_h, arrived), (w_in_h, w_in), (bias_h, bias), (w_out_h, w_out)]
    if not first:
        pairs.append((sources[5], sums))
    small = copies_of(pairs, sems)

    def table_move(c):
        return pltpu.make_async_copy(table_h.at[c], table.at[c], sems.at[5 + c])

    for c in range(min(AHEAD, chunks)):
        table_move(c).start()
    modes[...] = jnp.zeros_like(modes)
    cols[width:, :] = jnp.ones((16, cols.shape[1]), BF16)
    for copy in small:
        copy.wait()
    if first:
        sums[...] = jnp.zeros_like(sums)
    for p in range(lat_rows):
        piece = jnp.concatenate(
            [arrived[s, p * own : (p + 1) * own, :] for s in range(ranks)], axis=0
        ).T
        row = width * p
        fourier[row : row + width, :waves] = piece[:width]
        fourier[row : row + width, waves:] = piece[width:]
    half_bias = bias[...] * 0.5
    high = half_bias.astype(BF16).astype(F32)
    left = half_bias - high
    mid = left.astype(BF16).astype(F32)
    low = left - mid
    stack = jnp.concatenate(
        [
            w_in[...].astype(F32) * 0.5,
            w_out[...].astype(F32) * 0.5,
            high,
            mid,
            low,
            jnp.zeros((13, hid), F32),
        ],
        axis=0,
    ).T.astype(BF16)
    lane = lax.broadcasted_iota(jnp.int32, stack.shape, 1)
    is_out = (lane >= chans) & (lane < width)
    nothing = jnp.zeros_like(stack)
    inward = jnp.where(is_out, nothing, stack)
    outward = jnp.where(is_out, stack, nothing)
    for k in range(0, hid, unit):
        weights[2 * k : 2 * k + unit, :] = inward[k : k + unit]
        weights[2 * k + unit : 2 * k + 2 * unit, :] = outward[k : k + unit]

    def step(c, carry):
        table_move(c).wait()

        @pl.when(c + AHEAD < chunks)
        def _():
            table_move(c + AHEAD).start()

        values = dot(fourier[...], table[c]).astype(BF16)
        for p in range(lat_rows):
            cols[:width, p * size : (p + 1) * size] = values[width * p : width * (p + 1)]
        for p in range(lat_rows):
            here = slice(p * size, (p + 1) * size)
            for k in range(0, hid, unit):
                both = dot(weights[2 * k : 2 * k + 2 * unit, :], cols[:, here]).astype(BF16)
                half = both[:unit]
                th = jnp.tanh(half)
                rise = 1 + th
                act = half * rise
                acts[k : k + unit, here] = act
                acts[hid + k : hid + k + unit, here] = both[unit:] * (rise + act * (1 - th))
            grid[chans * p : chans * (p + 1), :] = dot(w_in[...], acts[hid:, here]).astype(BF16)
        sums[...] += dot_nt(acts[...], cols[...])
        modes[...] += dot_nt(table[c], grid[...])
        return carry

    lax.fori_loop(0, chunks, step, 0)

    real = modes[:waves].astype(BF16)
    imag = modes[waves:].astype(BF16)
    span = near * chans
    for q in range(near):
        a, b = q * chans, (q + 1) * chans
        piece = jnp.concatenate(
            [real[:, a:b], imag[:, a:b], real[:, span + a : span + b], imag[:, span + a : span + b]],
            axis=1,
        )
        for d in range(ranks):
            out[d, q * own : (q + 1) * own, :] = piece[d * own : (d + 1) * own]
    if not last:
        after[...] = sums[...]
        return
    base = near * own
    turned = sums[...].T
    main = jnp.concatenate([turned[:chans, hid:], turned[chans:width, :hid]], axis=0)
    total = turned[width : width + 1, hid:]
    lanes = 4 * chans
    cuts = range(0, hid, lanes)
    tail = [total[:, c : c + lanes] for c in cuts]
    share = width // ranks
    for d in range(ranks):
        rows = [main[d * share : (d + 1) * share, c : c + lanes] for c in cuts]
        rows = jnp.concatenate(rows + tail, axis=0).astype(BF16)
        out[d, base : base + rows.shape[0], :] = rows


def columns(arrived, table, w_in, bias, w_out, before, ranks, own, last):
    chans, hid = w_in.shape
    lat_rows = arrived.shape[1] // own
    waves = ranks * own
    chunks, _, size = table.shape
    rows_out = lat_rows // 2 * own
    lanes = 4 * chans
    if last:
        rows_out += (hid // lanes) * (2 * chans // ranks) + hid // lanes
    sums = (2 * hid, 2 * chans + 16)
    out_specs = [whole(ranks, rows_out, lanes)]
    out_shape = [jax.ShapeDtypeStruct((ranks, rows_out, lanes), BF16)]
    if not last:
        out_specs.append(whole(*sums))
        out_shape.append(jax.ShapeDtypeStruct(sums, F32))
    sources = [arrived, table, w_in, bias, w_out] + before
    result = pl.pallas_call(
        functools.partial(column_kernel, ranks, own, not before, last),
        grid=(1,),
        in_specs=[HBM] * len(sources),
        out_specs=out_specs,
        out_shape=out_shape,
        scratch_shapes=[
            pltpu.VMEM(arrived.shape, BF16),
            pltpu.VMEM(table.shape, BF16),
            pltpu.VMEM(w_in.shape, BF16),
            pltpu.VMEM(bias.shape, F32),
            pltpu.VMEM(w_out.shape, BF16),
            pltpu.VMEM(sums, F32),
            pltpu.VMEM((2 * chans * lat_rows, 2 * waves), BF16),
            pltpu.VMEM((2 * chans + 16, lat_rows * size), BF16),
            pltpu.VMEM((2 * hid, 2 * chans + 16), BF16),
            pltpu.VMEM((2 * hid, lat_rows * size), BF16),
            pltpu.VMEM((chans * lat_rows, size), BF16),
            pltpu.VMEM((2 * waves, chans * lat_rows), F32),
            pltpu.SemaphoreType.DMA((5 + chunks,)),
        ],
        compiler_params=params(60),
        name="column_physics",
    )(*sources)
    return result[0], list(result[1:])


def backward_kernel(ranks, near, block, *refs):
    arrived_h, refs = refs[:PARTS], refs[PARTS:]
    cot_h, leg_h, damping, out_h = refs[:4]
    arrived, refs = refs[4 : 4 + PARTS], refs[4 + PARTS :]
    cot, leg, out, rows, factor, in_sems, out_sems, sems = refs
    own, width, _ = cot.shape
    size = near * own
    early = copies_of(zip(arrived_h, arrived), sems)

    def moves(c):
        here = pl.ds(c * block, block)
        return [
            pltpu.make_async_copy(src.at[here], dst.at[here], in_sems.at[c, k])
            for k, (src, dst) in enumerate(((cot_h, cot), (leg_h, leg)))
        ]

    def leave(c):
        here = pl.ds(c * block, block)
        return pltpu.make_async_copy(out.at[here], out_h.at[here], out_sems.at[c])

    for c in range(min(AHEAD, own // block)):
        for move in moves(c):
            move.start()
    set_factor(factor, damping)
    for part in range(PARTS):
        early[part].wait()
        for s in range(ranks):
            row = (part * ranks + s) * size
            rows[row : row + size, :] = arrived[part][s, :size, :].astype(F32)

    def step(c, carry):
        for move in moves(c):
            move.wait()

        @pl.when(c + AHEAD < own // block)
        def _():
            for move in moves(c + AHEAD):
                move.start()

        for k in range(block):
            i = c * block + k
            mine = rows[pl.ds(i, PARTS * ranks * near, stride=own), :]
            mine = mine.T.astype(BF16)
            lhs = jnp.concatenate([mine[:width], mine[width:]], axis=1)
            out[i] = cot[i].astype(F32) * factor[...] + dot_nt(lhs, leg[i])
        leave(c).start()
        return carry

    lax.fori_loop(0, own // block, step, 0)
    for c in range(own // block):
        leave(c).wait()


def backward(arrived, cot, legendre, damping, ranks):
    own, width, degrees = cot.shape
    lat = legendre.shape[2]
    near = lat // ranks // 2 // PARTS
    block = block_of(own)
    return pl.pallas_call(
        functools.partial(backward_kernel, ranks, near, block),
        grid=(1,),
        in_specs=[HBM] * (PARTS + 2) + [whole(*damping.shape)],
        out_specs=HBM,
        out_shape=jax.ShapeDtypeStruct((own, width, degrees), F32),
        scratch_shapes=[pltpu.VMEM(piece.shape, BF16) for piece in arrived]
        + [
            pltpu.VMEM(cot.shape, BF16),
            pltpu.VMEM(legendre.shape, BF16),
            pltpu.VMEM(cot.shape, F32),
            pltpu.VMEM((PARTS * ranks * near * own, 2 * width), F32),
            pltpu.VMEM((width, degrees), F32),
            pltpu.SemaphoreType.DMA((own // block, 2)),
            pltpu.SemaphoreType.DMA((own // block,)),
            pltpu.SemaphoreType.DMA((PARTS,)),
        ],
        compiler_params=params(60),
        name="legendre_backward",
    )(*arrived, cot, legendre, damping)


def collect_kernel(base, arrived, out):
    total = arrived[0, base:, :].astype(F32)
    for s in range(1, arrived.shape[0]):
        total = total + arrived[s, base:, :].astype(F32)
    for s in range(out.shape[0]):
        out[s] = total


def collect(arrived, base, copies):
    shape = (copies, arrived.shape[1] - base, arrived.shape[2])
    return pl.pallas_call(
        functools.partial(collect_kernel, base),
        grid=(1,),
        in_specs=[whole(*arrived.shape)],
        out_specs=whole(*shape),
        out_shape=jax.ShapeDtypeStruct(shape, F32),
        compiler_params=params(60),
        name="collect_gradients",
    )(arrived)


def finish_kernel(groups, scale, parts, grad_in, grad_bias, grad_out):
    ranks = parts.shape[0] // groups
    chans, hid = grad_in.shape
    lanes = parts.shape[2]
    cuts = hid // lanes
    share = 2 * chans // ranks
    for r in range(ranks):
        total = parts[r]
        for g in range(1, groups):
            total = total + parts[g * ranks + r]
        total = total * scale
        row = r * share
        dest, row = (grad_in, row) if row < chans else (grad_out, row - chans)
        for c in range(cuts):
            dest[row : row + share, c * lanes : (c + 1) * lanes] = total[c * share : (c + 1) * share]
        if r == 0:
            for c in range(cuts):
                grad_bias[:, c * lanes : (c + 1) * lanes] = total[cuts * share + c : cuts * share + c + 1]


def finish(parts, hid, chans, groups, scale):
    return pl.pallas_call(
        functools.partial(finish_kernel, groups, scale),
        grid=(1,),
        in_specs=[whole(*parts.shape)],
        out_specs=(whole(chans, hid), whole(1, hid), whole(chans, hid)),
        out_shape=(
            jax.ShapeDtypeStruct((chans, hid), F32),
            jax.ShapeDtypeStruct((1, hid), F32),
            jax.ShapeDtypeStruct((chans, hid), F32),
        ),
        compiler_params=params(60),
        name="weight_gradients",
    )(parts)


def body(
    spectral_state, cotangent, legendre, quadrature, damping, physics_in, physics_bias, physics_out
):
    spectral = spectral_state[0]
    cot = cotangent[0]
    own, width, degrees = spectral.shape
    chans = width // 2
    hid = physics_in.shape[0]
    ranks = lax.axis_size("lat")
    groups = lax.axis_size("grp")
    lat = legendre.shape[2]
    lat_rows = lat // ranks
    table = jnp.asarray(longitude_table(own * ranks, NLON))
    damping = damping[None, :]
    exchange = functools.partial(
        lax.all_to_all, axis_name="lat", split_axis=0, concat_axis=0, tiled=True
    )

    sent = forward(spectral, cot, legendre, damping, quadrature[None, :], ranks)
    arrived = [exchange(piece) for piece in sent]
    sums = []
    returned = []
    for part in range(PARTS):
        back, sums = columns(
            arrived[part],
            table,
            physics_in.T,
            physics_bias[None, :],
            physics_out,
            sums,
            ranks,
            own,
            part == PARTS - 1,
        )
        if returned:
            back, returned[-1] = lax.optimization_barrier((back, returned[-1]))
        returned.append(exchange(back))

    base = lat_rows // 2 // PARTS * own
    spread = collect(returned[-1], base, groups * ranks)
    parts = lax.all_to_all(spread, ("grp", "lat"), split_axis=0, concat_axis=0, tiled=True)
    grad_state = backward(returned, cot, legendre, damping, ranks)
    scale = 1.0 / math.sqrt(groups * lat * NLON)
    grad_in, grad_bias, grad_out = finish(parts, hid, chans, groups, scale)
    return (grad_state[None], grad_in.T, grad_bias[0], grad_out)


def solution(mesh):
    in_specs = (
        P("grp", "lat", None, None),
        P("grp", "lat", None, None),
        P("lat", None, None),
        P(),
        P(),
        P(),
        P(),
        P(),
    )
    out_specs = (P("grp", "lat", None, None), P(), P(), P())
    return jax.shard_map(body, mesh=mesh, in_specs=in_specs, out_specs=out_specs, check_vma=False)
```

```python
import functools
import math

import jax
import jax.numpy as jnp
import numpy as np
import ml_dtypes
from jax import lax
from jax.experimental import pallas as pl
from jax.experimental.pallas import tpu as pltpu
from jax.sharding import PartitionSpec as P

NLON = 2560
MIB = 1024 * 1024
F32 = jnp.float32
BF16 = jnp.bfloat16
PARTS = 2
SLOTS = 256
HBM = pl.BlockSpec(memory_space=pl.ANY)


def longitude_tables(waves, points):
    slots = points // 2
    phase = np.arange(slots)[:, None] * np.arange(waves)[None, :] % points
    angle = phase * (2.0 * math.pi / points)
    scale = math.sqrt(2.0 / points)
    both = np.concatenate([np.cos(angle) * scale, -np.sin(angle) * scale], axis=1)
    both = both.astype(np.float32).astype(ml_dtypes.bfloat16).reshape(-1, SLOTS, 2 * waves)
    return both, np.ascontiguousarray(both.swapaxes(1, 2))


def dot(a, b):
    return jnp.dot(a, b, preferred_element_type=F32)


def dot_nt(a, b):
    return lax.dot_general(a, b, (((1,), (1,)), ((), ())), preferred_element_type=F32)


def params(mib):
    return pltpu.CompilerParams(vmem_limit_bytes=mib * MIB, dimension_semantics=("arbitrary",))


def whole(*shape):
    return pl.BlockSpec(shape, lambda i: (0,) * len(shape))


def block_of(waves):
    return max(size for size in range(1, 9) if waves % size == 0)


def set_factor(factor, damping):
    width, degrees = factor.shape
    chans = width // 2
    lanes = 128
    spread = jnp.broadcast_to(damping[...], (lanes, chans)).T
    for start in range(0, degrees, lanes):
        degree = (lax.broadcasted_iota(jnp.int32, (chans, lanes), 1) + start).astype(F32)
        ratio = degree * (degree + 1.0) / (degrees * (degrees + 1.0))
        piece = 1.0 / (1.0 + spread * ratio)
        factor[:chans, start : start + lanes] = piece
        factor[chans:, start : start + lanes] = piece


def copies_of(pairs, sems):
    copies = [pltpu.make_async_copy(src, dst, sems.at[k]) for k, (src, dst) in enumerate(pairs)]
    for copy in copies:
        copy.start()
    return copies


def forward_kernel(ranks, block, ahead, *refs):
    spec_h, cot_h, leg_h, damping, quad = refs[:5]
    outs = refs[5 : 5 + PARTS]
    spec, cot, leg, rows, factor, sems = refs[5 + PARTS :]
    own, width, _ = spec.shape
    chans = width // 2
    lat = leg.shape[2]
    near = lat // ranks // 2 // PARTS

    def moves(c):
        here = pl.ds(c * block, block)
        return [
            pltpu.make_async_copy(src.at[here], dst.at[here], sems.at[c, k])
            for k, (src, dst) in enumerate(((spec_h, spec), (cot_h, cot), (leg_h, leg)))
        ]

    for c in range(min(ahead, own // block)):
        for move in moves(c):
            move.start()
    set_factor(factor, damping)

    def step(c, carry):
        for move in moves(c):
            move.wait()

        @pl.when(c + ahead < own // block)
        def _():
            for move in moves(c + ahead):
                move.start()

        weight = quad[...]
        for k in range(block):
            i = c * block + k
            tend = (cot[i].astype(F32) * factor[...]).astype(BF16)
            state = spec[i]
            stacked = jnp.concatenate(
                [state[:chans], tend[:chans], state[chans:], tend[chans:]], axis=0
            )
            res = dot(stacked, leg[i])
            res = jnp.concatenate(
                [
                    res[:chans],
                    res[chans : 2 * chans] * weight,
                    res[2 * chans : 3 * chans],
                    res[3 * chans :] * weight,
                ],
                axis=0,
            )
            rows[pl.ds(i, lat, stride=own), :] = res.T
        return carry

    lax.fori_loop(0, own // block, step, 0)
    size = near * own
    for part in range(PARTS):
        for d in range(ranks):
            for side in range(2):
                start = ((side * PARTS + part) * ranks + d) * size
                outs[part][d, side * size : (side + 1) * size, :] = rows[
                    start : start + size, :
                ].astype(BF16)


def forward(spectral, cot, legendre, damping, quad, ranks):
    own, width, degrees = spectral.shape
    lat = legendre.shape[2]
    block = block_of(own)
    shape = (ranks, lat // ranks // PARTS * own, 2 * width)
    return pl.pallas_call(
        functools.partial(forward_kernel, ranks, block, own // block),
        grid=(1,),
        in_specs=[HBM] * 3 + [whole(*damping.shape), whole(1, lat)],
        out_specs=[whole(*shape)] * PARTS,
        out_shape=[jax.ShapeDtypeStruct(shape, BF16)] * PARTS,
        scratch_shapes=[
            pltpu.VMEM(spectral.shape, BF16),
            pltpu.VMEM(cot.shape, BF16),
            pltpu.VMEM(legendre.shape, BF16),
            pltpu.VMEM((lat * own, 2 * width), F32),
            pltpu.VMEM((width, degrees), F32),
            pltpu.SemaphoreType.DMA((own // block, 3)),
        ],
        compiler_params=params(60),
        name="legendre_forward",
    )(spectral, cot, legendre, damping, quad)


def column_kernel(ranks, own, first, last, *refs):
    given = 6 if first else 7
    sources, out = refs[:given], refs[given]
    refs = refs[given + 1 :]
    if not last:
        after, refs = refs[0], refs[1:]
    arrived, table, turned_table, w_in, bias, w_out, sums = refs[:7]
    fourier, cols, weights, acts, evens, odds, edge, modes, sems = refs[7:]
    chans, hid = w_in.shape
    waves = ranks * own
    lat_rows = arrived.shape[1] // own
    near = lat_rows // 2
    chunks, half, _ = table.shape
    size = 2 * half
    points = size * chunks
    scale = math.sqrt(2.0 / points)
    width = 2 * chans
    unit = 64
    arrived_h, table_h, turned_h, w_in_h, bias_h, w_out_h = sources[:6]
    pairs = [(arrived_h, arrived), (w_in_h, w_in), (bias_h, bias), (w_out_h, w_out)]
    if not first:
        pairs.append((sources[6], sums))
    small = copies_of(pairs, sems)

    def moves(c):
        return [
            pltpu.make_async_copy(table_h.at[c], table.at[c], sems.at[5 + 2 * c]),
            pltpu.make_async_copy(turned_h.at[c], turned_table.at[c], sems.at[6 + 2 * c]),
        ]

    for c in range(min(2, chunks)):
        for move in moves(c):
            move.start()
    modes[...] = jnp.zeros_like(modes)
    cols[width:, :] = jnp.ones((16, cols.shape[1]), BF16)
    for copy in small:
        copy.wait()
    if first:
        sums[...] = jnp.zeros_like(sums)
    for p in range(0, lat_rows, 2):
        pair = [
            jnp.concatenate(
                [arrived[s, i * own : (i + 1) * own, :] for s in range(ranks)], axis=0
            )
            for i in (p, p + 1)
        ]
        here = slice(width * p, width * (p + 2))
        fourier[:waves, here] = jnp.concatenate([piece[:, :width] for piece in pair], axis=1)
        fourier[waves:, here] = jnp.concatenate([piece[:, width:] for piece in pair], axis=1)
    wave = lax.broadcasted_iota(jnp.int32, (16, waves), 1)
    alternate = jnp.where(wave % 2 == 0, scale, -scale).astype(BF16)
    middle = dot(alternate, fourier[:waves, :])[:1]
    half_bias = bias[...] * 0.5
    high = half_bias.astype(BF16).astype(F32)
    left = half_bias - high
    mid = left.astype(BF16).astype(F32)
    low = left - mid
    stack = jnp.concatenate(
        [
            w_in[...].astype(F32) * 0.5,
            w_out[...].astype(F32) * 0.5,
            high,
            mid,
            low,
            jnp.zeros((13, hid), F32),
        ],
        axis=0,
    ).T.astype(BF16)
    lane = lax.broadcasted_iota(jnp.int32, stack.shape, 1)
    is_out = (lane >= chans) & (lane < width)
    nothing = jnp.zeros_like(stack)
    inward = jnp.where(is_out, nothing, stack)
    outward = jnp.where(is_out, stack, nothing)
    for k in range(0, hid, unit):
        weights[2 * k : 2 * k + unit, :] = inward[k : k + unit]
        weights[2 * k + unit : 2 * k + 2 * unit, :] = outward[k : k + unit]

    def step(c, carry):
        for move in moves(c):
            move.wait()

        @pl.when(c + 2 < chunks)
        def _():
            for move in moves(c + 2):
                move.start()

        begins = c == 0
        even = dot(table[c, :, :waves], fourier[:waves, :])
        odd = dot(table[c, :, waves:], fourier[waves:, :])
        slot = lax.broadcasted_iota(jnp.int32, even.shape, 0)
        mirror = jnp.where((slot == 0) & begins, middle, even - odd)
        front = (even + odd).astype(BF16).T
        rear = mirror.astype(BF16).T
        for p in range(lat_rows):
            here = slice(width * p, width * (p + 1))
            cols[:width, p * size : p * size + half] = front[here]
            cols[:width, p * size + half : (p + 1) * size] = rear[here]
        for p in range(lat_rows):
            here = slice(p * size, (p + 1) * size)
            for k in range(0, hid, unit):
                both = dot(weights[2 * k : 2 * k + 2 * unit, :], cols[:, here]).astype(BF16)
                arg = both[:unit]
                th = jnp.tanh(arg)
                rise = 1 + th
                act = arg * rise
                acts[k : k + unit, here] = act
                acts[hid + k : hid + k + unit, here] = both[unit:] * (rise + act * (1 - th))
            grad = dot(w_in[...], acts[hid:, here])
            front, rear = grad[:, :half], grad[:, half:]
            rows = slice(chans * p, chans * (p + 1))

            @pl.when(begins)
            def _():
                edge[rows, :] = rear[:, : edge.shape[1]].astype(BF16)

            slot = lax.broadcasted_iota(jnp.int32, rear.shape, 1)
            evens[rows, :] = (front + jnp.where((slot == 0) & begins, 0.0, rear)).astype(BF16)
            odds[rows, :] = (front - rear).astype(BF16)
        sums[...] += dot_nt(acts[...], cols[...])
        modes[:waves, :] += dot_nt(turned_table[c, :waves, :], evens[...])
        modes[waves:, :] += dot_nt(turned_table[c, waves:, :], odds[...])
        return carry

    lax.fori_loop(0, chunks, step, 0)

    wave = lax.broadcasted_iota(jnp.int32, (waves, edge.shape[1]), 0)
    lane = lax.broadcasted_iota(jnp.int32, (waves, edge.shape[1]), 1)
    alternate = jnp.where(lane == 0, jnp.where(wave % 2 == 0, scale, -scale), 0.0).astype(BF16)
    real = (modes[:waves] + dot_nt(alternate, edge[...])).astype(BF16)
    imag = modes[waves:].astype(BF16)
    span = near * chans
    for q in range(near):
        a, b = q * chans, (q + 1) * chans
        piece = jnp.concatenate(
            [real[:, a:b], imag[:, a:b], real[:, span + a : span + b], imag[:, span + a : span + b]],
            axis=1,
        )
        for d in range(ranks):
            out[d, q * own : (q + 1) * own, :] = piece[d * own : (d + 1) * own]
    if not last:
        after[...] = sums[...]
        return
    base = near * own
    turned = sums[...].T
    main = jnp.concatenate([turned[:chans, hid:], turned[chans:width, :hid]], axis=0)
    total = turned[width : width + 1, hid:]
    lanes = 4 * chans
    cuts = range(0, hid, lanes)
    tail = [total[:, c : c + lanes] for c in cuts]
    share = width // ranks
    for d in range(ranks):
        rows = [main[d * share : (d + 1) * share, c : c + lanes] for c in cuts]
        rows = jnp.concatenate(rows + tail, axis=0).astype(BF16)
        out[d, base : base + rows.shape[0], :] = rows


def columns(arrived, tables, w_in, bias, w_out, before, ranks, own, last):
    chans, hid = w_in.shape
    lat_rows = arrived.shape[1] // own
    waves = ranks * own
    chunks, half, _ = tables[0].shape
    size = 2 * half
    rows_out = lat_rows // 2 * own
    lanes = 4 * chans
    if last:
        rows_out += (hid // lanes) * (2 * chans // ranks) + hid // lanes
    sums = (2 * hid, 2 * chans + 16)
    out_specs = [whole(ranks, rows_out, lanes)]
    out_shape = [jax.ShapeDtypeStruct((ranks, rows_out, lanes), BF16)]
    if not last:
        out_specs.append(whole(*sums))
        out_shape.append(jax.ShapeDtypeStruct(sums, F32))
    sources = [arrived, *tables, w_in, bias, w_out] + before
    result = pl.pallas_call(
        functools.partial(column_kernel, ranks, own, not before, last),
        grid=(1,),
        in_specs=[HBM] * len(sources),
        out_specs=out_specs,
        out_shape=out_shape,
        scratch_shapes=[
            pltpu.VMEM(arrived.shape, BF16),
            pltpu.VMEM(tables[0].shape, BF16),
            pltpu.VMEM(tables[1].shape, BF16),
            pltpu.VMEM(w_in.shape, BF16),
            pltpu.VMEM(bias.shape, F32),
            pltpu.VMEM(w_out.shape, BF16),
            pltpu.VMEM(sums, F32),
            pltpu.VMEM((2 * waves, 2 * chans * lat_rows), BF16),
            pltpu.VMEM((2 * chans + 16, lat_rows * size), BF16),
            pltpu.VMEM((2 * hid, 2 * chans + 16), BF16),
            pltpu.VMEM((2 * hid, lat_rows * size), BF16),
            pltpu.VMEM((chans * lat_rows, half), BF16),
            pltpu.VMEM((chans * lat_rows, half), BF16),
            pltpu.VMEM((chans * lat_rows, 128), BF16),
            pltpu.VMEM((2 * waves, chans * lat_rows), F32),
            pltpu.SemaphoreType.DMA((5 + 2 * chunks,)),
        ],
        compiler_params=params(60),
        name="column_physics",
    )(*sources)
    return result[0], list(result[1:])


def backward_kernel(ranks, near, block, ahead, *refs):
    arrived_h, refs = refs[:PARTS], refs[PARTS:]
    cot_h, leg_h, damping, out_h = refs[:4]
    arrived, refs = refs[4 : 4 + PARTS], refs[4 + PARTS :]
    cot, leg, out, rows, factor, in_sems, out_sems, sems = refs
    own, width, _ = cot.shape
    size = near * own
    early = copies_of(zip(arrived_h, arrived), sems)

    def moves(c):
        here = pl.ds(c * block, block)
        return [
            pltpu.make_async_copy(src.at[here], dst.at[here], in_sems.at[c, k])
            for k, (src, dst) in enumerate(((cot_h, cot), (leg_h, leg)))
        ]

    def leave(c):
        here = pl.ds(c * block, block)
        return pltpu.make_async_copy(out.at[here], out_h.at[here], out_sems.at[c])

    for c in range(min(ahead, own // block)):
        for move in moves(c):
            move.start()
    set_factor(factor, damping)
    for part in range(PARTS):
        early[part].wait()
        for s in range(ranks):
            row = (part * ranks + s) * size
            rows[row : row + size, :] = arrived[part][s, :size, :].astype(F32)

    def step(c, carry):
        for move in moves(c):
            move.wait()

        @pl.when(c + ahead < own // block)
        def _():
            for move in moves(c + ahead):
                move.start()

        for k in range(block):
            i = c * block + k
            mine = rows[pl.ds(i, PARTS * ranks * near, stride=own), :]
            mine = mine.T.astype(BF16)
            lhs = jnp.concatenate([mine[:width], mine[width:]], axis=1)
            out[i] = cot[i].astype(F32) * factor[...] + dot_nt(lhs, leg[i])
        leave(c).start()
        return carry

    lax.fori_loop(0, own // block, step, 0)
    for c in range(own // block):
        leave(c).wait()


def backward(arrived, cot, legendre, damping, ranks):
    own, width, degrees = cot.shape
    lat = legendre.shape[2]
    near = lat // ranks // 2 // PARTS
    block = block_of(own)
    return pl.pallas_call(
        functools.partial(backward_kernel, ranks, near, block, 3),
        grid=(1,),
        in_specs=[HBM] * (PARTS + 2) + [whole(*damping.shape)],
        out_specs=HBM,
        out_shape=jax.ShapeDtypeStruct((own, width, degrees), F32),
        scratch_shapes=[pltpu.VMEM(piece.shape, BF16) for piece in arrived]
        + [
            pltpu.VMEM(cot.shape, BF16),
            pltpu.VMEM(legendre.shape, BF16),
            pltpu.VMEM(cot.shape, F32),
            pltpu.VMEM((PARTS * ranks * near * own, 2 * width), F32),
            pltpu.VMEM((width, degrees), F32),
            pltpu.SemaphoreType.DMA((own // block, 2)),
            pltpu.SemaphoreType.DMA((own // block,)),
            pltpu.SemaphoreType.DMA((PARTS,)),
        ],
        compiler_params=params(60),
        name="legendre_backward",
    )(*arrived, cot, legendre, damping)


def collect_kernel(base, arrived, out):
    total = arrived[0, base:, :].astype(F32)
    for s in range(1, arrived.shape[0]):
        total = total + arrived[s, base:, :].astype(F32)
    for s in range(out.shape[0]):
        out[s] = total


def collect(arrived, base, copies):
    shape = (copies, arrived.shape[1] - base, arrived.shape[2])
    return pl.pallas_call(
        functools.partial(collect_kernel, base),
        grid=(1,),
        in_specs=[whole(*arrived.shape)],
        out_specs=whole(*shape),
        out_shape=jax.ShapeDtypeStruct(shape, F32),
        compiler_params=params(60),
        name="collect_gradients",
    )(arrived)


def finish_kernel(groups, scale, parts, grad_in, grad_bias, grad_out):
    ranks = parts.shape[0] // groups
    chans, hid = grad_in.shape
    lanes = parts.shape[2]
    cuts = hid // lanes
    share = 2 * chans // ranks
    for r in range(ranks):
        total = parts[r]
        for g in range(1, groups):
            total = total + parts[g * ranks + r]
        total = total * scale
        row = r * share
        dest, row = (grad_in, row) if row < chans else (grad_out, row - chans)
        for c in range(cuts):
            dest[row : row + share, c * lanes : (c + 1) * lanes] = total[c * share : (c + 1) * share]
        if r == 0:
            for c in range(cuts):
                grad_bias[:, c * lanes : (c + 1) * lanes] = total[cuts * share + c : cuts * share + c + 1]


def finish(parts, hid, chans, groups, scale):
    return pl.pallas_call(
        functools.partial(finish_kernel, groups, scale),
        grid=(1,),
        in_specs=[whole(*parts.shape)],
        out_specs=(whole(chans, hid), whole(1, hid), whole(chans, hid)),
        out_shape=(
            jax.ShapeDtypeStruct((chans, hid), F32),
            jax.ShapeDtypeStruct((1, hid), F32),
            jax.ShapeDtypeStruct((chans, hid), F32),
        ),
        compiler_params=params(60),
        name="weight_gradients",
    )(parts)


def body(
    spectral_state, cotangent, legendre, quadrature, damping, physics_in, physics_bias, physics_out
):
    spectral = spectral_state[0]
    cot = cotangent[0]
    own, width, degrees = spectral.shape
    chans = width // 2
    hid = physics_in.shape[0]
    ranks = lax.axis_size("lat")
    groups = lax.axis_size("grp")
    lat = legendre.shape[2]
    lat_rows = lat // ranks
    tables = [jnp.asarray(table) for table in longitude_tables(own * ranks, NLON)]
    damping = damping[None, :]
    exchange = functools.partial(
        lax.all_to_all, axis_name="lat", split_axis=0, concat_axis=0, tiled=True
    )

    sent = forward(spectral, cot, legendre, damping, quadrature[None, :], ranks)
    arrived = [exchange(piece) for piece in sent]
    sums = []
    returned = []
    for part in range(PARTS):
        back, sums = columns(
            arrived[part],
            tables,
            physics_in.T,
            physics_bias[None, :],
            physics_out,
            sums,
            ranks,
            own,
            part == PARTS - 1,
        )
        if returned:
            back, returned[-1] = lax.optimization_barrier((back, returned[-1]))
        returned.append(exchange(back))

    base = lat_rows // 2 // PARTS * own
    spread = collect(returned[-1], base, groups * ranks)
    parts = lax.all_to_all(spread, ("grp", "lat"), split_axis=0, concat_axis=0, tiled=True)
    grad_state = backward(returned, cot, legendre, damping, ranks)
    scale = 1.0 / math.sqrt(groups * lat * NLON)
    grad_in, grad_bias, grad_out = finish(parts, hid, chans, groups, scale)
    return (grad_state[None], grad_in.T, grad_bias[0], grad_out)


def solution(mesh):
    in_specs = (
        P("grp", "lat", None, None),
        P("grp", "lat", None, None),
        P("lat", None, None),
        P(),
        P(),
        P(),
        P(),
        P(),
    )
    out_specs = (P("grp", "lat", None, None), P(), P(), P())
    return jax.shard_map(body, mesh=mesh, in_specs=in_specs, out_specs=out_specs, check_vma=False)
```

```python
import functools
import math

import jax
import jax.numpy as jnp
import numpy as np
import ml_dtypes
from jax import lax
from jax.experimental import pallas as pl
from jax.experimental.pallas import tpu as pltpu
from jax.sharding import PartitionSpec as P

NLON = 2560
MIB = 1024 * 1024
F32 = jnp.float32
BF16 = jnp.bfloat16
PARTS = 2
SLOTS = 256
SPAN = 512
UNIT = 64
HBM = pl.BlockSpec(memory_space=pl.ANY)


def longitude_table(waves, points):
    slots = points // 2
    phase = np.arange(waves)[:, None] * np.arange(slots)[None, :] % points
    angle = phase * (2.0 * math.pi / points)
    scale = math.sqrt(2.0 / points)
    both = np.concatenate([np.cos(angle) * scale, -np.sin(angle) * scale])
    return both.astype(np.float32).astype(ml_dtypes.bfloat16)


def dot(a, b):
    return jnp.dot(a, b, preferred_element_type=F32)


def dot_nt(a, b):
    return lax.dot_general(a, b, (((1,), (1,)), ((), ())), preferred_element_type=F32)


def params(mib):
    return pltpu.CompilerParams(vmem_limit_bytes=mib * MIB, dimension_semantics=("arbitrary",))


def whole(*shape):
    return pl.BlockSpec(shape, lambda i: (0,) * len(shape))


def block_of(waves):
    return max(size for size in range(1, 9) if waves % size == 0)


def set_factor(factor, damping):
    width, degrees = factor.shape
    chans = width // 2
    lanes = 128
    spread = jnp.broadcast_to(damping[...], (lanes, chans)).T
    for start in range(0, degrees, lanes):
        degree = (lax.broadcasted_iota(jnp.int32, (chans, lanes), 1) + start).astype(F32)
        ratio = degree * (degree + 1.0) / (degrees * (degrees + 1.0))
        piece = 1.0 / (1.0 + spread * ratio)
        factor[:chans, start : start + lanes] = piece
        factor[chans:, start : start + lanes] = piece


def copies_of(pairs, sems):
    copies = [pltpu.make_async_copy(src, dst, sems.at[k]) for k, (src, dst) in enumerate(pairs)]
    for copy in copies:
        copy.start()
    return copies


def forward_kernel(ranks, block, ahead, *refs):
    spec_h, cot_h, leg_h, damping, quad = refs[:5]
    outs = refs[5 : 5 + PARTS]
    spec, cot, leg, rows, factor, sems = refs[5 + PARTS :]
    own, width, _ = spec.shape
    chans = width // 2
    lat = leg.shape[2]
    near = lat // ranks // 2 // PARTS

    def moves(c):
        here = pl.ds(c * block, block)
        return [
            pltpu.make_async_copy(src.at[here], dst.at[here], sems.at[c, k])
            for k, (src, dst) in enumerate(((spec_h, spec), (cot_h, cot), (leg_h, leg)))
        ]

    for c in range(min(ahead, own // block)):
        for move in moves(c):
            move.start()
    set_factor(factor, damping)

    def step(c, carry):
        for move in moves(c):
            move.wait()

        @pl.when(c + ahead < own // block)
        def _():
            for move in moves(c + ahead):
                move.start()

        weight = quad[...]
        for k in range(block):
            i = c * block + k
            tend = (cot[i].astype(F32) * factor[...]).astype(BF16)
            state = spec[i]
            stacked = jnp.concatenate(
                [state[:chans], tend[:chans], state[chans:], tend[chans:]], axis=0
            )
            res = dot(stacked, leg[i])
            res = jnp.concatenate(
                [
                    res[:chans],
                    res[chans : 2 * chans] * weight,
                    res[2 * chans : 3 * chans],
                    res[3 * chans :] * weight,
                ],
                axis=0,
            )
            rows[pl.ds(i, lat, stride=own), :] = res.astype(BF16).T.astype(F32)
        return carry

    lax.fori_loop(0, own // block, step, 0)
    size = near * own
    for part in range(PARTS):
        for d in range(ranks):
            for side in range(2):
                start = ((side * PARTS + part) * ranks + d) * size
                outs[part][d, side * size : (side + 1) * size, :] = rows[
                    start : start + size, :
                ].astype(BF16)


def forward(spectral, cot, legendre, damping, quad, ranks):
    own, width, degrees = spectral.shape
    lat = legendre.shape[2]
    block = block_of(own)
    shape = (ranks, lat // ranks // PARTS * own, 2 * width)
    return pl.pallas_call(
        functools.partial(forward_kernel, ranks, block, own // block),
        grid=(1,),
        in_specs=[HBM] * 3 + [whole(*damping.shape), whole(1, lat)],
        out_specs=[whole(*shape)] * PARTS,
        out_shape=[jax.ShapeDtypeStruct(shape, BF16)] * PARTS,
        scratch_shapes=[
            pltpu.VMEM(spectral.shape, BF16),
            pltpu.VMEM(cot.shape, BF16),
            pltpu.VMEM(legendre.shape, BF16),
            pltpu.VMEM((lat * own, 2 * width), F32),
            pltpu.VMEM((width, degrees), F32),
            pltpu.SemaphoreType.DMA((own // block, 3)),
        ],
        compiler_params=params(60),
        name="legendre_forward",
    )(spectral, cot, legendre, damping, quad)


def column_kernel(ranks, own, first, last, *refs):
    given = 5 if first else 6
    sources, out = refs[:given], refs[given]
    refs = refs[given + 1 :]
    if not last:
        after, refs = refs[0], refs[1:]
    arrived, table, w_in, bias, w_out, sums = refs[:6]
    fourier, cols, weights, acts, evens, odds, edge, sems = refs[6:]
    chans, hid = w_in.shape
    waves = ranks * own
    lat_rows = arrived.shape[1] // own
    near = lat_rows // 2
    slots = table.shape[1]
    points = 2 * slots
    scale = math.sqrt(2.0 / points)
    width = 2 * chans
    arrived_h, table_h, w_in_h, bias_h, w_out_h = sources[:5]
    pairs = [(arrived_h, arrived), (w_in_h, w_in), (bias_h, bias), (w_out_h, w_out)]
    if not first:
        pairs.append((sources[5], sums))
    small = copies_of(pairs, sems)
    moves = []
    for c in range(slots // SLOTS):
        here = pl.ds(c * SLOTS, SLOTS)
        moves.append(
            pltpu.make_async_copy(table_h.at[:, here], table.at[:, here], sems.at[5 + c])
        )
        moves[c].start()
    for p in range(lat_rows):
        cols[p, width:, :] = jnp.ones((16, points), BF16)
    for copy in small:
        copy.wait()
    if first:
        sums[...] = jnp.zeros_like(sums)
    for p in range(lat_rows):
        piece = jnp.concatenate(
            [arrived[s, p * own : (p + 1) * own, :] for s in range(ranks)], axis=0
        ).T
        row = width * p
        fourier[row : row + width, :waves] = piece[:width]
        fourier[row : row + width, waves:] = piece[width:]
    half_bias = bias[...] * 0.5
    high = half_bias.astype(BF16).astype(F32)
    left = half_bias - high
    mid = left.astype(BF16).astype(F32)
    low = left - mid
    stack = jnp.concatenate(
        [
            w_in[...].astype(F32) * 0.5,
            w_out[...].astype(F32) * 0.5,
            high,
            mid,
            low,
            jnp.zeros((13, hid), F32),
        ],
        axis=0,
    ).T.astype(BF16)
    lane = lax.broadcasted_iota(jnp.int32, stack.shape, 1)
    is_out = (lane >= chans) & (lane < width)
    nothing = jnp.zeros_like(stack)
    inward = jnp.where(is_out, nothing, stack)
    outward = jnp.where(is_out, stack, nothing)
    for k in range(0, hid, UNIT):
        weights[2 * k : 2 * k + UNIT, :] = inward[k : k + UNIT]
        weights[2 * k + UNIT : 2 * k + 2 * UNIT, :] = outward[k : k + UNIT]

    wave = lax.broadcasted_iota(jnp.int32, (waves, 128), 0)
    lane = lax.broadcasted_iota(jnp.int32, (waves, 128), 1)
    alternate = jnp.where(lane == 0, jnp.where(wave % 2 == 0, scale, -scale), 0.0).astype(BF16)
    for c, move in enumerate(moves):
        move.wait()
        here = slice(c * SLOTS, (c + 1) * SLOTS)
        even = dot(fourier[:, :waves], table[:waves, here])
        odd = dot(fourier[:, waves:], table[waves:, here])
        front = (even + odd).astype(BF16)
        rear = even - odd
        if c == 0:
            middle = dot(fourier[:, :waves], alternate)
            lane = lax.broadcasted_iota(jnp.int32, middle.shape, 1)
            rear = jnp.concatenate(
                [jnp.where(lane == 0, middle, rear[:, :128]), rear[:, 128:]], axis=1
            )
        rear = rear.astype(BF16)
        there = slice(slots + c * SLOTS, slots + (c + 1) * SLOTS)
        for p in range(lat_rows):
            cols[p, :width, here] = front[width * p : width * (p + 1)]
            cols[p, :width, there] = rear[width * p : width * (p + 1)]

    together = acts.shape[0]

    def rows_step(g, carry):
        for r in range(together):
            p = g * together + r
            for n in range(0, points, SPAN):
                here = slice(n, n + SPAN)
                columns_here = cols[p, :, here]
                for k in range(0, hid, UNIT):
                    both = dot(weights[2 * k : 2 * k + 2 * UNIT, :], columns_here).astype(BF16)
                    arg = both[:UNIT]
                    th = jnp.tanh(arg)
                    rise = 1 + th
                    act = arg * rise
                    acts[r, k : k + UNIT, here] = act
                    acts[r, hid + k : hid + k + UNIT, here] = both[UNIT:] * (
                        rise + act * (1 - th)
                    )
            grad = dot(w_in[...], acts[r, hid:, :])
            front, rear = grad[:, :slots], grad[:, slots:]
            edge[p] = rear[:, :128].astype(BF16)
            slot = lax.broadcasted_iota(jnp.int32, rear.shape, 1)
            evens[p] = (front + jnp.where(slot == 0, 0.0, rear)).astype(BF16)
            odds[p] = (front - rear).astype(BF16)
            sums[...] += dot_nt(acts[r], cols[p])
        return carry

    lax.fori_loop(0, lat_rows // together, rows_step, 0)

    def joined(ref):
        return ref[...].reshape(chans * lat_rows, ref.shape[2])

    real = dot_nt(table[:waves, :], joined(evens)) + dot_nt(alternate, joined(edge))
    real = real.astype(BF16)
    imag = dot_nt(table[waves:, :], joined(odds)).astype(BF16)
    span = near * chans
    for q in range(near):
        a, b = q * chans, (q + 1) * chans
        piece = jnp.concatenate(
            [real[:, a:b], imag[:, a:b], real[:, span + a : span + b], imag[:, span + a : span + b]],
            axis=1,
        )
        for d in range(ranks):
            out[d, q * own : (q + 1) * own, :] = piece[d * own : (d + 1) * own]
    if not last:
        after[...] = sums[...]
        return
    base = near * own
    turned = sums[...].T
    main = jnp.concatenate([turned[:chans, hid:], turned[chans:width, :hid]], axis=0)
    total = turned[width : width + 1, hid:]
    lanes = 4 * chans
    cuts = range(0, hid, lanes)
    tail = [total[:, c : c + lanes] for c in cuts]
    share = width // ranks
    for d in range(ranks):
        rows = [main[d * share : (d + 1) * share, c : c + lanes] for c in cuts]
        rows = jnp.concatenate(rows + tail, axis=0).astype(BF16)
        out[d, base : base + rows.shape[0], :] = rows


def columns(arrived, table, w_in, bias, w_out, before, ranks, own, last):
    chans, hid = w_in.shape
    lat_rows = arrived.shape[1] // own
    waves = ranks * own
    slots = table.shape[1]
    points = 2 * slots
    together = 2
    rows_out = lat_rows // 2 * own
    lanes = 4 * chans
    if last:
        rows_out += (hid // lanes) * (2 * chans // ranks) + hid // lanes
    sums = (2 * hid, 2 * chans + 16)
    out_specs = [whole(ranks, rows_out, lanes)]
    out_shape = [jax.ShapeDtypeStruct((ranks, rows_out, lanes), BF16)]
    if not last:
        out_specs.append(whole(*sums))
        out_shape.append(jax.ShapeDtypeStruct(sums, F32))
    sources = [arrived, table, w_in, bias, w_out] + before
    result = pl.pallas_call(
        functools.partial(column_kernel, ranks, own, not before, last),
        grid=(1,),
        in_specs=[HBM] * len(sources),
        out_specs=out_specs,
        out_shape=out_shape,
        scratch_shapes=[
            pltpu.VMEM(arrived.shape, BF16),
            pltpu.VMEM(table.shape, BF16),
            pltpu.VMEM(w_in.shape, BF16),
            pltpu.VMEM(bias.shape, F32),
            pltpu.VMEM(w_out.shape, BF16),
            pltpu.VMEM(sums, F32),
            pltpu.VMEM((2 * chans * lat_rows, 2 * waves), BF16),
            pltpu.VMEM((lat_rows, 2 * chans + 16, points), BF16),
            pltpu.VMEM((2 * hid, 2 * chans + 16), BF16),
            pltpu.VMEM((together, 2 * hid, points), BF16),
            pltpu.VMEM((lat_rows, chans, slots), BF16),
            pltpu.VMEM((lat_rows, chans, slots), BF16),
            pltpu.VMEM((lat_rows, chans, 128), BF16),
            pltpu.SemaphoreType.DMA((5 + slots // SLOTS,)),
        ],
        compiler_params=params(60),
        name="column_physics",
    )(*sources)
    return result[0], list(result[1:])


def backward_kernel(ranks, near, block, ahead, *refs):
    arrived_h, refs = refs[:PARTS], refs[PARTS:]
    cot_h, leg_h, damping, out_h = refs[:4]
    arrived, refs = refs[4 : 4 + PARTS], refs[4 + PARTS :]
    cot, leg, out, rows, factor, in_sems, out_sems, sems = refs
    own, width, _ = cot.shape
    size = near * own
    early = copies_of(zip(arrived_h, arrived), sems)

    def moves(c):
        here = pl.ds(c * block, block)
        return [
            pltpu.make_async_copy(src.at[here], dst.at[here], in_sems.at[c, k])
            for k, (src, dst) in enumerate(((cot_h, cot), (leg_h, leg)))
        ]

    def leave(c):
        here = pl.ds(c * block, block)
        return pltpu.make_async_copy(out.at[here], out_h.at[here], out_sems.at[c])

    for c in range(min(ahead, own // block)):
        for move in moves(c):
            move.start()
    set_factor(factor, damping)
    for part in range(PARTS):
        early[part].wait()
        for s in range(ranks):
            row = (part * ranks + s) * size
            rows[row : row + size, :] = arrived[part][s, :size, :].astype(F32)

    def step(c, carry):
        for move in moves(c):
            move.wait()

        @pl.when(c + ahead < own // block)
        def _():
            for move in moves(c + ahead):
                move.start()

        group = 2 if block % 2 == 0 else 1
        count = PARTS * ranks * near
        for k in range(0, block, group):
            members = [c * block + k + j for j in range(group)]
            mine = [rows[pl.ds(i, count, stride=own), :].astype(BF16) for i in members]
            mine = jnp.concatenate(mine, axis=0).T
            for j, i in enumerate(members):
                here = slice(j * count, (j + 1) * count)
                lhs = jnp.concatenate([mine[:width, here], mine[width:, here]], axis=1)
                out[i] = cot[i].astype(F32) * factor[...] + dot_nt(lhs, leg[i])
        leave(c).start()
        return carry

    lax.fori_loop(0, own // block, step, 0)
    for c in range(own // block):
        leave(c).wait()


def backward(arrived, cot, legendre, damping, ranks):
    own, width, degrees = cot.shape
    lat = legendre.shape[2]
    near = lat // ranks // 2 // PARTS
    block = block_of(own)
    return pl.pallas_call(
        functools.partial(backward_kernel, ranks, near, block, 2),
        grid=(1,),
        in_specs=[HBM] * (PARTS + 2) + [whole(*damping.shape)],
        out_specs=HBM,
        out_shape=jax.ShapeDtypeStruct((own, width, degrees), F32),
        scratch_shapes=[pltpu.VMEM(piece.shape, BF16) for piece in arrived]
        + [
            pltpu.VMEM(cot.shape, BF16),
            pltpu.VMEM(legendre.shape, BF16),
            pltpu.VMEM(cot.shape, F32),
            pltpu.VMEM((PARTS * ranks * near * own, 2 * width), F32),
            pltpu.VMEM((width, degrees), F32),
            pltpu.SemaphoreType.DMA((own // block, 2)),
            pltpu.SemaphoreType.DMA((own // block,)),
            pltpu.SemaphoreType.DMA((PARTS,)),
        ],
        compiler_params=params(60),
        name="legendre_backward",
    )(*arrived, cot, legendre, damping)


def collect_kernel(base, arrived, out):
    total = arrived[0, base:, :].astype(F32)
    for s in range(1, arrived.shape[0]):
        total = total + arrived[s, base:, :].astype(F32)
    for s in range(out.shape[0]):
        out[s] = total


def collect(arrived, base, copies):
    shape = (copies, arrived.shape[1] - base, arrived.shape[2])
    return pl.pallas_call(
        functools.partial(collect_kernel, base),
        grid=(1,),
        in_specs=[whole(*arrived.shape)],
        out_specs=whole(*shape),
        out_shape=jax.ShapeDtypeStruct(shape, F32),
        compiler_params=params(60),
        name="collect_gradients",
    )(arrived)


def finish_kernel(groups, scale, parts, grad_in, grad_bias, grad_out):
    ranks = parts.shape[0] // groups
    chans, hid = grad_in.shape
    lanes = parts.shape[2]
    cuts = hid // lanes
    share = 2 * chans // ranks
    for r in range(ranks):
        total = parts[r]
        for g in range(1, groups):
            total = total + parts[g * ranks + r]
        total = total * scale
        row = r * share
        dest, row = (grad_in, row) if row < chans else (grad_out, row - chans)
        for c in range(cuts):
            dest[row : row + share, c * lanes : (c + 1) * lanes] = total[c * share : (c + 1) * share]
        if r == 0:
            for c in range(cuts):
                grad_bias[:, c * lanes : (c + 1) * lanes] = total[cuts * share + c : cuts * share + c + 1]


def finish(parts, hid, chans, groups, scale):
    return pl.pallas_call(
        functools.partial(finish_kernel, groups, scale),
        grid=(1,),
        in_specs=[whole(*parts.shape)],
        out_specs=(whole(chans, hid), whole(1, hid), whole(chans, hid)),
        out_shape=(
            jax.ShapeDtypeStruct((chans, hid), F32),
            jax.ShapeDtypeStruct((1, hid), F32),
            jax.ShapeDtypeStruct((chans, hid), F32),
        ),
        compiler_params=params(60),
        name="weight_gradients",
    )(parts)


def body(
    spectral_state, cotangent, legendre, quadrature, damping, physics_in, physics_bias, physics_out
):
    spectral = spectral_state[0]
    cot = cotangent[0]
    own, width, degrees = spectral.shape
    chans = width // 2
    hid = physics_in.shape[0]
    ranks = lax.axis_size("lat")
    groups = lax.axis_size("grp")
    lat = legendre.shape[2]
    lat_rows = lat // ranks
    table = jnp.asarray(longitude_table(own * ranks, NLON))
    damping = damping[None, :]
    exchange = functools.partial(
        lax.all_to_all, axis_name="lat", split_axis=0, concat_axis=0, tiled=True
    )

    sent = forward(spectral, cot, legendre, damping, quadrature[None, :], ranks)
    arrived = [exchange(piece) for piece in sent]
    sums = []
    returned = []
    for part in range(PARTS):
        back, sums = columns(
            arrived[part],
            table,
            physics_in.T,
            physics_bias[None, :],
            physics_out,
            sums,
            ranks,
            own,
            part == PARTS - 1,
        )
        if returned:
            back, returned[-1] = lax.optimization_barrier((back, returned[-1]))
        returned.append(exchange(back))

    base = lat_rows // 2 // PARTS * own
    spread = collect(returned[-1], base, groups * ranks)
    parts = lax.all_to_all(spread, ("grp", "lat"), split_axis=0, concat_axis=0, tiled=True)
    grad_state = backward(returned, cot, legendre, damping, ranks)
    scale = 1.0 / math.sqrt(groups * lat * NLON)
    grad_in, grad_bias, grad_out = finish(parts, hid, chans, groups, scale)
    return (grad_state[None], grad_in.T, grad_bias[0], grad_out)


def solution(mesh):
    in_specs = (
        P("grp", "lat", None, None),
        P("grp", "lat", None, None),
        P("lat", None, None),
        P(),
        P(),
        P(),
        P(),
        P(),
    )
    out_specs = (P("grp", "lat", None, None), P(), P(), P())
    return jax.shard_map(body, mesh=mesh, in_specs=in_specs, out_specs=out_specs, check_vma=False)
```

```python
import functools
import math

import jax
import jax.numpy as jnp
import numpy as np
import ml_dtypes
from jax import lax
from jax.experimental import pallas as pl
from jax.experimental.pallas import tpu as pltpu
from jax.sharding import PartitionSpec as P

NLON = 2560
MIB = 1024 * 1024
F32 = jnp.float32
BF16 = jnp.bfloat16
PARTS = 2
SLOTS = 256
SPAN = 512
UNIT = 64
HBM = pl.BlockSpec(memory_space=pl.ANY)


def longitude_table(waves, points):
    slots = points // 2
    phase = np.arange(waves)[:, None] * np.arange(slots)[None, :] % points
    angle = phase * (2.0 * math.pi / points)
    scale = math.sqrt(2.0 / points)
    both = np.concatenate([np.cos(angle) * scale, -np.sin(angle) * scale])
    return both.astype(np.float32).astype(ml_dtypes.bfloat16)


def dot(a, b):
    return jnp.dot(a, b, preferred_element_type=F32)


def dot_nt(a, b):
    return lax.dot_general(a, b, (((1,), (1,)), ((), ())), preferred_element_type=F32)


def params(mib):
    return pltpu.CompilerParams(vmem_limit_bytes=mib * MIB, dimension_semantics=("arbitrary",))


def whole(*shape):
    return pl.BlockSpec(shape, lambda i: (0,) * len(shape))


def block_of(waves):
    return max(size for size in range(1, 9) if waves % size == 0)


def set_factor(factor, damping):
    width, degrees = factor.shape
    chans = width // 2
    lanes = 128
    spread = jnp.broadcast_to(damping[...], (lanes, chans)).T
    for start in range(0, degrees, lanes):
        degree = (lax.broadcasted_iota(jnp.int32, (chans, lanes), 1) + start).astype(F32)
        ratio = degree * (degree + 1.0) / (degrees * (degrees + 1.0))
        piece = 1.0 / (1.0 + spread * ratio)
        factor[:chans, start : start + lanes] = piece
        factor[chans:, start : start + lanes] = piece


def copies_of(pairs, sems):
    copies = [pltpu.make_async_copy(src, dst, sems.at[k]) for k, (src, dst) in enumerate(pairs)]
    for copy in copies:
        copy.start()
    return copies


def forward_kernel(ranks, block, ahead, *refs):
    spec_h, cot_h, leg_h, damping, quad = refs[:5]
    outs = refs[5 : 5 + PARTS]
    spec, cot, leg, rows, factor, sems = refs[5 + PARTS :]
    own, width, _ = spec.shape
    chans = width // 2
    lat = leg.shape[2]
    near = lat // ranks // 2 // PARTS

    def moves(c):
        here = pl.ds(c * block, block)
        return [
            pltpu.make_async_copy(src.at[here], dst.at[here], sems.at[c, k])
            for k, (src, dst) in enumerate(((spec_h, spec), (cot_h, cot), (leg_h, leg)))
        ]

    for c in range(min(ahead, own // block)):
        for move in moves(c):
            move.start()
    set_factor(factor, damping)

    def step(c, carry):
        for move in moves(c):
            move.wait()

        @pl.when(c + ahead < own // block)
        def _():
            for move in moves(c + ahead):
                move.start()

        weight = quad[...]
        group = 2 if block % 2 == 0 else 1
        for k in range(0, block, group):
            members = [c * block + k + j for j in range(group)]
            stacked = []
            for i in members:
                tend = (cot[i].astype(F32) * factor[...]).astype(BF16)
                state = spec[i]
                stacked += [state[:chans], tend[:chans], state[chans:], tend[chans:]]
            product = dot(
                jnp.concatenate(stacked, axis=0),
                jnp.concatenate([leg[i] for i in members], axis=1),
            )
            for j, i in enumerate(members):
                res = product[2 * width * j : 2 * width * (j + 1), lat * j : lat * (j + 1)]
                res = jnp.concatenate(
                    [
                        res[:chans],
                        res[chans : 2 * chans] * weight,
                        res[2 * chans : 3 * chans],
                        res[3 * chans :] * weight,
                    ],
                    axis=0,
                )
                rows[pl.ds(i, lat, stride=own), :] = res.astype(BF16).T.astype(F32)
        return carry

    lax.fori_loop(0, own // block, step, 0)
    size = near * own
    for part in range(PARTS):
        for d in range(ranks):
            for side in range(2):
                start = ((side * PARTS + part) * ranks + d) * size
                outs[part][d, side * size : (side + 1) * size, :] = rows[
                    start : start + size, :
                ].astype(BF16)


def forward(spectral, cot, legendre, damping, quad, ranks):
    own, width, degrees = spectral.shape
    lat = legendre.shape[2]
    block = block_of(own)
    shape = (ranks, lat // ranks // PARTS * own, 2 * width)
    return pl.pallas_call(
        functools.partial(forward_kernel, ranks, block, own // block),
        grid=(1,),
        in_specs=[HBM] * 3 + [whole(*damping.shape), whole(1, lat)],
        out_specs=[whole(*shape)] * PARTS,
        out_shape=[jax.ShapeDtypeStruct(shape, BF16)] * PARTS,
        scratch_shapes=[
            pltpu.VMEM(spectral.shape, BF16),
            pltpu.VMEM(cot.shape, BF16),
            pltpu.VMEM(legendre.shape, BF16),
            pltpu.VMEM((lat * own, 2 * width), F32),
            pltpu.VMEM((width, degrees), F32),
            pltpu.SemaphoreType.DMA((own // block, 3)),
        ],
        compiler_params=params(60),
        name="legendre_forward",
    )(spectral, cot, legendre, damping, quad)


def column_kernel(ranks, own, first, last, *refs):
    given = 5 if first else 6
    sources, out = refs[:given], refs[given]
    refs = refs[given + 1 :]
    if not last:
        after, refs = refs[0], refs[1:]
    arrived, table, w_in, bias, w_out, sums = refs[:6]
    fourier, cols, weights, acts, evens, odds, edge, sems = refs[6:]
    chans, hid = w_in.shape
    waves = ranks * own
    lat_rows = arrived.shape[1] // own
    near = lat_rows // 2
    slots = table.shape[1]
    points = 2 * slots
    scale = math.sqrt(2.0 / points)
    width = 2 * chans
    arrived_h, table_h, w_in_h, bias_h, w_out_h = sources[:5]
    pairs = [(arrived_h, arrived), (w_in_h, w_in), (bias_h, bias), (w_out_h, w_out)]
    if not first:
        pairs.append((sources[5], sums))
    small = copies_of(pairs, sems)
    moves = []
    for c in range(slots // SLOTS):
        here = pl.ds(c * SLOTS, SLOTS)
        moves.append(
            pltpu.make_async_copy(table_h.at[:, here], table.at[:, here], sems.at[5 + c])
        )
        moves[c].start()
    for p in range(lat_rows):
        cols[p, width:, :] = jnp.ones((16, points), BF16)
    for copy in small:
        copy.wait()
    if first:
        sums[...] = jnp.zeros_like(sums)
    for p in range(lat_rows):
        piece = jnp.concatenate(
            [arrived[s, p * own : (p + 1) * own, :] for s in range(ranks)], axis=0
        ).T
        row = width * p
        fourier[row : row + width, :waves] = piece[:width]
        fourier[row : row + width, waves:] = piece[width:]
    half_bias = bias[...] * 0.5
    high = half_bias.astype(BF16).astype(F32)
    left = half_bias - high
    mid = left.astype(BF16).astype(F32)
    low = left - mid
    stack = jnp.concatenate(
        [
            w_in[...].astype(F32) * 0.5,
            w_out[...].astype(F32) * 0.5,
            high,
            mid,
            low,
            jnp.zeros((13, hid), F32),
        ],
        axis=0,
    ).T.astype(BF16)
    lane = lax.broadcasted_iota(jnp.int32, stack.shape, 1)
    is_out = (lane >= chans) & (lane < width)
    nothing = jnp.zeros_like(stack)
    inward = jnp.where(is_out, nothing, stack)
    outward = jnp.where(is_out, stack, nothing)
    for k in range(0, hid, UNIT):
        weights[2 * k : 2 * k + UNIT, :] = inward[k : k + UNIT]
        weights[2 * k + UNIT : 2 * k + 2 * UNIT, :] = outward[k : k + UNIT]

    wave = lax.broadcasted_iota(jnp.int32, (waves, 128), 0)
    lane = lax.broadcasted_iota(jnp.int32, (waves, 128), 1)
    alternate = jnp.where(lane == 0, jnp.where(wave % 2 == 0, scale, -scale), 0.0).astype(BF16)
    for c, move in enumerate(moves):
        move.wait()
        here = slice(c * SLOTS, (c + 1) * SLOTS)
        even = dot(fourier[:, :waves], table[:waves, here])
        odd = dot(fourier[:, waves:], table[waves:, here])
        front = (even + odd).astype(BF16)
        rear = even - odd
        if c == 0:
            middle = dot(fourier[:, :waves], alternate)
            lane = lax.broadcasted_iota(jnp.int32, middle.shape, 1)
            rear = jnp.concatenate(
                [jnp.where(lane == 0, middle, rear[:, :128]), rear[:, 128:]], axis=1
            )
        rear = rear.astype(BF16)
        there = slice(slots + c * SLOTS, slots + (c + 1) * SLOTS)
        for p in range(lat_rows):
            cols[p, :width, here] = front[width * p : width * (p + 1)]
            cols[p, :width, there] = rear[width * p : width * (p + 1)]

    together = acts.shape[0]

    def rows_step(g, carry):
        for r in range(together):
            p = g * together + r
            for n in range(0, points, SPAN):
                here = slice(n, n + SPAN)
                columns_here = cols[p, :, here]
                for k in range(0, hid, UNIT):
                    both = dot(weights[2 * k : 2 * k + 2 * UNIT, :], columns_here).astype(BF16)
                    arg = both[:UNIT]
                    th = jnp.tanh(arg)
                    rise = 1 + th
                    act = arg * rise
                    acts[r, k : k + UNIT, here] = act
                    acts[r, hid + k : hid + k + UNIT, here] = both[UNIT:] * (
                        rise + act * (1 - th)
                    )
            grad = dot(w_in[...], acts[r, hid:, :])
            front, rear = grad[:, :slots], grad[:, slots:]
            edge[p] = rear[:, :128].astype(BF16)
            slot = lax.broadcasted_iota(jnp.int32, rear.shape, 1)
            evens[p] = (front + jnp.where(slot == 0, 0.0, rear)).astype(BF16)
            odds[p] = (front - rear).astype(BF16)
            sums[...] += dot_nt(acts[r], cols[p])
        return carry

    lax.fori_loop(0, lat_rows // together, rows_step, 0)

    def joined(ref):
        return ref[...].reshape(chans * lat_rows, ref.shape[2])

    real = dot_nt(table[:waves, :], joined(evens)) + dot_nt(alternate, joined(edge))
    real = real.astype(BF16)
    imag = dot_nt(table[waves:, :], joined(odds)).astype(BF16)
    span = near * chans
    for q in range(near):
        a, b = q * chans, (q + 1) * chans
        piece = jnp.concatenate(
            [real[:, a:b], imag[:, a:b], real[:, span + a : span + b], imag[:, span + a : span + b]],
            axis=1,
        )
        for d in range(ranks):
            out[d, q * own : (q + 1) * own, :] = piece[d * own : (d + 1) * own]
    if not last:
        after[...] = sums[...]
        return
    base = near * own
    turned = sums[...].T
    main = jnp.concatenate([turned[:chans, hid:], turned[chans:width, :hid]], axis=0)
    total = turned[width : width + 1, hid:]
    lanes = 4 * chans
    cuts = range(0, hid, lanes)
    tail = [total[:, c : c + lanes] for c in cuts]
    share = width // ranks
    for d in range(ranks):
        rows = [main[d * share : (d + 1) * share, c : c + lanes] for c in cuts]
        rows = jnp.concatenate(rows + tail, axis=0).astype(BF16)
        out[d, base : base + rows.shape[0], :] = rows


def columns(arrived, table, w_in, bias, w_out, before, ranks, own, last):
    chans, hid = w_in.shape
    lat_rows = arrived.shape[1] // own
    waves = ranks * own
    slots = table.shape[1]
    points = 2 * slots
    together = 4 if last else 2
    rows_out = lat_rows // 2 * own
    lanes = 4 * chans
    if last:
        rows_out += (hid // lanes) * (2 * chans // ranks) + hid // lanes
    sums = (2 * hid, 2 * chans + 16)
    out_specs = [whole(ranks, rows_out, lanes)]
    out_shape = [jax.ShapeDtypeStruct((ranks, rows_out, lanes), BF16)]
    if not last:
        out_specs.append(whole(*sums))
        out_shape.append(jax.ShapeDtypeStruct(sums, F32))
    sources = [arrived, table, w_in, bias, w_out] + before
    result = pl.pallas_call(
        functools.partial(column_kernel, ranks, own, not before, last),
        grid=(1,),
        in_specs=[HBM] * len(sources),
        out_specs=out_specs,
        out_shape=out_shape,
        scratch_shapes=[
            pltpu.VMEM(arrived.shape, BF16),
            pltpu.VMEM(table.shape, BF16),
            pltpu.VMEM(w_in.shape, BF16),
            pltpu.VMEM(bias.shape, F32),
            pltpu.VMEM(w_out.shape, BF16),
            pltpu.VMEM(sums, F32),
            pltpu.VMEM((2 * chans * lat_rows, 2 * waves), BF16),
            pltpu.VMEM((lat_rows, 2 * chans + 16, points), BF16),
            pltpu.VMEM((2 * hid, 2 * chans + 16), BF16),
            pltpu.VMEM((together, 2 * hid, points), BF16),
            pltpu.VMEM((lat_rows, chans, slots), BF16),
            pltpu.VMEM((lat_rows, chans, slots), BF16),
            pltpu.VMEM((lat_rows, chans, 128), BF16),
            pltpu.SemaphoreType.DMA((5 + slots // SLOTS,)),
        ],
        compiler_params=params(60),
        name="column_physics",
    )(*sources)
    return result[0], list(result[1:])


def backward_kernel(ranks, near, block, ahead, *refs):
    arrived_h, refs = refs[:PARTS], refs[PARTS:]
    cot_h, leg_h, damping, out_h = refs[:4]
    arrived, refs = refs[4 : 4 + PARTS], refs[4 + PARTS :]
    cot, leg, out, rows, factor, in_sems, out_sems, sems = refs
    own, width, _ = cot.shape
    size = near * own
    early = copies_of(zip(arrived_h, arrived), sems)

    def moves(c):
        here = pl.ds(c * block, block)
        return [
            pltpu.make_async_copy(src.at[here], dst.at[here], in_sems.at[c, k])
            for k, (src, dst) in enumerate(((cot_h, cot), (leg_h, leg)))
        ]

    def leave(c):
        here = pl.ds(c * block, block)
        return pltpu.make_async_copy(out.at[here], out_h.at[here], out_sems.at[c])

    for c in range(min(ahead, own // block)):
        for move in moves(c):
            move.start()
    set_factor(factor, damping)
    for part in range(PARTS):
        early[part].wait()
        for s in range(ranks):
            row = (part * ranks + s) * size
            rows[row : row + size, :] = arrived[part][s, :size, :].astype(F32)

    def step(c, carry):
        for move in moves(c):
            move.wait()

        @pl.when(c + ahead < own // block)
        def _():
            for move in moves(c + ahead):
                move.start()

        group = 2 if block % 2 == 0 else 1
        count = PARTS * ranks * near
        for k in range(0, block, group):
            members = [c * block + k + j for j in range(group)]
            mine = [rows[pl.ds(i, count, stride=own), :].astype(BF16) for i in members]
            mine = jnp.concatenate(mine, axis=0).T
            lhs = []
            for j in range(group):
                here = slice(j * count, (j + 1) * count)
                piece = jnp.concatenate([mine[:width, here], mine[width:, here]], axis=1)
                blank = jnp.zeros_like(piece)
                lhs.append(
                    jnp.concatenate([piece if g == j else blank for g in range(group)], axis=1)
                )
            product = dot_nt(
                jnp.concatenate(lhs, axis=0), jnp.concatenate([leg[i] for i in members], axis=1)
            )
            for j, i in enumerate(members):
                here = slice(j * width, (j + 1) * width)
                out[i] = cot[i].astype(F32) * factor[...] + product[here]
        leave(c).start()
        return carry

    lax.fori_loop(0, own // block, step, 0)
    for c in range(own // block):
        leave(c).wait()


def backward(arrived, cot, legendre, damping, ranks):
    own, width, degrees = cot.shape
    lat = legendre.shape[2]
    near = lat // ranks // 2 // PARTS
    block = block_of(own)
    return pl.pallas_call(
        functools.partial(backward_kernel, ranks, near, block, 2),
        grid=(1,),
        in_specs=[HBM] * (PARTS + 2) + [whole(*damping.shape)],
        out_specs=HBM,
        out_shape=jax.ShapeDtypeStruct((own, width, degrees), F32),
        scratch_shapes=[pltpu.VMEM(piece.shape, BF16) for piece in arrived]
        + [
            pltpu.VMEM(cot.shape, BF16),
            pltpu.VMEM(legendre.shape, BF16),
            pltpu.VMEM(cot.shape, F32),
            pltpu.VMEM((PARTS * ranks * near * own, 2 * width), F32),
            pltpu.VMEM((width, degrees), F32),
            pltpu.SemaphoreType.DMA((own // block, 2)),
            pltpu.SemaphoreType.DMA((own // block,)),
            pltpu.SemaphoreType.DMA((PARTS,)),
        ],
        compiler_params=params(60),
        name="legendre_backward",
    )(*arrived, cot, legendre, damping)


def collect_kernel(base, arrived, out):
    total = arrived[0, base:, :].astype(F32)
    for s in range(1, arrived.shape[0]):
        total = total + arrived[s, base:, :].astype(F32)
    for s in range(out.shape[0]):
        out[s] = total.astype(BF16)


def collect(arrived, base, copies):
    shape = (copies, arrived.shape[1] - base, arrived.shape[2])
    return pl.pallas_call(
        functools.partial(collect_kernel, base),
        grid=(1,),
        in_specs=[whole(*arrived.shape)],
        out_specs=whole(*shape),
        out_shape=jax.ShapeDtypeStruct(shape, BF16),
        compiler_params=params(8),
        name="collect_gradients",
    )(arrived)


def finish_kernel(groups, scale, parts, grad_in, grad_bias, grad_out):
    ranks = parts.shape[0] // groups
    chans, hid = grad_in.shape
    lanes = parts.shape[2]
    cuts = hid // lanes
    share = 2 * chans // ranks
    for r in range(ranks):
        total = parts[r].astype(F32)
        for g in range(1, groups):
            total = total + parts[g * ranks + r].astype(F32)
        total = total * scale
        row = r * share
        dest, row = (grad_in, row) if row < chans else (grad_out, row - chans)
        for c in range(cuts):
            dest[row : row + share, c * lanes : (c + 1) * lanes] = total[c * share : (c + 1) * share]
        if r == 0:
            for c in range(cuts):
                grad_bias[:, c * lanes : (c + 1) * lanes] = total[cuts * share + c : cuts * share + c + 1]


def finish(parts, hid, chans, groups, scale):
    return pl.pallas_call(
        functools.partial(finish_kernel, groups, scale),
        grid=(1,),
        in_specs=[whole(*parts.shape)],
        out_specs=(whole(chans, hid), whole(1, hid), whole(chans, hid)),
        out_shape=(
            jax.ShapeDtypeStruct((chans, hid), F32),
            jax.ShapeDtypeStruct((1, hid), F32),
            jax.ShapeDtypeStruct((chans, hid), F32),
        ),
        compiler_params=params(8),
        name="weight_gradients",
    )(parts)


def body(
    spectral_state, cotangent, legendre, quadrature, damping, physics_in, physics_bias, physics_out
):
    spectral = spectral_state[0]
    cot = cotangent[0]
    own, width, degrees = spectral.shape
    chans = width // 2
    hid = physics_in.shape[0]
    ranks = lax.axis_size("lat")
    groups = lax.axis_size("grp")
    lat = legendre.shape[2]
    lat_rows = lat // ranks
    table = jnp.asarray(longitude_table(own * ranks, NLON))
    damping = damping[None, :]
    exchange = functools.partial(
        lax.all_to_all, axis_name="lat", split_axis=0, concat_axis=0, tiled=True
    )

    sent = forward(spectral, cot, legendre, damping, quadrature[None, :], ranks)
    arrived = [exchange(piece) for piece in sent]
    sums = []
    returned = []
    for part in range(PARTS):
        back, sums = columns(
            arrived[part],
            table,
            physics_in.T,
            physics_bias[None, :],
            physics_out,
            sums,
            ranks,
            own,
            part == PARTS - 1,
        )
        if returned:
            back, returned[-1] = lax.optimization_barrier((back, returned[-1]))
        returned.append(exchange(back))

    base = lat_rows // 2 // PARTS * own
    spread = collect(returned[-1], base, groups * ranks)
    parts = lax.all_to_all(spread, ("grp", "lat"), split_axis=0, concat_axis=0, tiled=True)
    grad_state = backward(returned, cot, legendre, damping, ranks)
    scale = 1.0 / math.sqrt(groups * lat * NLON)
    grad_in, grad_bias, grad_out = finish(parts, hid, chans, groups, scale)
    return (grad_state[None], grad_in.T, grad_bias[0], grad_out)


def solution(mesh):
    in_specs = (
        P("grp", "lat", None, None),
        P("grp", "lat", None, None),
        P("lat", None, None),
        P(),
        P(),
        P(),
        P(),
        P(),
    )
    out_specs = (P("grp", "lat", None, None), P(), P(), P())
    return jax.shard_map(body, mesh=mesh, in_specs=in_specs, out_specs=out_specs, check_vma=False)
```

```python
import functools
import math

import jax
import jax.numpy as jnp
import numpy as np
import ml_dtypes
from jax import lax
from jax.experimental import pallas as pl
from jax.experimental.pallas import tpu as pltpu
from jax.sharding import PartitionSpec as P

NLON = 2560
MIB = 1024 * 1024
F32 = jnp.float32
BF16 = jnp.bfloat16
PARTS = 2
SLOTS = 256
SPAN = 512
HBM = pl.BlockSpec(memory_space=pl.ANY)


def longitude_table(waves, points):
    slots = points // 2
    phase = np.arange(waves)[:, None] * np.arange(slots)[None, :] % points
    angle = phase * (2.0 * math.pi / points)
    scale = math.sqrt(2.0 / points)
    both = np.concatenate([np.cos(angle) * scale, -np.sin(angle) * scale])
    return both.astype(np.float32).astype(ml_dtypes.bfloat16)


def dot(a, b):
    return jnp.dot(a, b, preferred_element_type=F32)


def dot_nt(a, b):
    return lax.dot_general(a, b, (((1,), (1,)), ((), ())), preferred_element_type=F32)


def params(mib):
    return pltpu.CompilerParams(vmem_limit_bytes=mib * MIB, dimension_semantics=("arbitrary",))


def whole(*shape):
    return pl.BlockSpec(shape, lambda i: (0,) * len(shape))


def block_of(waves):
    return max(size for size in range(1, 9) if waves % size == 0)


def set_factor(factor, damping):
    width, degrees = factor.shape
    chans = width // 2
    lanes = 128
    spread = jnp.broadcast_to(damping[...], (lanes, chans)).T
    for start in range(0, degrees, lanes):
        degree = (lax.broadcasted_iota(jnp.int32, (chans, lanes), 1) + start).astype(F32)
        ratio = degree * (degree + 1.0) / (degrees * (degrees + 1.0))
        piece = 1.0 / (1.0 + spread * ratio)
        factor[:chans, start : start + lanes] = piece
        factor[chans:, start : start + lanes] = piece


def copies_of(pairs, sems):
    copies = [pltpu.make_async_copy(src, dst, sems.at[k]) for k, (src, dst) in enumerate(pairs)]
    for copy in copies:
        copy.start()
    return copies


def forward_kernel(ranks, block, ahead, *refs):
    spec_h, cot_h, leg_h, damping, quad = refs[:5]
    outs = refs[5 : 5 + PARTS]
    spec, cot, leg, rows, factor, sems = refs[5 + PARTS :]
    own, width, _ = spec.shape
    chans = width // 2
    lat = leg.shape[2]
    near = lat // ranks // 2 // PARTS

    def moves(c):
        here = pl.ds(c * block, block)
        return [
            pltpu.make_async_copy(src.at[here], dst.at[here], sems.at[c, k])
            for k, (src, dst) in enumerate(((spec_h, spec), (cot_h, cot), (leg_h, leg)))
        ]

    for c in range(min(ahead, own // block)):
        for move in moves(c):
            move.start()
    set_factor(factor, damping)

    def step(c, carry):
        for move in moves(c):
            move.wait()

        @pl.when(c + ahead < own // block)
        def _():
            for move in moves(c + ahead):
                move.start()

        weight = quad[...]
        group = 2 if block % 2 == 0 else 1
        for k in range(0, block, group):
            members = [c * block + k + j for j in range(group)]
            stacked = []
            for i in members:
                tend = (cot[i].astype(F32) * factor[...]).astype(BF16)
                state = spec[i]
                stacked += [state[:chans], tend[:chans], state[chans:], tend[chans:]]
            product = dot(
                jnp.concatenate(stacked, axis=0),
                jnp.concatenate([leg[i] for i in members], axis=1),
            )
            for j, i in enumerate(members):
                res = product[2 * width * j : 2 * width * (j + 1), lat * j : lat * (j + 1)]
                res = jnp.concatenate(
                    [
                        res[:chans],
                        res[chans : 2 * chans] * weight,
                        res[2 * chans : 3 * chans],
                        res[3 * chans :] * weight,
                    ],
                    axis=0,
                )
                rows[pl.ds(i, lat, stride=own), :] = res.astype(BF16).T.astype(F32)
        return carry

    lax.fori_loop(0, own // block, step, 0)
    size = near * own
    for part in range(PARTS):
        for d in range(ranks):
            for side in range(2):
                start = ((side * PARTS + part) * ranks + d) * size
                outs[part][d, side * size : (side + 1) * size, :] = rows[
                    start : start + size, :
                ].astype(BF16)


def forward(spectral, cot, legendre, damping, quad, ranks):
    own, width, degrees = spectral.shape
    lat = legendre.shape[2]
    block = block_of(own)
    shape = (ranks, lat // ranks // PARTS * own, 2 * width)
    return pl.pallas_call(
        functools.partial(forward_kernel, ranks, block, own // block),
        grid=(1,),
        in_specs=[HBM] * 3 + [whole(*damping.shape), whole(1, lat)],
        out_specs=[whole(*shape)] * PARTS,
        out_shape=[jax.ShapeDtypeStruct(shape, BF16)] * PARTS,
        scratch_shapes=[
            pltpu.VMEM(spectral.shape, BF16),
            pltpu.VMEM(cot.shape, BF16),
            pltpu.VMEM(legendre.shape, BF16),
            pltpu.VMEM((lat * own, 2 * width), F32),
            pltpu.VMEM((width, degrees), F32),
            pltpu.SemaphoreType.DMA((own // block, 3)),
        ],
        compiler_params=params(60),
        name="legendre_forward",
    )(spectral, cot, legendre, damping, quad)


def column_kernel(ranks, own, first, last, *refs):
    given = 5 if first else 6
    sources, out = refs[:given], refs[given]
    refs = refs[given + 1 :]
    if not last:
        after, refs = refs[0], refs[1:]
    arrived, table, w_in, bias, w_out, sums = refs[:6]
    fourier, cols, weights, acts, evens, odds, edge, sems = refs[6:]
    chans, hid = w_in.shape
    waves = ranks * own
    lat_rows = arrived.shape[1] // own
    near = lat_rows // 2
    slots = table.shape[1]
    points = 2 * slots
    scale = math.sqrt(2.0 / points)
    width = 2 * chans
    unit = 256 if last else 128
    arrived_h, table_h, w_in_h, bias_h, w_out_h = sources[:5]
    pairs = [(arrived_h, arrived), (w_in_h, w_in), (bias_h, bias), (w_out_h, w_out)]
    if not first:
        pairs.append((sources[5], sums))
    small = copies_of(pairs, sems)
    moves = []
    for c in range(slots // SLOTS):
        here = pl.ds(c * SLOTS, SLOTS)
        moves.append(
            pltpu.make_async_copy(table_h.at[:, here], table.at[:, here], sems.at[5 + c])
        )
        moves[c].start()
    for p in range(lat_rows):
        cols[p, width:, :] = jnp.ones((16, points), BF16)
    for copy in small:
        copy.wait()
    if first:
        sums[...] = jnp.zeros_like(sums)
    for p in range(lat_rows):
        piece = jnp.concatenate(
            [arrived[s, p * own : (p + 1) * own, :] for s in range(ranks)], axis=0
        ).T
        row = width * p
        fourier[row : row + width, :waves] = piece[:width]
        fourier[row : row + width, waves:] = piece[width:]
    half_bias = bias[...] * 0.5
    high = half_bias.astype(BF16).astype(F32)
    left = half_bias - high
    mid = left.astype(BF16).astype(F32)
    low = left - mid
    stack = jnp.concatenate(
        [
            w_in[...].astype(F32) * 0.5,
            w_out[...].astype(F32) * 0.5,
            high,
            mid,
            low,
            jnp.zeros((13, hid), F32),
        ],
        axis=0,
    ).T.astype(BF16)
    lane = lax.broadcasted_iota(jnp.int32, stack.shape, 1)
    is_out = (lane >= chans) & (lane < width)
    nothing = jnp.zeros_like(stack)
    inward = jnp.where(is_out, nothing, stack)
    outward = jnp.where(is_out, stack, nothing)
    for k in range(0, hid, unit):
        weights[2 * k : 2 * k + unit, :] = inward[k : k + unit]
        weights[2 * k + unit : 2 * k + 2 * unit, :] = outward[k : k + unit]

    wave = lax.broadcasted_iota(jnp.int32, (waves, 128), 0)
    lane = lax.broadcasted_iota(jnp.int32, (waves, 128), 1)
    alternate = jnp.where(lane == 0, jnp.where(wave % 2 == 0, scale, -scale), 0.0).astype(BF16)
    for c, move in enumerate(moves):
        move.wait()
        here = slice(c * SLOTS, (c + 1) * SLOTS)
        even = dot(fourier[:, :waves], table[:waves, here])
        odd = dot(fourier[:, waves:], table[waves:, here])
        front = (even + odd).astype(BF16)
        rear = even - odd
        if c == 0:
            middle = dot(fourier[:, :waves], alternate)
            lane = lax.broadcasted_iota(jnp.int32, middle.shape, 1)
            rear = jnp.concatenate(
                [jnp.where(lane == 0, middle, rear[:, :128]), rear[:, 128:]], axis=1
            )
        rear = rear.astype(BF16)
        there = slice(slots + c * SLOTS, slots + (c + 1) * SLOTS)
        for p in range(lat_rows):
            cols[p, :width, here] = front[width * p : width * (p + 1)]
            cols[p, :width, there] = rear[width * p : width * (p + 1)]

    together = acts.shape[0]

    def rows_step(g, carry):
        for r in range(together):
            p = g * together + r
            for n in range(0, points, SPAN):
                here = slice(n, n + SPAN)
                columns_here = cols[p, :, here]
                for k in range(0, hid, unit):
                    both = dot(weights[2 * k : 2 * k + 2 * unit, :], columns_here).astype(BF16)
                    arg = both[:unit]
                    th = jnp.tanh(arg)
                    rise = 1 + th
                    act = arg * rise
                    acts[r, k : k + unit, here] = act
                    acts[r, hid + k : hid + k + unit, here] = both[unit:] * (
                        rise + act * (1 - th)
                    )
            grad = dot(w_in[...], acts[r, hid:, :])
            front, rear = grad[:, :slots], grad[:, slots:]
            edge[p] = rear[:, :128].astype(BF16)
            slot = lax.broadcasted_iota(jnp.int32, rear.shape, 1)
            evens[p] = (front + jnp.where(slot == 0, 0.0, rear)).astype(BF16)
            odds[p] = (front - rear).astype(BF16)
            sums[...] += dot_nt(acts[r], cols[p])
        return carry

    lax.fori_loop(0, lat_rows // together, rows_step, 0)

    def joined(ref):
        return ref[...].reshape(chans * lat_rows, ref.shape[2])

    real = dot_nt(table[:waves, :], joined(evens)) + dot_nt(alternate, joined(edge))
    real = real.astype(BF16)
    imag = dot_nt(table[waves:, :], joined(odds)).astype(BF16)
    span = near * chans
    for q in range(near):
        a, b = q * chans, (q + 1) * chans
        piece = jnp.concatenate(
            [real[:, a:b], imag[:, a:b], real[:, span + a : span + b], imag[:, span + a : span + b]],
            axis=1,
        )
        for d in range(ranks):
            out[d, q * own : (q + 1) * own, :] = piece[d * own : (d + 1) * own]
    if not last:
        after[...] = sums[...]
        return
    base = near * own
    turned = sums[...].T
    main = jnp.concatenate([turned[:chans, hid:], turned[chans:width, :hid]], axis=0)
    total = turned[width : width + 1, hid:]
    lanes = 4 * chans
    cuts = range(0, hid, lanes)
    tail = [total[:, c : c + lanes] for c in cuts]
    share = width // ranks
    for d in range(ranks):
        rows = [main[d * share : (d + 1) * share, c : c + lanes] for c in cuts]
        rows = jnp.concatenate(rows + tail, axis=0).astype(BF16)
        out[d, base : base + rows.shape[0], :] = rows


def columns(arrived, table, w_in, bias, w_out, before, ranks, own, last):
    chans, hid = w_in.shape
    lat_rows = arrived.shape[1] // own
    waves = ranks * own
    slots = table.shape[1]
    points = 2 * slots
    together = 4
    rows_out = lat_rows // 2 * own
    lanes = 4 * chans
    if last:
        rows_out += (hid // lanes) * (2 * chans // ranks) + hid // lanes
    sums = (2 * hid, 2 * chans + 16)
    out_specs = [whole(ranks, rows_out, lanes)]
    out_shape = [jax.ShapeDtypeStruct((ranks, rows_out, lanes), BF16)]
    if not last:
        out_specs.append(whole(*sums))
        out_shape.append(jax.ShapeDtypeStruct(sums, F32))
    sources = [arrived, table, w_in, bias, w_out] + before
    result = pl.pallas_call(
        functools.partial(column_kernel, ranks, own, not before, last),
        grid=(1,),
        in_specs=[HBM] * len(sources),
        out_specs=out_specs,
        out_shape=out_shape,
        scratch_shapes=[
            pltpu.VMEM(arrived.shape, BF16),
            pltpu.VMEM(table.shape, BF16),
            pltpu.VMEM(w_in.shape, BF16),
            pltpu.VMEM(bias.shape, F32),
            pltpu.VMEM(w_out.shape, BF16),
            pltpu.VMEM(sums, F32),
            pltpu.VMEM((2 * chans * lat_rows, 2 * waves), BF16),
            pltpu.VMEM((lat_rows, 2 * chans + 16, points), BF16),
            pltpu.VMEM((2 * hid, 2 * chans + 16), BF16),
            pltpu.VMEM((together, 2 * hid, points), BF16),
            pltpu.VMEM((lat_rows, chans, slots), BF16),
            pltpu.VMEM((lat_rows, chans, slots), BF16),
            pltpu.VMEM((lat_rows, chans, 128), BF16),
            pltpu.SemaphoreType.DMA((5 + slots // SLOTS,)),
        ],
        compiler_params=params(60),
        name="column_physics",
    )(*sources)
    return result[0], list(result[1:])


def fetch_kernel(leg_h, cot_h, leg, cot, sems):
    for copy in copies_of([(leg_h, leg), (cot_h, cot)], sems):
        copy.wait()


def fetch(legendre, cot):
    return pl.pallas_call(
        fetch_kernel,
        in_specs=[HBM, HBM],
        out_specs=[HBM, HBM],
        out_shape=[
            jax.ShapeDtypeStruct(legendre.shape, BF16),
            jax.ShapeDtypeStruct(cot.shape, BF16),
        ],
        scratch_shapes=[pltpu.SemaphoreType.DMA((2,))],
        compiler_params=pltpu.CompilerParams(vmem_limit_bytes=40 * MIB),
        name="fetch_operands",
    )(legendre, cot)


def backward_kernel(ranks, near, block, ahead, *refs):
    arrived_h, refs = refs[:PARTS], refs[PARTS:]
    cot_h, leg_h, damping, out_h = refs[:4]
    arrived, refs = refs[4 : 4 + PARTS], refs[4 + PARTS :]
    cot, leg, out, rows, factor, in_sems, out_sems, sems = refs
    own, width, _ = cot.shape
    size = near * own
    early = copies_of(zip(arrived_h, arrived), sems)

    def moves(c):
        here = pl.ds(c * block, block)
        return [
            pltpu.make_async_copy(src.at[here], dst.at[here], in_sems.at[c, k])
            for k, (src, dst) in enumerate(((cot_h, cot), (leg_h, leg)))
        ]

    def leave(c):
        here = pl.ds(c * block, block)
        return pltpu.make_async_copy(out.at[here], out_h.at[here], out_sems.at[c])

    for c in range(min(ahead, own // block)):
        for move in moves(c):
            move.start()
    set_factor(factor, damping)
    for part in range(PARTS):
        early[part].wait()
        for s in range(ranks):
            row = (part * ranks + s) * size
            rows[row : row + size, :] = arrived[part][s, :size, :].astype(F32)

    def step(c, carry):
        for move in moves(c):
            move.wait()

        @pl.when(c + ahead < own // block)
        def _():
            for move in moves(c + ahead):
                move.start()

        group = 2 if block % 2 == 0 else 1
        count = PARTS * ranks * near
        for k in range(0, block, group):
            members = [c * block + k + j for j in range(group)]
            mine = [rows[pl.ds(i, count, stride=own), :].astype(BF16) for i in members]
            mine = jnp.concatenate(mine, axis=0).T
            lhs = []
            for j in range(group):
                here = slice(j * count, (j + 1) * count)
                piece = jnp.concatenate([mine[:width, here], mine[width:, here]], axis=1)
                blank = jnp.zeros_like(piece)
                lhs.append(
                    jnp.concatenate([piece if g == j else blank for g in range(group)], axis=1)
                )
            product = dot_nt(
                jnp.concatenate(lhs, axis=0), jnp.concatenate([leg[i] for i in members], axis=1)
            )
            for j, i in enumerate(members):
                here = slice(j * width, (j + 1) * width)
                out[i] = cot[i].astype(F32) * factor[...] + product[here]
        leave(c).start()
        return carry

    lax.fori_loop(0, own // block, step, 0)
    for c in range(own // block):
        leave(c).wait()


def backward(arrived, cot, legendre, damping, ranks):
    own, width, degrees = cot.shape
    lat = legendre.shape[2]
    near = lat // ranks // 2 // PARTS
    block = block_of(own)
    return pl.pallas_call(
        functools.partial(backward_kernel, ranks, near, block, 2),
        grid=(1,),
        in_specs=[HBM] * (PARTS + 2) + [whole(*damping.shape)],
        out_specs=HBM,
        out_shape=jax.ShapeDtypeStruct((own, width, degrees), F32),
        scratch_shapes=[pltpu.VMEM(piece.shape, BF16) for piece in arrived]
        + [
            pltpu.VMEM(cot.shape, BF16),
            pltpu.VMEM(legendre.shape, BF16),
            pltpu.VMEM(cot.shape, F32),
            pltpu.VMEM((PARTS * ranks * near * own, 2 * width), F32),
            pltpu.VMEM((width, degrees), F32),
            pltpu.SemaphoreType.DMA((own // block, 2)),
            pltpu.SemaphoreType.DMA((own // block,)),
            pltpu.SemaphoreType.DMA((PARTS,)),
        ],
        compiler_params=params(28),
        name="legendre_backward",
    )(*arrived, cot, legendre, damping)


def collect_kernel(base, arrived, out):
    total = arrived[0, base:, :].astype(F32)
    for s in range(1, arrived.shape[0]):
        total = total + arrived[s, base:, :].astype(F32)
    for s in range(out.shape[0]):
        out[s] = total.astype(BF16)


def collect(arrived, base, copies):
    shape = (copies, arrived.shape[1] - base, arrived.shape[2])
    return pl.pallas_call(
        functools.partial(collect_kernel, base),
        grid=(1,),
        in_specs=[whole(*arrived.shape)],
        out_specs=whole(*shape),
        out_shape=jax.ShapeDtypeStruct(shape, BF16),
        compiler_params=params(8),
        name="collect_gradients",
    )(arrived)


def finish_kernel(groups, scale, parts, grad_in, grad_bias, grad_out):
    ranks = parts.shape[0] // groups
    chans, hid = grad_in.shape
    lanes = parts.shape[2]
    cuts = hid // lanes
    share = 2 * chans // ranks
    for r in range(ranks):
        total = parts[r].astype(F32)
        for g in range(1, groups):
            total = total + parts[g * ranks + r].astype(F32)
        total = total * scale
        row = r * share
        dest, row = (grad_in, row) if row < chans else (grad_out, row - chans)
        for c in range(cuts):
            dest[row : row + share, c * lanes : (c + 1) * lanes] = total[c * share : (c + 1) * share]
        if r == 0:
            for c in range(cuts):
                grad_bias[:, c * lanes : (c + 1) * lanes] = total[cuts * share + c : cuts * share + c + 1]


def finish(parts, hid, chans, groups, scale):
    return pl.pallas_call(
        functools.partial(finish_kernel, groups, scale),
        grid=(1,),
        in_specs=[whole(*parts.shape)],
        out_specs=(whole(chans, hid), whole(1, hid), whole(chans, hid)),
        out_shape=(
            jax.ShapeDtypeStruct((chans, hid), F32),
            jax.ShapeDtypeStruct((1, hid), F32),
            jax.ShapeDtypeStruct((chans, hid), F32),
        ),
        compiler_params=params(8),
        name="weight_gradients",
    )(parts)


def body(
    spectral_state, cotangent, legendre, quadrature, damping, physics_in, physics_bias, physics_out
):
    spectral = spectral_state[0]
    cot = cotangent[0]
    own, width, degrees = spectral.shape
    chans = width // 2
    hid = physics_in.shape[0]
    ranks = lax.axis_size("lat")
    groups = lax.axis_size("grp")
    lat = legendre.shape[2]
    lat_rows = lat // ranks
    table = jnp.asarray(longitude_table(own * ranks, NLON))
    damping = damping[None, :]
    exchange = functools.partial(
        lax.all_to_all, axis_name="lat", split_axis=0, concat_axis=0, tiled=True
    )

    sent = forward(spectral, cot, legendre, damping, quadrature[None, :], ranks)
    arrived = [exchange(piece) for piece in sent]
    sums = []
    returned = []
    for part in range(PARTS):
        back, sums = columns(
            arrived[part],
            table,
            physics_in.T,
            physics_bias[None, :],
            physics_out,
            sums,
            ranks,
            own,
            part == PARTS - 1,
        )
        if returned:
            back, returned[-1], late = lax.optimization_barrier(
                (back, returned[-1], (legendre, cot))
            )
        returned.append(exchange(back))
    late = fetch(*late)

    base = lat_rows // 2 // PARTS * own
    spread = collect(returned[-1], base, groups * ranks)
    parts = lax.all_to_all(spread, ("grp", "lat"), split_axis=0, concat_axis=0, tiled=True)
    grad_state = backward(returned, late[1], late[0], damping, ranks)
    scale = 1.0 / math.sqrt(groups * lat * NLON)
    grad_in, grad_bias, grad_out = finish(parts, hid, chans, groups, scale)
    return (grad_state[None], grad_in.T, grad_bias[0], grad_out)


def solution(mesh):
    in_specs = (
        P("grp", "lat", None, None),
        P("grp", "lat", None, None),
        P("lat", None, None),
        P(),
        P(),
        P(),
        P(),
        P(),
    )
    out_specs = (P("grp", "lat", None, None), P(), P(), P())
    return jax.shard_map(body, mesh=mesh, in_specs=in_specs, out_specs=out_specs, check_vma=False)
```

```python
import functools
import math

import jax
import jax.numpy as jnp
import numpy as np
import ml_dtypes
from jax import lax
from jax.experimental import pallas as pl
from jax.experimental.pallas import tpu as pltpu
from jax.sharding import PartitionSpec as P

NLON = 2560
MIB = 1024 * 1024
F32 = jnp.float32
BF16 = jnp.bfloat16
PARTS = 2
SLOTS = 256
SPAN = 512
HBM = pl.BlockSpec(memory_space=pl.ANY)


def longitude_table(waves, points):
    slots = points // 2
    phase = np.arange(waves)[:, None] * np.arange(slots)[None, :] % points
    angle = phase * (2.0 * math.pi / points)
    scale = math.sqrt(2.0 / points)
    both = np.concatenate([np.cos(angle) * scale, -np.sin(angle) * scale])
    return both.astype(np.float32).astype(ml_dtypes.bfloat16)


def dot(a, b):
    return jnp.dot(a, b, preferred_element_type=F32)


def dot_nt(a, b):
    return lax.dot_general(a, b, (((1,), (1,)), ((), ())), preferred_element_type=F32)


def params(mib):
    return pltpu.CompilerParams(vmem_limit_bytes=mib * MIB, dimension_semantics=("arbitrary",))


def whole(*shape):
    return pl.BlockSpec(shape, lambda i: (0,) * len(shape))


def block_of(waves):
    return max(size for size in range(1, 9) if waves % size == 0)


def set_factor(factor, damping):
    width, degrees = factor.shape
    chans = width // 2
    lanes = 128
    spread = jnp.broadcast_to(damping[...], (lanes, chans)).T
    for start in range(0, degrees, lanes):
        degree = (lax.broadcasted_iota(jnp.int32, (chans, lanes), 1) + start).astype(F32)
        ratio = degree * (degree + 1.0) / (degrees * (degrees + 1.0))
        piece = 1.0 / (1.0 + spread * ratio)
        factor[:chans, start : start + lanes] = piece
        factor[chans:, start : start + lanes] = piece


def copies_of(pairs, sems):
    copies = [pltpu.make_async_copy(src, dst, sems.at[k]) for k, (src, dst) in enumerate(pairs)]
    for copy in copies:
        copy.start()
    return copies


def forward_kernel(ranks, block, ahead, *refs):
    spec_h, cot_h, leg_h, damping, quad = refs[:5]
    outs = refs[5 : 5 + PARTS]
    spec, cot, leg, rows, factor, sems = refs[5 + PARTS :]
    own, width, _ = spec.shape
    chans = width // 2
    lat = leg.shape[2]
    near = lat // ranks // 2 // PARTS

    def moves(c):
        here = pl.ds(c * block, block)
        return [
            pltpu.make_async_copy(src.at[here], dst.at[here], sems.at[c, k])
            for k, (src, dst) in enumerate(((spec_h, spec), (cot_h, cot), (leg_h, leg)))
        ]

    for c in range(min(ahead, own // block)):
        for move in moves(c):
            move.start()
    set_factor(factor, damping)

    def step(c, carry):
        for move in moves(c):
            move.wait()

        @pl.when(c + ahead < own // block)
        def _():
            for move in moves(c + ahead):
                move.start()

        weight = quad[...]
        group = 2 if block % 2 == 0 else 1
        for k in range(0, block, group):
            members = [c * block + k + j for j in range(group)]
            stacked = []
            for i in members:
                tend = (cot[i].astype(F32) * factor[...]).astype(BF16)
                state = spec[i]
                stacked += [state[:chans], tend[:chans], state[chans:], tend[chans:]]
            product = dot(
                jnp.concatenate(stacked, axis=0),
                jnp.concatenate([leg[i] for i in members], axis=1),
            )
            for j, i in enumerate(members):
                res = product[2 * width * j : 2 * width * (j + 1), lat * j : lat * (j + 1)]
                res = jnp.concatenate(
                    [
                        res[:chans],
                        res[chans : 2 * chans] * weight,
                        res[2 * chans : 3 * chans],
                        res[3 * chans :] * weight,
                    ],
                    axis=0,
                )
                rows[pl.ds(i, lat, stride=own), :] = res.astype(BF16).T.astype(F32)
        return carry

    lax.fori_loop(0, own // block, step, 0)
    size = near * own
    for part in range(PARTS):
        for d in range(ranks):
            for side in range(2):
                start = ((side * PARTS + part) * ranks + d) * size
                outs[part][d, side * size : (side + 1) * size, :] = rows[
                    start : start + size, :
                ].astype(BF16)


def forward(spectral, cot, legendre, damping, quad, ranks):
    own, width, degrees = spectral.shape
    lat = legendre.shape[2]
    block = block_of(own)
    shape = (ranks, lat // ranks // PARTS * own, 2 * width)
    return pl.pallas_call(
        functools.partial(forward_kernel, ranks, block, own // block),
        grid=(1,),
        in_specs=[HBM] * 3 + [whole(*damping.shape), whole(1, lat)],
        out_specs=[whole(*shape)] * PARTS,
        out_shape=[jax.ShapeDtypeStruct(shape, BF16)] * PARTS,
        scratch_shapes=[
            pltpu.VMEM(spectral.shape, BF16),
            pltpu.VMEM(cot.shape, BF16),
            pltpu.VMEM(legendre.shape, BF16),
            pltpu.VMEM((lat * own, 2 * width), F32),
            pltpu.VMEM((width, degrees), F32),
            pltpu.SemaphoreType.DMA((own // block, 3)),
        ],
        compiler_params=params(60),
        name="legendre_forward",
    )(spectral, cot, legendre, damping, quad)


def column_kernel(ranks, own, first, last, *refs):
    given = 5 if first else 6
    sources, out = refs[:given], refs[given]
    refs = refs[given + 1 :]
    after, refs = refs[0], refs[1:]
    arrived, table, w_in, bias, w_out, sums = refs[:6]
    fourier, cols, weights, acts, evens, odds, edge, sems = refs[6:]
    chans, hid = w_in.shape
    waves = ranks * own
    lat_rows = arrived.shape[1] // own
    near = lat_rows // 2
    slots = table.shape[1]
    points = 2 * slots
    scale = math.sqrt(2.0 / points)
    width = 2 * chans
    unit = 128
    arrived_h, table_h, w_in_h, bias_h, w_out_h = sources[:5]
    pairs = [(arrived_h, arrived), (w_in_h, w_in), (bias_h, bias), (w_out_h, w_out)]
    if not first:
        pairs.append((sources[5], sums))
    small = copies_of(pairs, sems)
    moves = []
    for c in range(slots // SLOTS):
        here = pl.ds(c * SLOTS, SLOTS)
        moves.append(
            pltpu.make_async_copy(table_h.at[:, here], table.at[:, here], sems.at[5 + c])
        )
        moves[c].start()
    for p in range(lat_rows):
        cols[p, width:, :] = jnp.ones((16, points), BF16)
    for copy in small:
        copy.wait()
    if first:
        sums[...] = jnp.zeros_like(sums)
    for p in range(lat_rows):
        piece = jnp.concatenate(
            [arrived[s, p * own : (p + 1) * own, :] for s in range(ranks)], axis=0
        ).T
        row = width * p
        fourier[row : row + width, :waves] = piece[:width]
        fourier[row : row + width, waves:] = piece[width:]
    half_bias = bias[...] * 0.5
    high = half_bias.astype(BF16).astype(F32)
    left = half_bias - high
    mid = left.astype(BF16).astype(F32)
    low = left - mid
    stack = jnp.concatenate(
        [
            w_in[...].astype(F32) * 0.5,
            w_out[...].astype(F32) * 0.5,
            high,
            mid,
            low,
            jnp.zeros((13, hid), F32),
        ],
        axis=0,
    ).T.astype(BF16)
    lane = lax.broadcasted_iota(jnp.int32, stack.shape, 1)
    is_out = (lane >= chans) & (lane < width)
    nothing = jnp.zeros_like(stack)
    inward = jnp.where(is_out, nothing, stack)
    outward = jnp.where(is_out, stack, nothing)
    for k in range(0, hid, unit):
        weights[2 * k : 2 * k + unit, :] = inward[k : k + unit]
        weights[2 * k + unit : 2 * k + 2 * unit, :] = outward[k : k + unit]

    wave = lax.broadcasted_iota(jnp.int32, (waves, 128), 0)
    lane = lax.broadcasted_iota(jnp.int32, (waves, 128), 1)
    alternate = jnp.where(lane == 0, jnp.where(wave % 2 == 0, scale, -scale), 0.0).astype(BF16)
    for c, move in enumerate(moves):
        move.wait()
        here = slice(c * SLOTS, (c + 1) * SLOTS)
        even = dot(fourier[:, :waves], table[:waves, here])
        odd = dot(fourier[:, waves:], table[waves:, here])
        front = (even + odd).astype(BF16)
        rear = even - odd
        if c == 0:
            middle = dot(fourier[:, :waves], alternate)
            lane = lax.broadcasted_iota(jnp.int32, middle.shape, 1)
            rear = jnp.concatenate(
                [jnp.where(lane == 0, middle, rear[:, :128]), rear[:, 128:]], axis=1
            )
        rear = rear.astype(BF16)
        there = slice(slots + c * SLOTS, slots + (c + 1) * SLOTS)
        for p in range(lat_rows):
            cols[p, :width, here] = front[width * p : width * (p + 1)]
            cols[p, :width, there] = rear[width * p : width * (p + 1)]

    together = acts.shape[0]

    def rows_step(g, carry):
        for r in range(together):
            p = g * together + r
            for n in range(0, points, SPAN):
                here = slice(n, n + SPAN)
                columns_here = cols[p, :, here]
                for k in range(0, hid, unit):
                    both = dot(weights[2 * k : 2 * k + 2 * unit, :], columns_here).astype(BF16)
                    arg = both[:unit]
                    th = jnp.tanh(arg)
                    rise = 1 + th
                    act = arg * rise
                    acts[r, k : k + unit, here] = act
                    acts[r, hid + k : hid + k + unit, here] = both[unit:] * (
                        rise + act * (1 - th)
                    )
            grad = dot(w_in[...], acts[r, hid:, :])
            front, rear = grad[:, :slots], grad[:, slots:]
            edge[p] = rear[:, :128].astype(BF16)
            slot = lax.broadcasted_iota(jnp.int32, rear.shape, 1)
            evens[p] = (front + jnp.where(slot == 0, 0.0, rear)).astype(BF16)
            odds[p] = (front - rear).astype(BF16)
            sums[...] += dot_nt(acts[r], cols[p])
        return carry

    lax.fori_loop(0, lat_rows // together, rows_step, 0)

    def joined(ref):
        return ref[...].reshape(chans * lat_rows, ref.shape[2])

    real = dot_nt(table[:waves, :], joined(evens)) + dot_nt(alternate, joined(edge))
    real = real.astype(BF16)
    imag = dot_nt(table[waves:, :], joined(odds)).astype(BF16)
    span = near * chans
    for q in range(near):
        a, b = q * chans, (q + 1) * chans
        piece = jnp.concatenate(
            [real[:, a:b], imag[:, a:b], real[:, span + a : span + b], imag[:, span + a : span + b]],
            axis=1,
        )
        for d in range(ranks):
            out[d, q * own : (q + 1) * own, :] = piece[d * own : (d + 1) * own]
    if not last:
        after[...] = sums[...]
        return
    base = near * own
    turned = sums[...].T
    main = jnp.concatenate([turned[:chans, hid:], turned[chans:width, :hid]], axis=0)
    lanes = 4 * chans
    cuts = range(0, hid, lanes)
    after[...] = turned[width : width + 1, hid:]
    share = width // ranks
    for d in range(ranks):
        rows = [main[d * share : (d + 1) * share, c : c + lanes] for c in cuts]
        rows = jnp.concatenate(rows, axis=0).astype(BF16)
        out[d, base : base + rows.shape[0], :] = rows


def columns(arrived, table, w_in, bias, w_out, before, ranks, own, last):
    chans, hid = w_in.shape
    lat_rows = arrived.shape[1] // own
    waves = ranks * own
    slots = table.shape[1]
    points = 2 * slots
    together = 4
    rows_out = lat_rows // 2 * own
    lanes = 4 * chans
    if last:
        rows_out += (hid // lanes) * (2 * chans // ranks)
    sums = (2 * hid, 2 * chans + 16)
    after = (1, hid) if last else sums
    out_specs = [whole(ranks, rows_out, lanes), whole(*after)]
    out_shape = [
        jax.ShapeDtypeStruct((ranks, rows_out, lanes), BF16),
        jax.ShapeDtypeStruct(after, F32),
    ]
    sources = [arrived, table, w_in, bias, w_out] + before
    result = pl.pallas_call(
        functools.partial(column_kernel, ranks, own, not before, last),
        grid=(1,),
        in_specs=[HBM] * len(sources),
        out_specs=out_specs,
        out_shape=out_shape,
        scratch_shapes=[
            pltpu.VMEM(arrived.shape, BF16),
            pltpu.VMEM(table.shape, BF16),
            pltpu.VMEM(w_in.shape, BF16),
            pltpu.VMEM(bias.shape, F32),
            pltpu.VMEM(w_out.shape, BF16),
            pltpu.VMEM(sums, F32),
            pltpu.VMEM((2 * chans * lat_rows, 2 * waves), BF16),
            pltpu.VMEM((lat_rows, 2 * chans + 16, points), BF16),
            pltpu.VMEM((2 * hid, 2 * chans + 16), BF16),
            pltpu.VMEM((together, 2 * hid, points), BF16),
            pltpu.VMEM((lat_rows, chans, slots), BF16),
            pltpu.VMEM((lat_rows, chans, slots), BF16),
            pltpu.VMEM((lat_rows, chans, 128), BF16),
            pltpu.SemaphoreType.DMA((5 + slots // SLOTS,)),
        ],
        compiler_params=params(60),
        name="column_physics",
    )(*sources)
    return result[0], list(result[1:])


def fetch_kernel(leg_h, cot_h, leg, cot, sems):
    for copy in copies_of([(leg_h, leg), (cot_h, cot)], sems):
        copy.wait()


def fetch(legendre, cot):
    return pl.pallas_call(
        fetch_kernel,
        in_specs=[HBM, HBM],
        out_specs=[HBM, HBM],
        out_shape=[
            jax.ShapeDtypeStruct(legendre.shape, BF16),
            jax.ShapeDtypeStruct(cot.shape, BF16),
        ],
        scratch_shapes=[pltpu.SemaphoreType.DMA((2,))],
        compiler_params=pltpu.CompilerParams(vmem_limit_bytes=40 * MIB),
        name="fetch_operands",
    )(legendre, cot)


def backward_kernel(ranks, near, block, *refs):
    arrived_h, refs = refs[:PARTS], refs[PARTS:]
    cot, leg, damping, out_h = refs[:4]
    arrived, refs = refs[4 : 4 + PARTS], refs[4 + PARTS :]
    out, rows, factor, out_sems, sems = refs
    own, width, _ = cot.shape
    size = near * own
    early = copies_of(zip(arrived_h, arrived), sems)

    def leave(c):
        here = pl.ds(c * block, block)
        return pltpu.make_async_copy(out.at[here], out_h.at[here], out_sems.at[c])

    set_factor(factor, damping)
    for part in range(PARTS):
        early[part].wait()
        for s in range(ranks):
            row = (part * ranks + s) * size
            rows[row : row + size, :] = arrived[part][s, :size, :].astype(F32)

    def step(c, carry):
        group = 2 if block % 2 == 0 else 1
        count = PARTS * ranks * near
        for k in range(0, block, group):
            members = [c * block + k + j for j in range(group)]
            mine = [rows[pl.ds(i, count, stride=own), :].astype(BF16) for i in members]
            mine = jnp.concatenate(mine, axis=0).T
            lhs = []
            for j in range(group):
                here = slice(j * count, (j + 1) * count)
                piece = jnp.concatenate([mine[:width, here], mine[width:, here]], axis=1)
                blank = jnp.zeros_like(piece)
                lhs.append(
                    jnp.concatenate([piece if g == j else blank for g in range(group)], axis=1)
                )
            product = dot_nt(
                jnp.concatenate(lhs, axis=0), jnp.concatenate([leg[i] for i in members], axis=1)
            )
            for j, i in enumerate(members):
                here = slice(j * width, (j + 1) * width)
                out[i] = cot[i].astype(F32) * factor[...] + product[here]
        leave(c).start()
        return carry

    lax.fori_loop(0, own // block, step, 0)
    for c in range(own // block):
        leave(c).wait()


def backward(arrived, cot, legendre, damping, ranks):
    own, width, degrees = cot.shape
    lat = legendre.shape[2]
    near = lat // ranks // 2 // PARTS
    block = block_of(own)
    return pl.pallas_call(
        functools.partial(backward_kernel, ranks, near, block),
        in_specs=[HBM] * PARTS + [pl.BlockSpec(memory_space=pltpu.VMEM)] * 3,
        out_specs=HBM,
        out_shape=jax.ShapeDtypeStruct((own, width, degrees), F32),
        scratch_shapes=[pltpu.VMEM(piece.shape, BF16) for piece in arrived]
        + [
            pltpu.VMEM(cot.shape, F32),
            pltpu.VMEM((PARTS * ranks * near * own, 2 * width), F32),
            pltpu.VMEM((width, degrees), F32),
            pltpu.SemaphoreType.DMA((own // block,)),
            pltpu.SemaphoreType.DMA((PARTS,)),
        ],
        compiler_params=pltpu.CompilerParams(vmem_limit_bytes=28 * MIB),
        name="legendre_backward",
    )(*arrived, cot, legendre, damping)


def collect_kernel(base, arrived, bias, out):
    lanes = arrived.shape[2]
    total = arrived[0, base:, :].astype(F32)
    for s in range(1, arrived.shape[0]):
        total = total + arrived[s, base:, :].astype(F32)
    cuts = range(0, bias.shape[1], lanes)
    total = jnp.concatenate([total] + [bias[:, c : c + lanes] for c in cuts], axis=0).astype(BF16)
    for s in range(out.shape[0]):
        out[s] = total


def collect(arrived, bias, base, copies):
    lanes = arrived.shape[2]
    shape = (copies, arrived.shape[1] - base + bias.shape[1] // lanes, lanes)
    return pl.pallas_call(
        functools.partial(collect_kernel, base),
        grid=(1,),
        in_specs=[whole(*arrived.shape), whole(*bias.shape)],
        out_specs=whole(*shape),
        out_shape=jax.ShapeDtypeStruct(shape, BF16),
        compiler_params=params(8),
        name="collect_gradients",
    )(arrived, bias)


def finish_kernel(groups, scale, parts, grad_in, grad_bias, grad_out):
    ranks = parts.shape[0] // groups
    chans, hid = grad_in.shape
    lanes = parts.shape[2]
    cuts = hid // lanes
    share = 2 * chans // ranks
    for r in range(ranks):
        total = parts[r].astype(F32)
        for g in range(1, groups):
            total = total + parts[g * ranks + r].astype(F32)
        total = total * scale
        row = r * share
        dest, row = (grad_in, row) if row < chans else (grad_out, row - chans)
        for c in range(cuts):
            dest[row : row + share, c * lanes : (c + 1) * lanes] = total[c * share : (c + 1) * share]
    tail = parts[0, cuts * share :].astype(F32)
    for s in range(1, parts.shape[0]):
        tail = tail + parts[s, cuts * share :].astype(F32)
    for c in range(cuts):
        grad_bias[:, c * lanes : (c + 1) * lanes] = tail[c : c + 1] * scale


def finish(parts, hid, chans, groups, scale):
    return pl.pallas_call(
        functools.partial(finish_kernel, groups, scale),
        grid=(1,),
        in_specs=[whole(*parts.shape)],
        out_specs=(whole(chans, hid), whole(1, hid), whole(chans, hid)),
        out_shape=(
            jax.ShapeDtypeStruct((chans, hid), F32),
            jax.ShapeDtypeStruct((1, hid), F32),
            jax.ShapeDtypeStruct((chans, hid), F32),
        ),
        compiler_params=params(8),
        name="weight_gradients",
    )(parts)


def body(
    spectral_state, cotangent, legendre, quadrature, damping, physics_in, physics_bias, physics_out
):
    spectral = spectral_state[0]
    cot = cotangent[0]
    own, width, degrees = spectral.shape
    chans = width // 2
    hid = physics_in.shape[0]
    ranks = lax.axis_size("lat")
    groups = lax.axis_size("grp")
    lat = legendre.shape[2]
    lat_rows = lat // ranks
    table = jnp.asarray(longitude_table(own * ranks, NLON))
    damping = damping[None, :]
    exchange = functools.partial(
        lax.all_to_all, axis_name="lat", split_axis=0, concat_axis=0, tiled=True
    )

    sent = forward(spectral, cot, legendre, damping, quadrature[None, :], ranks)
    arrived = [exchange(piece) for piece in sent]
    sums = []
    returned = []
    for part in range(PARTS):
        back, sums = columns(
            arrived[part],
            table,
            physics_in.T,
            physics_bias[None, :],
            physics_out,
            sums,
            ranks,
            own,
            part == PARTS - 1,
        )
        if returned:
            back, returned[-1], late = lax.optimization_barrier(
                (back, returned[-1], (legendre, cot))
            )
        returned.append(exchange(back))
    returned[-1], late = lax.optimization_barrier((returned[-1], fetch(*late)))

    base = lat_rows // 2 // PARTS * own
    spread = collect(returned[-1], sums[0], base, groups * ranks)
    parts = lax.all_to_all(spread, ("grp", "lat"), split_axis=0, concat_axis=0, tiled=True)
    grad_state = backward(returned, late[1], late[0], damping, ranks)
    scale = 1.0 / math.sqrt(groups * lat * NLON)
    grad_in, grad_bias, grad_out = finish(parts, hid, chans, groups, scale)
    return (grad_state[None], grad_in.T, grad_bias[0], grad_out)


def solution(mesh):
    in_specs = (
        P("grp", "lat", None, None),
        P("grp", "lat", None, None),
        P("lat", None, None),
        P(),
        P(),
        P(),
        P(),
        P(),
    )
    out_specs = (P("grp", "lat", None, None), P(), P(), P())
    return jax.shard_map(body, mesh=mesh, in_specs=in_specs, out_specs=out_specs, check_vma=False)
```

```python
import functools
import math

import jax
import jax.numpy as jnp
import numpy as np
import ml_dtypes
from jax import lax
from jax.experimental import pallas as pl
from jax.experimental.pallas import tpu as pltpu
from jax.sharding import PartitionSpec as P

NLON = 2560
MIB = 1024 * 1024
F32 = jnp.float32
BF16 = jnp.bfloat16
PARTS = 2
SLOTS = 256
SPAN = 512
UNIT = 128
HBM = pl.BlockSpec(memory_space=pl.ANY)


def longitude_table(waves, points):
    slots = points // 2
    phase = np.arange(waves)[:, None] * np.arange(slots)[None, :] % points
    angle = phase * (2.0 * math.pi / points)
    scale = math.sqrt(2.0 / points)
    both = np.concatenate([np.cos(angle) * scale, -np.sin(angle) * scale])
    return both.astype(np.float32).astype(ml_dtypes.bfloat16)


def dot(a, b):
    return jnp.dot(a, b, preferred_element_type=F32)


def dot_nt(a, b):
    return lax.dot_general(a, b, (((1,), (1,)), ((), ())), preferred_element_type=F32)


def params(mib):
    return pltpu.CompilerParams(vmem_limit_bytes=mib * MIB, dimension_semantics=("arbitrary",))


def whole(*shape):
    return pl.BlockSpec(shape, lambda i: (0,) * len(shape))


def block_of(waves):
    return max(size for size in range(1, 9) if waves % size == 0)


def set_factor(factor, damping):
    width, degrees = factor.shape
    chans = width // 2
    lanes = 128
    spread = jnp.broadcast_to(damping[...], (lanes, chans)).T
    for start in range(0, degrees, lanes):
        degree = (lax.broadcasted_iota(jnp.int32, (chans, lanes), 1) + start).astype(F32)
        ratio = degree * (degree + 1.0) / (degrees * (degrees + 1.0))
        piece = 1.0 / (1.0 + spread * ratio)
        factor[:chans, start : start + lanes] = piece
        factor[chans:, start : start + lanes] = piece


def copies_of(pairs, sems):
    copies = [pltpu.make_async_copy(src, dst, sems.at[k]) for k, (src, dst) in enumerate(pairs)]
    for copy in copies:
        copy.start()
    return copies


def forward_kernel(ranks, block, part, *refs):
    spec_h, cot_h, leg_h, damping, quad, out = refs[:6]
    spec, cot, leg, rows, factor, sems = refs[6:]
    own, width, _ = spec.shape
    chans = width // 2
    lat = leg.shape[2]
    near = lat // ranks // 2 // PARTS
    span = ranks * near

    def moves(c):
        here = pl.ds(c * block, block)
        return [
            pltpu.make_async_copy(src.at[here], dst.at[here], sems.at[c, k])
            for k, (src, dst) in enumerate(((spec_h, spec), (cot_h, cot), (leg_h, leg)))
        ]

    for c in range(own // block):
        for move in moves(c):
            move.start()
    set_factor(factor, damping)

    def step(c, carry):
        for move in moves(c):
            move.wait()
        weight = quad[...]
        for k in range(block):
            i = c * block + k
            tend = (cot[i].astype(F32) * factor[...]).astype(BF16)
            state = spec[i]
            stacked = jnp.concatenate(
                [state[:chans], tend[:chans], state[chans:], tend[chans:]], axis=0
            )
            res = dot(stacked, leg[i])
            res = jnp.concatenate(
                [
                    res[:chans],
                    res[chans : 2 * chans] * weight,
                    res[2 * chans : 3 * chans],
                    res[3 * chans :] * weight,
                ],
                axis=0,
            )
            res = res.astype(BF16).T.astype(F32)
            for side in range(2):
                start = (side * PARTS + part) * span
                rows[pl.ds(side * span * own + i, span, stride=own), :] = res[start : start + span]
        return carry

    lax.fori_loop(0, own // block, step, 0)
    size = near * own
    for d in range(ranks):
        for side in range(2):
            start = (side * ranks + d) * size
            out[d, side * size : (side + 1) * size, :] = rows[start : start + size, :].astype(BF16)


def forward(spectral, cot, legendre, damping, quad, ranks, part):
    own, width, degrees = spectral.shape
    lat = legendre.shape[2]
    block = block_of(own)
    shape = (ranks, lat // ranks // PARTS * own, 2 * width)
    return pl.pallas_call(
        functools.partial(forward_kernel, ranks, block, part),
        grid=(1,),
        in_specs=[HBM] * 3 + [whole(*damping.shape), whole(1, lat)],
        out_specs=whole(*shape),
        out_shape=jax.ShapeDtypeStruct(shape, BF16),
        scratch_shapes=[
            pltpu.VMEM(spectral.shape, BF16),
            pltpu.VMEM(cot.shape, BF16),
            pltpu.VMEM(legendre.shape, BF16),
            pltpu.VMEM((lat // PARTS * own, 2 * width), F32),
            pltpu.VMEM((width, degrees), F32),
            pltpu.SemaphoreType.DMA((own // block, 3)),
        ],
        compiler_params=params(60),
        name="legendre_forward",
    )(spectral, cot, legendre, damping, quad)


def weights_kernel(w_in, bias, w_out, weights):
    chans, hid = w_in.shape
    width = 2 * chans
    half_bias = bias[...] * 0.5
    high = half_bias.astype(BF16).astype(F32)
    left = half_bias - high
    mid = left.astype(BF16).astype(F32)
    low = left - mid
    stack = jnp.concatenate(
        [
            w_in[...].astype(F32) * 0.5,
            w_out[...].astype(F32) * 0.5,
            high,
            mid,
            low,
            jnp.zeros((13, hid), F32),
        ],
        axis=0,
    ).T.astype(BF16)
    lane = lax.broadcasted_iota(jnp.int32, stack.shape, 1)
    is_out = (lane >= chans) & (lane < width)
    nothing = jnp.zeros_like(stack)
    inward = jnp.where(is_out, nothing, stack)
    outward = jnp.where(is_out, stack, nothing)
    for k in range(0, hid, UNIT):
        weights[2 * k : 2 * k + UNIT, :] = inward[k : k + UNIT]
        weights[2 * k + UNIT : 2 * k + 2 * UNIT, :] = outward[k : k + UNIT]


def column_weights(w_in, bias, w_out):
    chans, hid = w_in.shape
    shape = (2 * hid, 2 * chans + 16)
    return pl.pallas_call(
        weights_kernel,
        grid=(1,),
        in_specs=[whole(*w_in.shape), whole(*bias.shape), whole(*w_out.shape)],
        out_specs=whole(*shape),
        out_shape=jax.ShapeDtypeStruct(shape, BF16),
        compiler_params=params(8),
        name="column_weights",
    )(w_in, bias, w_out)


def column_kernel(ranks, own, first, last, *refs):
    given = 4 if first else 5
    sources, out = refs[:given], refs[given]
    refs = refs[given + 1 :]
    after, refs = refs[0], refs[1:]
    arrived, table, w_in, weights, sums = refs[:5]
    fourier, cols, acts, evens, odds, edge, sems = refs[5:]
    chans, hid = w_in.shape
    waves = ranks * own
    lat_rows = arrived.shape[1] // own
    near = lat_rows // 2
    slots = table.shape[1]
    points = 2 * slots
    scale = math.sqrt(2.0 / points)
    width = 2 * chans
    arrived_h, table_h, w_in_h, weights_h = sources[:4]
    pairs = [(arrived_h, arrived), (w_in_h, w_in), (weights_h, weights)]
    if not first:
        pairs.append((sources[4], sums))
    small = copies_of(pairs, sems)
    moves = []
    for c in range(slots // SLOTS):
        here = pl.ds(c * SLOTS, SLOTS)
        moves.append(
            pltpu.make_async_copy(table_h.at[:, here], table.at[:, here], sems.at[4 + c])
        )
        moves[c].start()
    for p in range(lat_rows):
        cols[p, width:, :] = jnp.ones((16, points), BF16)
    for copy in small:
        copy.wait()
    if first:
        sums[...] = jnp.zeros_like(sums)
    for p in range(lat_rows):
        piece = jnp.concatenate(
            [arrived[s, p * own : (p + 1) * own, :] for s in range(ranks)], axis=0
        ).T
        row = width * p
        fourier[row : row + width, :waves] = piece[:width]
        fourier[row : row + width, waves:] = piece[width:]
    wave = lax.broadcasted_iota(jnp.int32, (waves, 128), 0)
    lane = lax.broadcasted_iota(jnp.int32, (waves, 128), 1)
    alternate = jnp.where(lane == 0, jnp.where(wave % 2 == 0, scale, -scale), 0.0).astype(BF16)
    for c, move in enumerate(moves):
        move.wait()
        here = slice(c * SLOTS, (c + 1) * SLOTS)
        even = dot(fourier[:, :waves], table[:waves, here])
        odd = dot(fourier[:, waves:], table[waves:, here])
        front = (even + odd).astype(BF16)
        rear = even - odd
        if c == 0:
            middle = dot(fourier[:, :waves], alternate)
            lane = lax.broadcasted_iota(jnp.int32, middle.shape, 1)
            rear = jnp.concatenate(
                [jnp.where(lane == 0, middle, rear[:, :128]), rear[:, 128:]], axis=1
            )
        rear = rear.astype(BF16)
        there = slice(slots + c * SLOTS, slots + (c + 1) * SLOTS)
        for p in range(lat_rows):
            cols[p, :width, here] = front[width * p : width * (p + 1)]
            cols[p, :width, there] = rear[width * p : width * (p + 1)]

    together = acts.shape[0]

    def rows_step(g, carry):
        for r in range(together):
            p = g * together + r
            for n in range(0, points, SPAN):
                here = slice(n, n + SPAN)
                columns_here = cols[p, :, here]
                for k in range(0, hid, UNIT):
                    both = dot(weights[2 * k : 2 * k + 2 * UNIT, :], columns_here).astype(BF16)
                    arg = both[:UNIT]
                    th = jnp.tanh(arg)
                    rise = 1 + th
                    act = arg * rise
                    acts[r, k : k + UNIT, here] = act
                    acts[r, hid + k : hid + k + UNIT, here] = both[UNIT:] * (
                        rise + act * (1 - th)
                    )
            grad = dot(w_in[...], acts[r, hid:, :])
            front, rear = grad[:, :slots], grad[:, slots:]
            edge[p] = rear[:, :128].astype(BF16)
            slot = lax.broadcasted_iota(jnp.int32, rear.shape, 1)
            evens[p] = (front + jnp.where(slot == 0, 0.0, rear)).astype(BF16)
            odds[p] = (front - rear).astype(BF16)
            sums[...] += dot_nt(acts[r], cols[p])
        return carry

    lax.fori_loop(0, lat_rows // together, rows_step, 0)

    def joined(ref):
        return ref[...].reshape(chans * lat_rows, ref.shape[2])

    real = dot_nt(table[:waves, :], joined(evens)) + dot_nt(alternate, joined(edge))
    real = real.astype(BF16)
    imag = dot_nt(table[waves:, :], joined(odds)).astype(BF16)
    span = near * chans
    for q in range(near):
        a, b = q * chans, (q + 1) * chans
        piece = jnp.concatenate(
            [real[:, a:b], imag[:, a:b], real[:, span + a : span + b], imag[:, span + a : span + b]],
            axis=1,
        )
        for d in range(ranks):
            out[d, q * own : (q + 1) * own, :] = piece[d * own : (d + 1) * own]
    if not last:
        after[...] = sums[...]
        return
    base = near * own
    turned = sums[...].T
    main = jnp.concatenate([turned[:chans, hid:], turned[chans:width, :hid]], axis=0)
    lanes = 4 * chans
    cuts = range(0, hid, lanes)
    after[...] = turned[width : width + 1, hid:]
    share = width // ranks
    for d in range(ranks):
        rows = [main[d * share : (d + 1) * share, c : c + lanes] for c in cuts]
        rows = jnp.concatenate(rows, axis=0).astype(BF16)
        out[d, base : base + rows.shape[0], :] = rows


def columns(arrived, table, w_in, weights, before, ranks, own, last):
    chans, hid = w_in.shape
    lat_rows = arrived.shape[1] // own
    waves = ranks * own
    slots = table.shape[1]
    points = 2 * slots
    together = 4
    rows_out = lat_rows // 2 * own
    lanes = 4 * chans
    if last:
        rows_out += (hid // lanes) * (2 * chans // ranks)
    sums = (2 * hid, 2 * chans + 16)
    after = (1, hid) if last else sums
    out_specs = [whole(ranks, rows_out, lanes), whole(*after)]
    out_shape = [
        jax.ShapeDtypeStruct((ranks, rows_out, lanes), BF16),
        jax.ShapeDtypeStruct(after, F32),
    ]
    sources = [arrived, table, w_in, weights] + before
    result = pl.pallas_call(
        functools.partial(column_kernel, ranks, own, not before, last),
        grid=(1,),
        in_specs=[HBM] * len(sources),
        out_specs=out_specs,
        out_shape=out_shape,
        scratch_shapes=[
            pltpu.VMEM(arrived.shape, BF16),
            pltpu.VMEM(table.shape, BF16),
            pltpu.VMEM(w_in.shape, BF16),
            pltpu.VMEM(weights.shape, BF16),
            pltpu.VMEM(sums, F32),
            pltpu.VMEM((2 * chans * lat_rows, 2 * waves), BF16),
            pltpu.VMEM((lat_rows, 2 * chans + 16, points), BF16),
            pltpu.VMEM((together, 2 * hid, points), BF16),
            pltpu.VMEM((lat_rows, chans, slots), BF16),
            pltpu.VMEM((lat_rows, chans, slots), BF16),
            pltpu.VMEM((lat_rows, chans, 128), BF16),
            pltpu.SemaphoreType.DMA((4 + slots // SLOTS,)),
        ],
        compiler_params=params(60),
        name="column_physics",
    )(*sources)
    return result[0], list(result[1:])


def backward_kernel(ranks, near, block, ahead, *refs):
    arrived_h, refs = refs[:PARTS], refs[PARTS:]
    cot_h, leg_h, damping, out_h = refs[:4]
    arrived, refs = refs[4 : 4 + PARTS], refs[4 + PARTS :]
    cot, leg, out, rows, factor, in_sems, out_sems, sems = refs
    own, width, _ = cot.shape
    size = near * own
    early = copies_of(zip(arrived_h, arrived), sems)

    def moves(c):
        here = pl.ds(c * block, block)
        return [
            pltpu.make_async_copy(src.at[here], dst.at[here], in_sems.at[c, k])
            for k, (src, dst) in enumerate(((cot_h, cot), (leg_h, leg)))
        ]

    def leave(c):
        here = pl.ds(c * block, block)
        return pltpu.make_async_copy(out.at[here], out_h.at[here], out_sems.at[c])

    for c in range(min(ahead, own // block)):
        for move in moves(c):
            move.start()
    set_factor(factor, damping)
    for part in range(PARTS):
        early[part].wait()
        for s in range(ranks):
            row = (part * ranks + s) * size
            rows[row : row + size, :] = arrived[part][s, :size, :].astype(F32)

    def step(c, carry):
        for move in moves(c):
            move.wait()

        @pl.when(c + ahead < own // block)
        def _():
            for move in moves(c + ahead):
                move.start()

        group = 2 if block % 2 == 0 else 1
        count = PARTS * ranks * near
        for k in range(0, block, group):
            members = [c * block + k + j for j in range(group)]
            mine = [rows[pl.ds(i, count, stride=own), :].astype(BF16) for i in members]
            mine = jnp.concatenate(mine, axis=0).T
            lhs = []
            for j in range(group):
                here = slice(j * count, (j + 1) * count)
                piece = jnp.concatenate([mine[:width, here], mine[width:, here]], axis=1)
                blank = jnp.zeros_like(piece)
                lhs.append(
                    jnp.concatenate([piece if g == j else blank for g in range(group)], axis=1)
                )
            product = dot_nt(
                jnp.concatenate(lhs, axis=0), jnp.concatenate([leg[i] for i in members], axis=1)
            )
            for j, i in enumerate(members):
                here = slice(j * width, (j + 1) * width)
                out[i] = cot[i].astype(F32) * factor[...] + product[here]
        leave(c).start()
        return carry

    lax.fori_loop(0, own // block, step, 0)
    for c in range(own // block):
        leave(c).wait()


def backward(arrived, cot, legendre, damping, ranks):
    own, width, degrees = cot.shape
    lat = legendre.shape[2]
    near = lat // ranks // 2 // PARTS
    block = block_of(own)
    return pl.pallas_call(
        functools.partial(backward_kernel, ranks, near, block, 2),
        grid=(1,),
        in_specs=[HBM] * (PARTS + 2) + [whole(*damping.shape)],
        out_specs=HBM,
        out_shape=jax.ShapeDtypeStruct((own, width, degrees), F32),
        scratch_shapes=[pltpu.VMEM(piece.shape, BF16) for piece in arrived]
        + [
            pltpu.VMEM(cot.shape, BF16),
            pltpu.VMEM(legendre.shape, BF16),
            pltpu.VMEM(cot.shape, F32),
            pltpu.VMEM((PARTS * ranks * near * own, 2 * width), F32),
            pltpu.VMEM((width, degrees), F32),
            pltpu.SemaphoreType.DMA((own // block, 2)),
            pltpu.SemaphoreType.DMA((own // block,)),
            pltpu.SemaphoreType.DMA((PARTS,)),
        ],
        compiler_params=params(60),
        name="legendre_backward",
    )(*arrived, cot, legendre, damping)


def collect_kernel(base, arrived, bias, out):
    lanes = arrived.shape[2]
    total = arrived[0, base:, :].astype(F32)
    for s in range(1, arrived.shape[0]):
        total = total + arrived[s, base:, :].astype(F32)
    cuts = range(0, bias.shape[1], lanes)
    total = jnp.concatenate([total] + [bias[:, c : c + lanes] for c in cuts], axis=0).astype(BF16)
    for s in range(out.shape[0]):
        out[s] = total


def collect(arrived, bias, base, copies):
    lanes = arrived.shape[2]
    shape = (copies, arrived.shape[1] - base + bias.shape[1] // lanes, lanes)
    return pl.pallas_call(
        functools.partial(collect_kernel, base),
        grid=(1,),
        in_specs=[whole(*arrived.shape), whole(*bias.shape)],
        out_specs=whole(*shape),
        out_shape=jax.ShapeDtypeStruct(shape, BF16),
        compiler_params=params(8),
        name="collect_gradients",
    )(arrived, bias)


def finish_kernel(groups, scale, parts, grad_in, grad_bias, grad_out):
    ranks = parts.shape[0] // groups
    chans, hid = grad_in.shape
    lanes = parts.shape[2]
    cuts = hid // lanes
    share = 2 * chans // ranks
    for r in range(ranks):
        total = parts[r].astype(F32)
        for g in range(1, groups):
            total = total + parts[g * ranks + r].astype(F32)
        total = total * scale
        row = r * share
        dest, row = (grad_in, row) if row < chans else (grad_out, row - chans)
        for c in range(cuts):
            dest[row : row + share, c * lanes : (c + 1) * lanes] = total[c * share : (c + 1) * share]
    tail = parts[0, cuts * share :].astype(F32)
    for s in range(1, parts.shape[0]):
        tail = tail + parts[s, cuts * share :].astype(F32)
    for c in range(cuts):
        grad_bias[:, c * lanes : (c + 1) * lanes] = tail[c : c + 1] * scale


def finish(parts, hid, chans, groups, scale):
    return pl.pallas_call(
        functools.partial(finish_kernel, groups, scale),
        grid=(1,),
        in_specs=[whole(*parts.shape)],
        out_specs=(whole(chans, hid), whole(1, hid), whole(chans, hid)),
        out_shape=(
            jax.ShapeDtypeStruct((chans, hid), F32),
            jax.ShapeDtypeStruct((1, hid), F32),
            jax.ShapeDtypeStruct((chans, hid), F32),
        ),
        compiler_params=params(8),
        name="weight_gradients",
    )(parts)


def body(
    spectral_state, cotangent, legendre, quadrature, damping, physics_in, physics_bias, physics_out
):
    spectral = spectral_state[0]
    cot = cotangent[0]
    own, width, degrees = spectral.shape
    chans = width // 2
    hid = physics_in.shape[0]
    ranks = lax.axis_size("lat")
    groups = lax.axis_size("grp")
    lat = legendre.shape[2]
    lat_rows = lat // ranks
    table = jnp.asarray(longitude_table(own * ranks, NLON))
    damping = damping[None, :]
    exchange = functools.partial(
        lax.all_to_all, axis_name="lat", split_axis=0, concat_axis=0, tiled=True
    )

    weights = column_weights(physics_in.T, physics_bias[None, :], physics_out)
    arrived = []
    for part in range(PARTS):
        sent = forward(spectral, cot, legendre, damping, quadrature[None, :], ranks, part)
        if arrived:
            sent, weights, arrived[-1] = lax.optimization_barrier((sent, weights, arrived[-1]))
        arrived.append(exchange(sent))
    sums = []
    returned = []
    for part in range(PARTS):
        back, sums = columns(
            arrived[part],
            table,
            physics_in.T,
            weights,
            sums,
            ranks,
            own,
            part == PARTS - 1,
        )
        if returned:
            back, returned[-1] = lax.optimization_barrier((back, returned[-1]))
        returned.append(exchange(back))

    base = lat_rows // 2 // PARTS * own
    spread = collect(returned[-1], sums[0], base, groups * ranks)
    parts = lax.all_to_all(spread, ("grp", "lat"), split_axis=0, concat_axis=0, tiled=True)
    grad_state = backward(returned, cot, legendre, damping, ranks)
    scale = 1.0 / math.sqrt(groups * lat * NLON)
    grad_in, grad_bias, grad_out = finish(parts, hid, chans, groups, scale)
    return (grad_state[None], grad_in.T, grad_bias[0], grad_out)


def solution(mesh):
    in_specs = (
        P("grp", "lat", None, None),
        P("grp", "lat", None, None),
        P("lat", None, None),
        P(),
        P(),
        P(),
        P(),
        P(),
    )
    out_specs = (P("grp", "lat", None, None), P(), P(), P())
    return jax.shard_map(body, mesh=mesh, in_specs=in_specs, out_specs=out_specs, check_vma=False)
```

```python
import functools
import math

import jax
import jax.numpy as jnp
import numpy as np
import ml_dtypes
from jax import lax
from jax.experimental import pallas as pl
from jax.experimental.pallas import tpu as pltpu
from jax.sharding import PartitionSpec as P

NLON = 2560
MIB = 1024 * 1024
F32 = jnp.float32
BF16 = jnp.bfloat16
PARTS = 2
SLOTS = 256
UNIT = 128
HBM = pl.BlockSpec(memory_space=pl.ANY)


def longitude_table(waves, points):
    slots = points // 2
    phase = np.arange(waves)[:, None] * np.arange(slots)[None, :] % points
    angle = phase * (2.0 * math.pi / points)
    scale = math.sqrt(2.0 / points)
    both = np.concatenate([np.cos(angle) * scale, -np.sin(angle) * scale])
    return both.astype(np.float32).astype(ml_dtypes.bfloat16)


def dot(a, b):
    return jnp.dot(a, b, preferred_element_type=F32)


def dot_nt(a, b):
    return lax.dot_general(a, b, (((1,), (1,)), ((), ())), preferred_element_type=F32)


def params(mib):
    return pltpu.CompilerParams(vmem_limit_bytes=mib * MIB, dimension_semantics=("arbitrary",))


def whole(*shape):
    return pl.BlockSpec(shape, lambda i: (0,) * len(shape))


def block_of(waves):
    return max(size for size in range(1, 5) if waves % size == 0)


def set_factor(factor, damping):
    width, degrees = factor.shape
    chans = width // 2
    lanes = 128
    spread = jnp.broadcast_to(damping[...], (lanes, chans)).T
    for start in range(0, degrees, lanes):
        degree = (lax.broadcasted_iota(jnp.int32, (chans, lanes), 1) + start).astype(F32)
        ratio = degree * (degree + 1.0) / (degrees * (degrees + 1.0))
        piece = 1.0 / (1.0 + spread * ratio)
        factor[:chans, start : start + lanes] = piece
        factor[chans:, start : start + lanes] = piece


def copies_of(pairs, sems):
    copies = [pltpu.make_async_copy(src, dst, sems.at[k]) for k, (src, dst) in enumerate(pairs)]
    for copy in copies:
        copy.start()
    return copies


def forward_kernel(ranks, block, part, *refs):
    spec_h, cot_h, leg_h, damping, quad, out = refs[:6]
    spec, cot, leg, rows, factor, sems = refs[6:]
    own, width, _ = spec.shape
    chans = width // 2
    lat = leg.shape[2]
    near = lat // ranks // 2 // PARTS
    span = ranks * near

    def moves(c):
        here = pl.ds(c * block, block)
        return [
            pltpu.make_async_copy(src.at[here], dst.at[here], sems.at[c, k])
            for k, (src, dst) in enumerate(((spec_h, spec), (cot_h, cot), (leg_h, leg)))
        ]

    for c in range(own // block):
        for move in moves(c):
            move.start()
    set_factor(factor, damping)

    def step(c, carry):
        for move in moves(c):
            move.wait()
        weight = quad[...]
        for k in range(block):
            i = c * block + k
            tend = (cot[i].astype(F32) * factor[...]).astype(BF16)
            state = spec[i]
            stacked = jnp.concatenate(
                [state[:chans], tend[:chans], state[chans:], tend[chans:]], axis=0
            )
            res = dot(stacked, leg[i])
            res = jnp.concatenate(
                [
                    res[:chans],
                    res[chans : 2 * chans] * weight,
                    res[2 * chans : 3 * chans],
                    res[3 * chans :] * weight,
                ],
                axis=0,
            )
            res = res.astype(BF16).T.astype(F32)
            for side in range(2):
                start = (side * PARTS + part) * span
                rows[pl.ds(side * span * own + i, span, stride=own), :] = res[start : start + span]
        return carry

    lax.fori_loop(0, own // block, step, 0)
    size = near * own
    for d in range(ranks):
        for side in range(2):
            start = (side * ranks + d) * size
            out[d, side * size : (side + 1) * size, :] = rows[start : start + size, :].astype(BF16)


def forward(spectral, cot, legendre, damping, quad, ranks, part):
    own, width, degrees = spectral.shape
    lat = legendre.shape[2]
    block = block_of(own)
    shape = (ranks, lat // ranks // PARTS * own, 2 * width)
    return pl.pallas_call(
        functools.partial(forward_kernel, ranks, block, part),
        grid=(1,),
        in_specs=[HBM] * 3 + [whole(*damping.shape), whole(1, lat)],
        out_specs=whole(*shape),
        out_shape=jax.ShapeDtypeStruct(shape, BF16),
        scratch_shapes=[
            pltpu.VMEM(spectral.shape, BF16),
            pltpu.VMEM(cot.shape, BF16),
            pltpu.VMEM(legendre.shape, BF16),
            pltpu.VMEM((lat // PARTS * own, 2 * width), F32),
            pltpu.VMEM((width, degrees), F32),
            pltpu.SemaphoreType.DMA((own // block, 3)),
        ],
        compiler_params=params(60),
        name="legendre_forward",
    )(spectral, cot, legendre, damping, quad)


def weights_kernel(w_in, bias, w_out, weights):
    chans, hid = w_in.shape
    width = 2 * chans
    half_bias = bias[...] * 0.5
    high = half_bias.astype(BF16).astype(F32)
    left = half_bias - high
    mid = left.astype(BF16).astype(F32)
    low = left - mid
    stack = jnp.concatenate(
        [
            w_in[...].astype(F32) * 0.5,
            w_out[...].astype(F32) * 0.5,
            high,
            mid,
            low,
            jnp.zeros((13, hid), F32),
        ],
        axis=0,
    ).T.astype(BF16)
    lane = lax.broadcasted_iota(jnp.int32, stack.shape, 1)
    is_out = (lane >= chans) & (lane < width)
    nothing = jnp.zeros_like(stack)
    inward = jnp.where(is_out, nothing, stack)
    outward = jnp.where(is_out, stack, nothing)
    for k in range(0, hid, UNIT):
        weights[2 * k : 2 * k + UNIT, :] = inward[k : k + UNIT]
        weights[2 * k + UNIT : 2 * k + 2 * UNIT, :] = outward[k : k + UNIT]


def column_weights(w_in, bias, w_out):
    chans, hid = w_in.shape
    shape = (2 * hid, 2 * chans + 16)
    return pl.pallas_call(
        weights_kernel,
        grid=(1,),
        in_specs=[whole(*w_in.shape), whole(*bias.shape), whole(*w_out.shape)],
        out_specs=whole(*shape),
        out_shape=jax.ShapeDtypeStruct(shape, BF16),
        compiler_params=params(60),
        name="column_weights",
    )(w_in, bias, w_out)


def column_kernel(ranks, own, first, last, *refs):
    given = 4 if first else 5
    sources, out = refs[:given], refs[given]
    refs = refs[given + 1 :]
    after, refs = refs[0], refs[1:]
    arrived, table, w_in, weights, sums = refs[:5]
    fourier, cols, acts, evens, odds, edge, sems = refs[5:]
    chans, hid = w_in.shape
    waves = ranks * own
    lat_rows = arrived.shape[1] // own
    near = lat_rows // 2
    slots = table.shape[1]
    points = 2 * slots
    scale = math.sqrt(2.0 / points)
    width = 2 * chans
    arrived_h, table_h, w_in_h, weights_h = sources[:4]
    pairs = [(arrived_h, arrived), (w_in_h, w_in), (weights_h, weights)]
    if not first:
        pairs.append((sources[4], sums))
    small = copies_of(pairs, sems)
    moves = []
    for c in range(slots // SLOTS):
        here = pl.ds(c * SLOTS, SLOTS)
        moves.append(
            pltpu.make_async_copy(table_h.at[:, here], table.at[:, here], sems.at[4 + c])
        )
        moves[c].start()
    for p in range(lat_rows):
        cols[p, width:, :] = jnp.ones((16, points), BF16)
    for copy in small:
        copy.wait()
    if first:
        sums[...] = jnp.zeros_like(sums)
    for p in range(lat_rows):
        piece = jnp.concatenate(
            [arrived[s, p * own : (p + 1) * own, :] for s in range(ranks)], axis=0
        ).T
        row = width * p
        fourier[row : row + width, :waves] = piece[:width]
        fourier[row : row + width, waves:] = piece[width:]
    wave = lax.broadcasted_iota(jnp.int32, (waves, 128), 0)
    lane = lax.broadcasted_iota(jnp.int32, (waves, 128), 1)
    alternate = jnp.where(lane == 0, jnp.where(wave % 2 == 0, scale, -scale), 0.0).astype(BF16)
    for c, move in enumerate(moves):
        move.wait()
        here = slice(c * SLOTS, (c + 1) * SLOTS)
        even = dot(fourier[:, :waves], table[:waves, here])
        odd = dot(fourier[:, waves:], table[waves:, here])
        front = (even + odd).astype(BF16)
        rear = even - odd
        if c == 0:
            middle = dot(fourier[:, :waves], alternate)
            lane = lax.broadcasted_iota(jnp.int32, middle.shape, 1)
            rear = jnp.concatenate(
                [jnp.where(lane == 0, middle, rear[:, :128]), rear[:, 128:]], axis=1
            )
        rear = rear.astype(BF16)
        there = slice(slots + c * SLOTS, slots + (c + 1) * SLOTS)
        for p in range(lat_rows):
            cols[p, :width, here] = front[width * p : width * (p + 1)]
            cols[p, :width, there] = rear[width * p : width * (p + 1)]

    together = acts.shape[0]
    span = 256 if last else 1280

    def rows_step(g, carry):
        for r in range(together):
            p = g * together + r
            for n in range(0, points, span):
                here = slice(n, n + span)
                columns_here = cols[p, :, here]
                for k in range(0, hid, UNIT):
                    both = dot(weights[2 * k : 2 * k + 2 * UNIT, :], columns_here).astype(BF16)
                    arg = both[:UNIT]
                    th = jnp.tanh(arg)
                    rise = 1 + th
                    act = arg * rise
                    acts[r, k : k + UNIT, here] = act
                    acts[r, hid + k : hid + k + UNIT, here] = both[UNIT:] * (
                        rise + act * (1 - th)
                    )
            grad = dot(w_in[...], acts[r, hid:, :])
            front, rear = grad[:, :slots], grad[:, slots:]
            edge[p] = rear[:, :128].astype(BF16)
            slot = lax.broadcasted_iota(jnp.int32, rear.shape, 1)
            evens[p] = (front + jnp.where(slot == 0, 0.0, rear)).astype(BF16)
            odds[p] = (front - rear).astype(BF16)
            sums[...] += dot_nt(acts[r], cols[p])
        return carry

    lax.fori_loop(0, lat_rows // together, rows_step, 0)

    def joined(ref):
        return ref[...].reshape(chans * lat_rows, ref.shape[2])

    real = dot_nt(table[:waves, :], joined(evens)) + dot_nt(alternate, joined(edge))
    real = real.astype(BF16)
    imag = dot_nt(table[waves:, :], joined(odds)).astype(BF16)
    span = near * chans
    for q in range(near):
        a, b = q * chans, (q + 1) * chans
        piece = jnp.concatenate(
            [real[:, a:b], imag[:, a:b], real[:, span + a : span + b], imag[:, span + a : span + b]],
            axis=1,
        )
        for d in range(ranks):
            out[d, q * own : (q + 1) * own, :] = piece[d * own : (d + 1) * own]
    if not last:
        after[...] = sums[...]
        return
    base = near * own
    turned = sums[...].T
    main = jnp.concatenate([turned[:chans, hid:], turned[chans:width, :hid]], axis=0)
    lanes = 4 * chans
    cuts = range(0, hid, lanes)
    after[...] = turned[width : width + 1, hid:]
    share = width // ranks
    for d in range(ranks):
        rows = [main[d * share : (d + 1) * share, c : c + lanes] for c in cuts]
        rows = jnp.concatenate(rows, axis=0).astype(BF16)
        out[d, base : base + rows.shape[0], :] = rows


def columns(arrived, table, w_in, weights, before, ranks, own, last):
    chans, hid = w_in.shape
    lat_rows = arrived.shape[1] // own
    waves = ranks * own
    slots = table.shape[1]
    points = 2 * slots
    together = 4
    rows_out = lat_rows // 2 * own
    lanes = 4 * chans
    if last:
        rows_out += (hid // lanes) * (2 * chans // ranks)
    sums = (2 * hid, 2 * chans + 16)
    after = (1, hid) if last else sums
    out_specs = [whole(ranks, rows_out, lanes), whole(*after)]
    out_shape = [
        jax.ShapeDtypeStruct((ranks, rows_out, lanes), BF16),
        jax.ShapeDtypeStruct(after, F32),
    ]
    sources = [arrived, table, w_in, weights] + before
    result = pl.pallas_call(
        functools.partial(column_kernel, ranks, own, not before, last),
        grid=(1,),
        in_specs=[HBM] * len(sources),
        out_specs=out_specs,
        out_shape=out_shape,
        scratch_shapes=[
            pltpu.VMEM(arrived.shape, BF16),
            pltpu.VMEM(table.shape, BF16),
            pltpu.VMEM(w_in.shape, BF16),
            pltpu.VMEM(weights.shape, BF16),
            pltpu.VMEM(sums, F32),
            pltpu.VMEM((2 * chans * lat_rows, 2 * waves), BF16),
            pltpu.VMEM((lat_rows, 2 * chans + 16, points), BF16),
            pltpu.VMEM((together, 2 * hid, points), BF16),
            pltpu.VMEM((lat_rows, chans, slots), BF16),
            pltpu.VMEM((lat_rows, chans, slots), BF16),
            pltpu.VMEM((lat_rows, chans, 128), BF16),
            pltpu.SemaphoreType.DMA((4 + slots // SLOTS,)),
        ],
        compiler_params=params(60),
        name="column_physics",
    )(*sources)
    return result[0], list(result[1:])


def backward_kernel(ranks, near, block, ahead, *refs):
    arrived_h, refs = refs[:PARTS], refs[PARTS:]
    cot_h, leg_h, damping, out_h = refs[:4]
    arrived, refs = refs[4 : 4 + PARTS], refs[4 + PARTS :]
    cot, leg, out, rows, factor, in_sems, out_sems, sems = refs
    own, width, _ = cot.shape
    size = near * own
    early = copies_of(zip(arrived_h, arrived), sems)

    def moves(c):
        here = pl.ds(c * block, block)
        return [
            pltpu.make_async_copy(src.at[here], dst.at[here], in_sems.at[c, k])
            for k, (src, dst) in enumerate(((cot_h, cot), (leg_h, leg)))
        ]

    def leave(c):
        here = pl.ds(c * block, block)
        return pltpu.make_async_copy(out.at[here], out_h.at[here], out_sems.at[c])

    for c in range(min(ahead, own // block)):
        for move in moves(c):
            move.start()
    set_factor(factor, damping)
    for part in range(PARTS):
        early[part].wait()
        for s in range(ranks):
            row = (part * ranks + s) * size
            rows[row : row + size, :] = arrived[part][s, :size, :].astype(F32)

    def step(c, carry):
        for move in moves(c):
            move.wait()

        @pl.when(c + ahead < own // block)
        def _():
            for move in moves(c + ahead):
                move.start()

        group = 2 if block % 2 == 0 else 1
        count = PARTS * ranks * near
        for k in range(0, block, group):
            members = [c * block + k + j for j in range(group)]
            mine = [rows[pl.ds(i, count, stride=own), :].astype(BF16) for i in members]
            mine = jnp.concatenate(mine, axis=0).T
            lhs = []
            for j in range(group):
                here = slice(j * count, (j + 1) * count)
                piece = jnp.concatenate([mine[:width, here], mine[width:, here]], axis=1)
                blank = jnp.zeros_like(piece)
                lhs.append(
                    jnp.concatenate([piece if g == j else blank for g in range(group)], axis=1)
                )
            product = dot_nt(
                jnp.concatenate(lhs, axis=0), jnp.concatenate([leg[i] for i in members], axis=1)
            )
            for j, i in enumerate(members):
                here = slice(j * width, (j + 1) * width)
                out[i] = cot[i].astype(F32) * factor[...] + product[here]
        leave(c).start()
        return carry

    lax.fori_loop(0, own // block, step, 0)
    for c in range(own // block):
        leave(c).wait()


def backward(arrived, cot, legendre, damping, ranks):
    own, width, degrees = cot.shape
    lat = legendre.shape[2]
    near = lat // ranks // 2 // PARTS
    block = block_of(own)
    return pl.pallas_call(
        functools.partial(backward_kernel, ranks, near, block, 3),
        grid=(1,),
        in_specs=[HBM] * (PARTS + 2) + [whole(*damping.shape)],
        out_specs=HBM,
        out_shape=jax.ShapeDtypeStruct((own, width, degrees), F32),
        scratch_shapes=[pltpu.VMEM(piece.shape, BF16) for piece in arrived]
        + [
            pltpu.VMEM(cot.shape, BF16),
            pltpu.VMEM(legendre.shape, BF16),
            pltpu.VMEM(cot.shape, F32),
            pltpu.VMEM((PARTS * ranks * near * own, 2 * width), F32),
            pltpu.VMEM((width, degrees), F32),
            pltpu.SemaphoreType.DMA((own // block, 2)),
            pltpu.SemaphoreType.DMA((own // block,)),
            pltpu.SemaphoreType.DMA((PARTS,)),
        ],
        compiler_params=params(60),
        name="legendre_backward",
    )(*arrived, cot, legendre, damping)


def collect_kernel(base, arrived, bias, out):
    lanes = arrived.shape[2]
    total = arrived[0, base:, :].astype(F32)
    for s in range(1, arrived.shape[0]):
        total = total + arrived[s, base:, :].astype(F32)
    cuts = range(0, bias.shape[1], lanes)
    total = jnp.concatenate([total] + [bias[:, c : c + lanes] for c in cuts], axis=0).astype(BF16)
    for s in range(out.shape[0]):
        out[s] = total


def collect(arrived, bias, base, copies):
    lanes = arrived.shape[2]
    shape = (copies, arrived.shape[1] - base + bias.shape[1] // lanes, lanes)
    return pl.pallas_call(
        functools.partial(collect_kernel, base),
        grid=(1,),
        in_specs=[whole(*arrived.shape), whole(*bias.shape)],
        out_specs=whole(*shape),
        out_shape=jax.ShapeDtypeStruct(shape, BF16),
        compiler_params=params(8),
        name="collect_gradients",
    )(arrived, bias)


def finish_kernel(groups, scale, parts, grad_in, grad_bias, grad_out):
    ranks = parts.shape[0] // groups
    chans, hid = grad_in.shape
    lanes = parts.shape[2]
    cuts = hid // lanes
    share = 2 * chans // ranks
    for r in range(ranks):
        total = parts[r].astype(F32)
        for g in range(1, groups):
            total = total + parts[g * ranks + r].astype(F32)
        total = total * scale
        row = r * share
        dest, row = (grad_in, row) if row < chans else (grad_out, row - chans)
        for c in range(cuts):
            dest[row : row + share, c * lanes : (c + 1) * lanes] = total[c * share : (c + 1) * share]
    tail = parts[0, cuts * share :].astype(F32)
    for s in range(1, parts.shape[0]):
        tail = tail + parts[s, cuts * share :].astype(F32)
    for c in range(cuts):
        grad_bias[:, c * lanes : (c + 1) * lanes] = tail[c : c + 1] * scale


def finish(parts, hid, chans, groups, scale):
    return pl.pallas_call(
        functools.partial(finish_kernel, groups, scale),
        grid=(1,),
        in_specs=[whole(*parts.shape)],
        out_specs=(whole(chans, hid), whole(1, hid), whole(chans, hid)),
        out_shape=(
            jax.ShapeDtypeStruct((chans, hid), F32),
            jax.ShapeDtypeStruct((1, hid), F32),
            jax.ShapeDtypeStruct((chans, hid), F32),
        ),
        compiler_params=params(8),
        name="weight_gradients",
    )(parts)


def body(
    spectral_state, cotangent, legendre, quadrature, damping, physics_in, physics_bias, physics_out
):
    spectral = spectral_state[0]
    cot = cotangent[0]
    own, width, degrees = spectral.shape
    chans = width // 2
    hid = physics_in.shape[0]
    ranks = lax.axis_size("lat")
    groups = lax.axis_size("grp")
    lat = legendre.shape[2]
    lat_rows = lat // ranks
    table = jnp.asarray(longitude_table(own * ranks, NLON))
    damping = damping[None, :]
    exchange = functools.partial(
        lax.all_to_all, axis_name="lat", split_axis=0, concat_axis=0, tiled=True
    )

    weights = column_weights(physics_in.T, physics_bias[None, :], physics_out)
    arrived = []
    for part in range(PARTS):
        sent = forward(spectral, cot, legendre, damping, quadrature[None, :], ranks, part)
        if arrived:
            sent, weights, arrived[-1] = lax.optimization_barrier((sent, weights, arrived[-1]))
        arrived.append(exchange(sent))
    sums = []
    returned = []
    for part in range(PARTS):
        back, sums = columns(
            arrived[part],
            table,
            physics_in.T,
            weights,
            sums,
            ranks,
            own,
            part == PARTS - 1,
        )
        if returned:
            back, returned[-1] = lax.optimization_barrier((back, returned[-1]))
        returned.append(exchange(back))

    base = lat_rows // 2 // PARTS * own
    spread = collect(returned[-1], sums[0], base, groups * ranks)
    parts = lax.all_to_all(spread, ("grp", "lat"), split_axis=0, concat_axis=0, tiled=True)
    grad_state = backward(returned, cot, legendre, damping, ranks)
    scale = 1.0 / math.sqrt(groups * lat * NLON)
    grad_in, grad_bias, grad_out = finish(parts, hid, chans, groups, scale)
    return (grad_state[None], grad_in.T, grad_bias[0], grad_out)


def solution(mesh):
    in_specs = (
        P("grp", "lat", None, None),
        P("grp", "lat", None, None),
        P("lat", None, None),
        P(),
        P(),
        P(),
        P(),
        P(),
    )
    out_specs = (P("grp", "lat", None, None), P(), P(), P())
    return jax.shard_map(body, mesh=mesh, in_specs=in_specs, out_specs=out_specs, check_vma=False)
```

```python
import functools
import math

import jax
import jax.numpy as jnp
import numpy as np
import ml_dtypes
from jax import lax
from jax.experimental import pallas as pl
from jax.experimental.pallas import tpu as pltpu
from jax.sharding import PartitionSpec as P

NLON = 2560
MIB = 1024 * 1024
F32 = jnp.float32
BF16 = jnp.bfloat16
PARTS = 2
SLOTS = 256
UNIT = 128
HBM = pl.BlockSpec(memory_space=pl.ANY)


def longitude_table(waves, points):
    slots = points // 2
    phase = np.arange(waves)[:, None] * np.arange(slots)[None, :] % points
    angle = phase * (2.0 * math.pi / points)
    scale = math.sqrt(2.0 / points)
    both = np.concatenate([np.cos(angle) * scale, -np.sin(angle) * scale])
    return both.astype(np.float32).astype(ml_dtypes.bfloat16)


def dot(a, b):
    return jnp.dot(a, b, preferred_element_type=F32)


def dot_nt(a, b):
    return lax.dot_general(a, b, (((1,), (1,)), ((), ())), preferred_element_type=F32)


def params(mib):
    return pltpu.CompilerParams(vmem_limit_bytes=mib * MIB, dimension_semantics=("arbitrary",))


def whole(*shape):
    return pl.BlockSpec(shape, lambda i: (0,) * len(shape))


def block_of(waves):
    return max(size for size in range(1, 9) if waves % size == 0)


def set_factor(factor, damping):
    width, degrees = factor.shape
    chans = width // 2
    lanes = 128
    spread = jnp.broadcast_to(damping[...], (lanes, chans)).T
    for start in range(0, degrees, lanes):
        degree = (lax.broadcasted_iota(jnp.int32, (chans, lanes), 1) + start).astype(F32)
        ratio = degree * (degree + 1.0) / (degrees * (degrees + 1.0))
        piece = 1.0 / (1.0 + spread * ratio)
        factor[:chans, start : start + lanes] = piece
        factor[chans:, start : start + lanes] = piece


def copies_of(pairs, sems):
    copies = [pltpu.make_async_copy(src, dst, sems.at[k]) for k, (src, dst) in enumerate(pairs)]
    for copy in copies:
        copy.start()
    return copies


def forward_kernel(ranks, block, part, *refs):
    spec_h, cot_h, leg_h, damping_h, quad_h, out = refs[:6]
    spec, cot, leg, damping, quad, rows, factor, sems, small_sems = refs[6:]
    own, width, _ = spec.shape
    chans = width // 2
    lat = leg.shape[2]
    near = lat // ranks // 2 // PARTS
    span = ranks * near

    def moves(c):
        here = pl.ds(c * block, block)
        return [
            pltpu.make_async_copy(src.at[here], dst.at[here], sems.at[c, k])
            for k, (src, dst) in enumerate(((spec_h, spec), (cot_h, cot), (leg_h, leg)))
        ]

    small = copies_of([(damping_h, damping), (quad_h, quad)], small_sems)
    for c in range(own // block):
        for move in moves(c):
            move.start()
    for copy in small:
        copy.wait()
    set_factor(factor, damping)

    def step(c, carry):
        for move in moves(c):
            move.wait()
        weight = quad[...]
        for k in range(block):
            i = c * block + k
            tend = (cot[i].astype(F32) * factor[...]).astype(BF16)
            state = spec[i]
            stacked = jnp.concatenate(
                [state[:chans], tend[:chans], state[chans:], tend[chans:]], axis=0
            )
            res = dot(stacked, leg[i])
            res = jnp.concatenate(
                [
                    res[:chans],
                    res[chans : 2 * chans] * weight,
                    res[2 * chans : 3 * chans],
                    res[3 * chans :] * weight,
                ],
                axis=0,
            )
            res = res.astype(BF16).T.astype(F32)
            for side in range(2):
                start = (side * PARTS + part) * span
                rows[pl.ds(side * span * own + i, span, stride=own), :] = res[start : start + span]
        return carry

    lax.fori_loop(0, own // block, step, 0)
    size = near * own
    for d in range(ranks):
        for side in range(2):
            start = (side * ranks + d) * size
            out[d, side * size : (side + 1) * size, :] = rows[start : start + size, :].astype(BF16)


def forward(spectral, cot, legendre, damping, quad, ranks, part):
    own, width, degrees = spectral.shape
    lat = legendre.shape[2]
    block = block_of(own)
    shape = (ranks, lat // ranks // PARTS * own, 2 * width)
    return pl.pallas_call(
        functools.partial(forward_kernel, ranks, block, part),
        grid=(1,),
        in_specs=[HBM] * 5,
        out_specs=whole(*shape),
        out_shape=jax.ShapeDtypeStruct(shape, BF16),
        scratch_shapes=[
            pltpu.VMEM(spectral.shape, BF16),
            pltpu.VMEM(cot.shape, BF16),
            pltpu.VMEM(legendre.shape, BF16),
            pltpu.VMEM(damping.shape, F32),
            pltpu.VMEM(quad.shape, F32),
            pltpu.VMEM((lat // PARTS * own, 2 * width), F32),
            pltpu.VMEM((width, degrees), F32),
            pltpu.SemaphoreType.DMA((own // block, 3)),
            pltpu.SemaphoreType.DMA((2,)),
        ],
        compiler_params=params(60),
        name="legendre_forward",
    )(spectral, cot, legendre, damping, quad)


def weights_kernel(w_in, bias, w_out, weights):
    chans, hid = w_in.shape
    width = 2 * chans
    half_bias = bias[...] * 0.5
    high = half_bias.astype(BF16).astype(F32)
    left = half_bias - high
    mid = left.astype(BF16).astype(F32)
    low = left - mid
    stack = jnp.concatenate(
        [
            w_in[...].astype(F32) * 0.5,
            w_out[...].astype(F32) * 0.5,
            high,
            mid,
            low,
            jnp.zeros((13, hid), F32),
        ],
        axis=0,
    ).T.astype(BF16)
    lane = lax.broadcasted_iota(jnp.int32, stack.shape, 1)
    is_out = (lane >= chans) & (lane < width)
    nothing = jnp.zeros_like(stack)
    inward = jnp.where(is_out, nothing, stack)
    outward = jnp.where(is_out, stack, nothing)
    for k in range(0, hid, UNIT):
        weights[2 * k : 2 * k + UNIT, :] = inward[k : k + UNIT]
        weights[2 * k + UNIT : 2 * k + 2 * UNIT, :] = outward[k : k + UNIT]


def column_weights(w_in, bias, w_out):
    chans, hid = w_in.shape
    shape = (2 * hid, 2 * chans + 16)
    return pl.pallas_call(
        weights_kernel,
        grid=(1,),
        in_specs=[whole(*w_in.shape), whole(*bias.shape), whole(*w_out.shape)],
        out_specs=whole(*shape),
        out_shape=jax.ShapeDtypeStruct(shape, BF16),
        compiler_params=params(60),
        name="column_weights",
    )(w_in, bias, w_out)


def column_kernel(ranks, own, first, last, *refs):
    given = 4 if first else 5
    sources, out = refs[:given], refs[given]
    refs = refs[given + 1 :]
    after, refs = refs[0], refs[1:]
    arrived, table, w_in, weights, sums = refs[:5]
    fourier, cols, acts, evens, odds, edge, sems = refs[5:]
    chans, hid = w_in.shape
    waves = ranks * own
    lat_rows = arrived.shape[1] // own
    near = lat_rows // 2
    slots = table.shape[1]
    points = 2 * slots
    scale = math.sqrt(2.0 / points)
    width = 2 * chans
    arrived_h, table_h, w_in_h, weights_h = sources[:4]
    pairs = [(arrived_h, arrived), (w_in_h, w_in), (weights_h, weights)]
    if not first:
        pairs.append((sources[4], sums))
    small = copies_of(pairs, sems)
    moves = []
    for c in range(slots // SLOTS):
        here = pl.ds(c * SLOTS, SLOTS)
        moves.append(
            pltpu.make_async_copy(table_h.at[:, here], table.at[:, here], sems.at[4 + c])
        )
        moves[c].start()
    for p in range(lat_rows):
        cols[p, width:, :] = jnp.ones((16, points), BF16)
    for copy in small:
        copy.wait()
    if first:
        sums[...] = jnp.zeros_like(sums)
    for p in range(lat_rows):
        piece = jnp.concatenate(
            [arrived[s, p * own : (p + 1) * own, :] for s in range(ranks)], axis=0
        ).T
        row = width * p
        fourier[row : row + width, :waves] = piece[:width]
        fourier[row : row + width, waves:] = piece[width:]
    wave = lax.broadcasted_iota(jnp.int32, (waves, 128), 0)
    lane = lax.broadcasted_iota(jnp.int32, (waves, 128), 1)
    alternate = jnp.where(lane == 0, jnp.where(wave % 2 == 0, scale, -scale), 0.0).astype(BF16)
    for c, move in enumerate(moves):
        move.wait()
        here = slice(c * SLOTS, (c + 1) * SLOTS)
        even = dot(fourier[:, :waves], table[:waves, here])
        odd = dot(fourier[:, waves:], table[waves:, here])
        front = (even + odd).astype(BF16)
        rear = even - odd
        if c == 0:
            middle = dot(fourier[:, :waves], alternate)
            lane = lax.broadcasted_iota(jnp.int32, middle.shape, 1)
            rear = jnp.concatenate(
                [jnp.where(lane == 0, middle, rear[:, :128]), rear[:, 128:]], axis=1
            )
        rear = rear.astype(BF16)
        there = slice(slots + c * SLOTS, slots + (c + 1) * SLOTS)
        for p in range(lat_rows):
            cols[p, :width, here] = front[width * p : width * (p + 1)]
            cols[p, :width, there] = rear[width * p : width * (p + 1)]

    together = acts.shape[0]
    span = 512

    def rows_step(g, carry):
        for r in range(together):
            p = g * together + r
            for n in range(0, points, span):
                here = slice(n, n + span)
                columns_here = cols[p, :, here]
                for k in range(0, hid, UNIT):
                    both = dot(weights[2 * k : 2 * k + 2 * UNIT, :], columns_here).astype(BF16)
                    arg = both[:UNIT]
                    th = jnp.tanh(arg)
                    rise = 1 + th
                    act = arg * rise
                    acts[r, k : k + UNIT, here] = act
                    acts[r, hid + k : hid + k + UNIT, here] = both[UNIT:] * (
                        rise + act * (1 - th)
                    )
            grad = dot(w_in[...], acts[r, hid:, :])
            front, rear = grad[:, :slots], grad[:, slots:]
            edge[p] = rear[:, :128].astype(BF16)
            slot = lax.broadcasted_iota(jnp.int32, rear.shape, 1)
            evens[p] = (front + jnp.where(slot == 0, 0.0, rear)).astype(BF16)
            odds[p] = (front - rear).astype(BF16)
            sums[...] += dot_nt(acts[r], cols[p])
        return carry

    lax.fori_loop(0, lat_rows // together, rows_step, 0)

    def joined(ref):
        return ref[...].reshape(chans * lat_rows, ref.shape[2])

    real = dot_nt(table[:waves, :], joined(evens)) + dot_nt(alternate, joined(edge))
    real = real.astype(BF16)
    imag = dot_nt(table[waves:, :], joined(odds)).astype(BF16)
    span = near * chans
    for q in range(near):
        a, b = q * chans, (q + 1) * chans
        piece = jnp.concatenate(
            [real[:, a:b], imag[:, a:b], real[:, span + a : span + b], imag[:, span + a : span + b]],
            axis=1,
        )
        for d in range(ranks):
            out[d, q * own : (q + 1) * own, :] = piece[d * own : (d + 1) * own]
    if not last:
        after[...] = sums[...]
        return
    base = near * own
    turned = sums[...].T
    main = jnp.concatenate([turned[:chans, hid:], turned[chans:width, :hid]], axis=0)
    lanes = 4 * chans
    cuts = range(0, hid, lanes)
    after[...] = turned[width : width + 1, hid:]
    share = width // ranks
    for d in range(ranks):
        rows = [main[d * share : (d + 1) * share, c : c + lanes] for c in cuts]
        rows = jnp.concatenate(rows, axis=0).astype(BF16)
        out[d, base : base + rows.shape[0], :] = rows


def columns(arrived, table, w_in, weights, before, ranks, own, last):
    chans, hid = w_in.shape
    lat_rows = arrived.shape[1] // own
    waves = ranks * own
    slots = table.shape[1]
    points = 2 * slots
    together = 4
    rows_out = lat_rows // 2 * own
    lanes = 4 * chans
    if last:
        rows_out += (hid // lanes) * (2 * chans // ranks)
    sums = (2 * hid, 2 * chans + 16)
    after = (1, hid) if last else sums
    out_specs = [whole(ranks, rows_out, lanes), whole(*after)]
    out_shape = [
        jax.ShapeDtypeStruct((ranks, rows_out, lanes), BF16),
        jax.ShapeDtypeStruct(after, F32),
    ]
    sources = [arrived, table, w_in, weights] + before
    result = pl.pallas_call(
        functools.partial(column_kernel, ranks, own, not before, last),
        grid=(1,),
        in_specs=[HBM] * len(sources),
        out_specs=out_specs,
        out_shape=out_shape,
        scratch_shapes=[
            pltpu.VMEM(arrived.shape, BF16),
            pltpu.VMEM(table.shape, BF16),
            pltpu.VMEM(w_in.shape, BF16),
            pltpu.VMEM(weights.shape, BF16),
            pltpu.VMEM(sums, F32),
            pltpu.VMEM((2 * chans * lat_rows, 2 * waves), BF16),
            pltpu.VMEM((lat_rows, 2 * chans + 16, points), BF16),
            pltpu.VMEM((together, 2 * hid, points), BF16),
            pltpu.VMEM((lat_rows, chans, slots), BF16),
            pltpu.VMEM((lat_rows, chans, slots), BF16),
            pltpu.VMEM((lat_rows, chans, 128), BF16),
            pltpu.SemaphoreType.DMA((4 + slots // SLOTS,)),
        ],
        compiler_params=params(57),
        name="column_physics",
    )(*sources)
    return result[0], list(result[1:])


def backward_kernel(ranks, near, block, ahead, *refs):
    arrived_h, refs = refs[:PARTS], refs[PARTS:]
    cot_h, leg_h, damping_h, out_h = refs[:4]
    arrived, refs = refs[4 : 4 + PARTS], refs[4 + PARTS :]
    cot, leg, damping, out, rows, factor, in_sems, out_sems, sems = refs
    own, width, _ = cot.shape
    size = near * own
    early = copies_of([(damping_h, damping), *zip(arrived_h, arrived)], sems)

    def moves(c):
        here = pl.ds(c * block, block)
        return [
            pltpu.make_async_copy(src.at[here], dst.at[here], in_sems.at[c, k])
            for k, (src, dst) in enumerate(((cot_h, cot), (leg_h, leg)))
        ]

    def leave(c):
        here = pl.ds(c * block, block)
        return pltpu.make_async_copy(out.at[here], out_h.at[here], out_sems.at[c])

    for c in range(min(ahead, own // block)):
        for move in moves(c):
            move.start()
    early[0].wait()
    set_factor(factor, damping)
    for part in range(PARTS):
        early[1 + part].wait()
        for s in range(ranks):
            row = (part * ranks + s) * size
            rows[row : row + size, :] = arrived[part][s, :size, :].astype(F32)

    def step(c, carry):
        for move in moves(c):
            move.wait()

        @pl.when(c + ahead < own // block)
        def _():
            for move in moves(c + ahead):
                move.start()

        group = 2 if block % 2 == 0 else 1
        count = PARTS * ranks * near
        for k in range(0, block, group):
            members = [c * block + k + j for j in range(group)]
            mine = [rows[pl.ds(i, count, stride=own), :].astype(BF16) for i in members]
            mine = jnp.concatenate(mine, axis=0).T
            lhs = []
            for j in range(group):
                here = slice(j * count, (j + 1) * count)
                piece = jnp.concatenate([mine[:width, here], mine[width:, here]], axis=1)
                blank = jnp.zeros_like(piece)
                lhs.append(
                    jnp.concatenate([piece if g == j else blank for g in range(group)], axis=1)
                )
            product = dot_nt(
                jnp.concatenate(lhs, axis=0), jnp.concatenate([leg[i] for i in members], axis=1)
            )
            for j, i in enumerate(members):
                here = slice(j * width, (j + 1) * width)
                out[i] = cot[i].astype(F32) * factor[...] + product[here]
        leave(c).start()
        return carry

    lax.fori_loop(0, own // block, step, 0)
    for c in range(own // block):
        leave(c).wait()


def backward(arrived, cot, legendre, damping, ranks):
    own, width, degrees = cot.shape
    lat = legendre.shape[2]
    near = lat // ranks // 2 // PARTS
    block = block_of(own)
    return pl.pallas_call(
        functools.partial(backward_kernel, ranks, near, block, 2),
        grid=(1,),
        in_specs=[HBM] * (PARTS + 3),
        out_specs=HBM,
        out_shape=jax.ShapeDtypeStruct((own, width, degrees), F32),
        scratch_shapes=[pltpu.VMEM(piece.shape, BF16) for piece in arrived]
        + [
            pltpu.VMEM(cot.shape, BF16),
            pltpu.VMEM(legendre.shape, BF16),
            pltpu.VMEM(damping.shape, F32),
            pltpu.VMEM(cot.shape, F32),
            pltpu.VMEM((PARTS * ranks * near * own, 2 * width), F32),
            pltpu.VMEM((width, degrees), F32),
            pltpu.SemaphoreType.DMA((own // block, 2)),
            pltpu.SemaphoreType.DMA((own // block,)),
            pltpu.SemaphoreType.DMA((PARTS + 1,)),
        ],
        compiler_params=params(57),
        name="legendre_backward",
    )(*arrived, cot, legendre, damping)


def collect_kernel(base, arrived, bias, out):
    lanes = arrived.shape[2]
    total = arrived[0, base:, :].astype(F32)
    for s in range(1, arrived.shape[0]):
        total = total + arrived[s, base:, :].astype(F32)
    cuts = range(0, bias.shape[1], lanes)
    total = jnp.concatenate([total] + [bias[:, c : c + lanes] for c in cuts], axis=0).astype(BF16)
    for s in range(out.shape[0]):
        out[s] = total


def collect(arrived, bias, base, copies):
    lanes = arrived.shape[2]
    shape = (copies, arrived.shape[1] - base + bias.shape[1] // lanes, lanes)
    return pl.pallas_call(
        functools.partial(collect_kernel, base),
        grid=(1,),
        in_specs=[whole(*arrived.shape), whole(*bias.shape)],
        out_specs=whole(*shape),
        out_shape=jax.ShapeDtypeStruct(shape, BF16),
        compiler_params=params(8),
        name="collect_gradients",
    )(arrived, bias)


def finish_kernel(groups, scale, parts, grad_in, grad_bias, grad_out):
    ranks = parts.shape[0] // groups
    chans, hid = grad_in.shape
    lanes = parts.shape[2]
    cuts = hid // lanes
    share = 2 * chans // ranks
    for r in range(ranks):
        total = parts[r].astype(F32)
        for g in range(1, groups):
            total = total + parts[g * ranks + r].astype(F32)
        total = total * scale
        row = r * share
        dest, row = (grad_in, row) if row < chans else (grad_out, row - chans)
        for c in range(cuts):
            dest[row : row + share, c * lanes : (c + 1) * lanes] = total[c * share : (c + 1) * share]
    tail = parts[0, cuts * share :].astype(F32)
    for s in range(1, parts.shape[0]):
        tail = tail + parts[s, cuts * share :].astype(F32)
    for c in range(cuts):
        grad_bias[:, c * lanes : (c + 1) * lanes] = tail[c : c + 1] * scale


def finish(parts, hid, chans, groups, scale):
    return pl.pallas_call(
        functools.partial(finish_kernel, groups, scale),
        grid=(1,),
        in_specs=[whole(*parts.shape)],
        out_specs=(whole(chans, hid), whole(1, hid), whole(chans, hid)),
        out_shape=(
            jax.ShapeDtypeStruct((chans, hid), F32),
            jax.ShapeDtypeStruct((1, hid), F32),
            jax.ShapeDtypeStruct((chans, hid), F32),
        ),
        compiler_params=params(8),
        name="weight_gradients",
    )(parts)


def body(
    spectral_state, cotangent, legendre, quadrature, damping, physics_in, physics_bias, physics_out
):
    spectral = spectral_state[0]
    cot = cotangent[0]
    own, width, degrees = spectral.shape
    chans = width // 2
    hid = physics_in.shape[0]
    ranks = lax.axis_size("lat")
    groups = lax.axis_size("grp")
    lat = legendre.shape[2]
    lat_rows = lat // ranks
    table = jnp.asarray(longitude_table(own * ranks, NLON))
    damping = damping[None, :]
    exchange = functools.partial(
        lax.all_to_all, axis_name="lat", split_axis=0, concat_axis=0, tiled=True
    )

    weights = column_weights(physics_in.T, physics_bias[None, :], physics_out)
    arrived = []
    for part in range(PARTS):
        sent = forward(spectral, cot, legendre, damping, quadrature[None, :], ranks, part)
        if arrived:
            sent, weights, arrived[-1] = lax.optimization_barrier((sent, weights, arrived[-1]))
        arrived.append(exchange(sent))
    sums = []
    returned = []
    for part in range(PARTS):
        back, sums = columns(
            arrived[part],
            table,
            physics_in.T,
            weights,
            sums,
            ranks,
            own,
            part == PARTS - 1,
        )
        if returned:
            back, returned[-1] = lax.optimization_barrier((back, returned[-1]))
        returned.append(exchange(back))

    base = lat_rows // 2 // PARTS * own
    spread = collect(returned[-1], sums[0], base, groups * ranks)
    parts = lax.all_to_all(spread, ("grp", "lat"), split_axis=0, concat_axis=0, tiled=True)
    grad_state = backward(returned, cot, legendre, damping, ranks)
    scale = 1.0 / math.sqrt(groups * lat * NLON)
    grad_in, grad_bias, grad_out = finish(parts, hid, chans, groups, scale)
    return (grad_state[None], grad_in.T, grad_bias[0], grad_out)


def solution(mesh):
    in_specs = (
        P("grp", "lat", None, None),
        P("grp", "lat", None, None),
        P("lat", None, None),
        P(),
        P(),
        P(),
        P(),
        P(),
    )
    out_specs = (P("grp", "lat", None, None), P(), P(), P())
    return jax.shard_map(body, mesh=mesh, in_specs=in_specs, out_specs=out_specs, check_vma=False)
```

```python
import functools
import math

import jax
import jax.numpy as jnp
import numpy as np
import ml_dtypes
from jax import lax
from jax.experimental import pallas as pl
from jax.experimental.pallas import tpu as pltpu
from jax.sharding import PartitionSpec as P

NLON = 2560
MIB = 1024 * 1024
F32 = jnp.float32
BF16 = jnp.bfloat16
PARTS = 2
SLOTS = 256
UNIT = 128
HBM = pl.BlockSpec(memory_space=pl.ANY)


def longitude_table(waves, points):
    slots = points // 2
    phase = np.arange(waves)[:, None] * np.arange(slots)[None, :] % points
    angle = phase * (2.0 * math.pi / points)
    scale = math.sqrt(2.0 / points)
    both = np.concatenate([np.cos(angle) * scale, -np.sin(angle) * scale])
    return both.astype(np.float32).astype(ml_dtypes.bfloat16)


def dot(a, b):
    return jnp.dot(a, b, preferred_element_type=F32)


def dot_nt(a, b):
    return lax.dot_general(a, b, (((1,), (1,)), ((), ())), preferred_element_type=F32)


def params(mib):
    return pltpu.CompilerParams(vmem_limit_bytes=mib * MIB, dimension_semantics=("arbitrary",))


def whole(*shape):
    return pl.BlockSpec(shape, lambda i: (0,) * len(shape))


def block_of(waves, most):
    return max(size for size in range(1, most + 1) if waves % size == 0)


def set_factor(factor, damping):
    width, degrees = factor.shape
    chans = width // 2
    lanes = 128
    spread = jnp.broadcast_to(damping[...], (lanes, chans)).T
    for start in range(0, degrees, lanes):
        degree = (lax.broadcasted_iota(jnp.int32, (chans, lanes), 1) + start).astype(F32)
        ratio = degree * (degree + 1.0) / (degrees * (degrees + 1.0))
        piece = 1.0 / (1.0 + spread * ratio)
        factor[:chans, start : start + lanes] = piece
        factor[chans:, start : start + lanes] = piece


def copies_of(pairs, sems):
    copies = [pltpu.make_async_copy(src, dst, sems.at[k]) for k, (src, dst) in enumerate(pairs)]
    for copy in copies:
        copy.start()
    return copies


def forward_kernel(ranks, block, part, *refs):
    spec_h, cot_h, leg_h, damping, quad, out = refs[:6]
    spec, cot, leg, rows, factor, sems = refs[6:]
    own, width, _ = spec.shape
    chans = width // 2
    lat = leg.shape[2]
    near = lat // ranks // 2 // PARTS
    span = ranks * near

    def moves(c):
        here = pl.ds(c * block, block)
        return [
            pltpu.make_async_copy(src.at[here], dst.at[here], sems.at[c, k])
            for k, (src, dst) in enumerate(((spec_h, spec), (cot_h, cot), (leg_h, leg)))
        ]

    ahead = 4
    for c in range(min(ahead, own // block)):
        for move in moves(c):
            move.start()
    set_factor(factor, damping)

    def step(c, carry):
        for move in moves(c):
            move.wait()

        @pl.when(c + ahead < own // block)
        def _():
            for move in moves(c + ahead):
                move.start()

        weight = quad[...]
        for k in range(block):
            i = c * block + k
            tend = (cot[i].astype(F32) * factor[...]).astype(BF16)
            state = spec[i]
            stacked = jnp.concatenate(
                [state[:chans], tend[:chans], state[chans:], tend[chans:]], axis=0
            )
            res = dot(stacked, leg[i])
            res = jnp.concatenate(
                [
                    res[:chans],
                    res[chans : 2 * chans] * weight,
                    res[2 * chans : 3 * chans],
                    res[3 * chans :] * weight,
                ],
                axis=0,
            )
            res = res.astype(BF16).T.astype(F32)
            for side in range(2):
                start = (side * PARTS + part) * span
                rows[pl.ds(side * span * own + i, span, stride=own), :] = res[start : start + span]
        return carry

    lax.fori_loop(0, own // block, step, 0)
    size = near * own
    for d in range(ranks):
        for side in range(2):
            start = (side * ranks + d) * size
            out[d, side * size : (side + 1) * size, :] = rows[start : start + size, :].astype(BF16)


def forward(spectral, cot, legendre, damping, quad, ranks, part):
    own, width, degrees = spectral.shape
    lat = legendre.shape[2]
    block = block_of(own, 4)
    shape = (ranks, lat // ranks // PARTS * own, 2 * width)
    return pl.pallas_call(
        functools.partial(forward_kernel, ranks, block, part),
        grid=(1,),
        in_specs=[HBM] * 3 + [whole(*damping.shape), whole(1, lat)],
        out_specs=whole(*shape),
        out_shape=jax.ShapeDtypeStruct(shape, BF16),
        scratch_shapes=[
            pltpu.VMEM(spectral.shape, BF16),
            pltpu.VMEM(cot.shape, BF16),
            pltpu.VMEM(legendre.shape, BF16),
            pltpu.VMEM((lat // PARTS * own, 2 * width), F32),
            pltpu.VMEM((width, degrees), F32),
            pltpu.SemaphoreType.DMA((own // block, 3)),
        ],
        compiler_params=params(60),
        name="legendre_forward",
    )(spectral, cot, legendre, damping, quad)


def weights_kernel(w_in, bias, w_out, weights):
    chans, hid = w_in.shape
    width = 2 * chans
    half_bias = bias[...] * 0.5
    high = half_bias.astype(BF16).astype(F32)
    left = half_bias - high
    mid = left.astype(BF16).astype(F32)
    low = left - mid
    stack = jnp.concatenate(
        [
            w_in[...].astype(F32) * 0.5,
            w_out[...].astype(F32) * 0.5,
            high,
            mid,
            low,
            jnp.zeros((13, hid), F32),
        ],
        axis=0,
    ).T.astype(BF16)
    lane = lax.broadcasted_iota(jnp.int32, stack.shape, 1)
    is_out = (lane >= chans) & (lane < width)
    nothing = jnp.zeros_like(stack)
    inward = jnp.where(is_out, nothing, stack)
    outward = jnp.where(is_out, stack, nothing)
    for k in range(0, hid, UNIT):
        weights[2 * k : 2 * k + UNIT, :] = inward[k : k + UNIT]
        weights[2 * k + UNIT : 2 * k + 2 * UNIT, :] = outward[k : k + UNIT]


def column_weights(w_in, bias, w_out):
    chans, hid = w_in.shape
    shape = (2 * hid, 2 * chans + 16)
    return pl.pallas_call(
        weights_kernel,
        grid=(1,),
        in_specs=[whole(*w_in.shape), whole(*bias.shape), whole(*w_out.shape)],
        out_specs=whole(*shape),
        out_shape=jax.ShapeDtypeStruct(shape, BF16),
        compiler_params=params(60),
        name="column_weights",
    )(w_in, bias, w_out)


def column_kernel(ranks, own, first, last, *refs):
    given = 4 if first else 5
    sources, out = refs[:given], refs[given]
    refs = refs[given + 1 :]
    after, refs = refs[0], refs[1:]
    arrived, table, w_in, weights, sums = refs[:5]
    fourier, cols, acts, evens, odds, edge, sems = refs[5:]
    chans, hid = w_in.shape
    waves = ranks * own
    lat_rows = arrived.shape[1] // own
    near = lat_rows // 2
    slots = table.shape[1]
    points = 2 * slots
    scale = math.sqrt(2.0 / points)
    width = 2 * chans
    arrived_h, table_h, w_in_h, weights_h = sources[:4]
    pairs = [(arrived_h, arrived), (w_in_h, w_in), (weights_h, weights)]
    if not first:
        pairs.append((sources[4], sums))
    small = copies_of(pairs, sems)
    moves = []
    for c in range(slots // SLOTS):
        here = pl.ds(c * SLOTS, SLOTS)
        moves.append(
            pltpu.make_async_copy(table_h.at[:, here], table.at[:, here], sems.at[4 + c])
        )
    moves[0].start()
    for p in range(lat_rows):
        cols[p, width:, :] = jnp.ones((16, points), BF16)
    for copy in small:
        copy.wait()
    for move in moves[1:]:
        move.start()
    if first:
        sums[...] = jnp.zeros_like(sums)
    for p in range(lat_rows):
        piece = jnp.concatenate(
            [arrived[s, p * own : (p + 1) * own, :] for s in range(ranks)], axis=0
        ).T
        row = width * p
        fourier[row : row + width, :waves] = piece[:width]
        fourier[row : row + width, waves:] = piece[width:]
    wave = lax.broadcasted_iota(jnp.int32, (waves, 128), 0)
    lane = lax.broadcasted_iota(jnp.int32, (waves, 128), 1)
    alternate = jnp.where(lane == 0, jnp.where(wave % 2 == 0, scale, -scale), 0.0).astype(BF16)
    for c, move in enumerate(moves):
        move.wait()
        here = slice(c * SLOTS, (c + 1) * SLOTS)
        even = dot(fourier[:, :waves], table[:waves, here])
        odd = dot(fourier[:, waves:], table[waves:, here])
        front = (even + odd).astype(BF16)
        rear = even - odd
        if c == 0:
            middle = dot(fourier[:, :waves], alternate)
            lane = lax.broadcasted_iota(jnp.int32, middle.shape, 1)
            rear = jnp.concatenate(
                [jnp.where(lane == 0, middle, rear[:, :128]), rear[:, 128:]], axis=1
            )
        rear = rear.astype(BF16)
        there = slice(slots + c * SLOTS, slots + (c + 1) * SLOTS)
        for p in range(lat_rows):
            cols[p, :width, here] = front[width * p : width * (p + 1)]
            cols[p, :width, there] = rear[width * p : width * (p + 1)]

    together = acts.shape[0]
    span = 512

    def rows_step(g, carry):
        for r in range(together):
            p = g * together + r
            for n in range(0, points, span):
                here = slice(n, n + span)
                columns_here = cols[p, :, here]
                for k in range(0, hid, UNIT):
                    both = dot(weights[2 * k : 2 * k + 2 * UNIT, :], columns_here).astype(BF16)
                    arg = both[:UNIT]
                    th = jnp.tanh(arg)
                    rise = 1 + th
                    act = arg * rise
                    acts[r, k : k + UNIT, here] = act
                    acts[r, hid + k : hid + k + UNIT, here] = both[UNIT:] * (
                        rise + act * (1 - th)
                    )
            grad = dot(w_in[...], acts[r, hid:, :])
            front, rear = grad[:, :slots], grad[:, slots:]
            edge[p] = rear[:, :128].astype(BF16)
            slot = lax.broadcasted_iota(jnp.int32, rear.shape, 1)
            evens[p] = (front + jnp.where(slot == 0, 0.0, rear)).astype(BF16)
            odds[p] = (front - rear).astype(BF16)
            sums[...] += dot_nt(acts[r], cols[p])
        return carry

    lax.fori_loop(0, lat_rows // together, rows_step, 0)

    def joined(ref):
        return ref[...].reshape(chans * lat_rows, ref.shape[2])

    real = dot_nt(table[:waves, :], joined(evens)) + dot_nt(alternate, joined(edge))
    real = real.astype(BF16)
    imag = dot_nt(table[waves:, :], joined(odds)).astype(BF16)
    span = near * chans
    for q in range(near):
        a, b = q * chans, (q + 1) * chans
        piece = jnp.concatenate(
            [real[:, a:b], imag[:, a:b], real[:, span + a : span + b], imag[:, span + a : span + b]],
            axis=1,
        )
        for d in range(ranks):
            out[d, q * own : (q + 1) * own, :] = piece[d * own : (d + 1) * own]
    if not last:
        after[...] = sums[...]
        return
    base = near * own
    turned = sums[...].T
    main = jnp.concatenate([turned[:chans, hid:], turned[chans:width, :hid]], axis=0)
    lanes = 4 * chans
    cuts = range(0, hid, lanes)
    after[...] = turned[width : width + 1, hid:]
    share = width // ranks
    for d in range(ranks):
        rows = [main[d * share : (d + 1) * share, c : c + lanes] for c in cuts]
        rows = jnp.concatenate(rows, axis=0).astype(BF16)
        out[d, base : base + rows.shape[0], :] = rows


def columns(arrived, table, w_in, weights, before, ranks, own, last):
    chans, hid = w_in.shape
    lat_rows = arrived.shape[1] // own
    waves = ranks * own
    slots = table.shape[1]
    points = 2 * slots
    together = 4
    rows_out = lat_rows // 2 * own
    lanes = 4 * chans
    if last:
        rows_out += (hid // lanes) * (2 * chans // ranks)
    sums = (2 * hid, 2 * chans + 16)
    after = (1, hid) if last else sums
    out_specs = [whole(ranks, rows_out, lanes), whole(*after)]
    out_shape = [
        jax.ShapeDtypeStruct((ranks, rows_out, lanes), BF16),
        jax.ShapeDtypeStruct(after, F32),
    ]
    sources = [arrived, table, w_in, weights] + before
    result = pl.pallas_call(
        functools.partial(column_kernel, ranks, own, not before, last),
        grid=(1,),
        in_specs=[HBM] * len(sources),
        out_specs=out_specs,
        out_shape=out_shape,
        scratch_shapes=[
            pltpu.VMEM(arrived.shape, BF16),
            pltpu.VMEM(table.shape, BF16),
            pltpu.VMEM(w_in.shape, BF16),
            pltpu.VMEM(weights.shape, BF16),
            pltpu.VMEM(sums, F32),
            pltpu.VMEM((2 * chans * lat_rows, 2 * waves), BF16),
            pltpu.VMEM((lat_rows, 2 * chans + 16, points), BF16),
            pltpu.VMEM((together, 2 * hid, points), BF16),
            pltpu.VMEM((lat_rows, chans, slots), BF16),
            pltpu.VMEM((lat_rows, chans, slots), BF16),
            pltpu.VMEM((lat_rows, chans, 128), BF16),
            pltpu.SemaphoreType.DMA((4 + slots // SLOTS,)),
        ],
        compiler_params=params(57),
        name="column_physics",
    )(*sources)
    return result[0], list(result[1:])


def backward_kernel(ranks, near, block, ahead, *refs):
    arrived_h, refs = refs[:PARTS], refs[PARTS:]
    cot_h, leg_h, damping_h, out_h = refs[:4]
    arrived, refs = refs[4 : 4 + PARTS], refs[4 + PARTS :]
    cot, leg, damping, out, rows, factor, in_sems, out_sems, sems = refs
    own, width, _ = cot.shape
    size = near * own
    early = copies_of([(damping_h, damping), *zip(arrived_h, arrived)], sems)

    def moves(c):
        here = pl.ds(c * block, block)
        return [
            pltpu.make_async_copy(src.at[here], dst.at[here], in_sems.at[c, k])
            for k, (src, dst) in enumerate(((cot_h, cot), (leg_h, leg)))
        ]

    def leave(c):
        here = pl.ds(c * block, block)
        return pltpu.make_async_copy(out.at[here], out_h.at[here], out_sems.at[c])

    for c in range(min(ahead, own // block)):
        for move in moves(c):
            move.start()
    early[0].wait()
    set_factor(factor, damping)
    for part in range(PARTS):
        early[1 + part].wait()
        for s in range(ranks):
            row = (part * ranks + s) * size
            rows[row : row + size, :] = arrived[part][s, :size, :].astype(F32)

    def step(c, carry):
        for move in moves(c):
            move.wait()

        @pl.when(c + ahead < own // block)
        def _():
            for move in moves(c + ahead):
                move.start()

        group = 2 if block % 2 == 0 else 1
        count = PARTS * ranks * near
        for k in range(0, block, group):
            members = [c * block + k + j for j in range(group)]
            mine = [rows[pl.ds(i, count, stride=own), :].astype(BF16) for i in members]
            mine = jnp.concatenate(mine, axis=0).T
            lhs = []
            for j in range(group):
                here = slice(j * count, (j + 1) * count)
                piece = jnp.concatenate([mine[:width, here], mine[width:, here]], axis=1)
                blank = jnp.zeros_like(piece)
                lhs.append(
                    jnp.concatenate([piece if g == j else blank for g in range(group)], axis=1)
                )
            product = dot_nt(
                jnp.concatenate(lhs, axis=0), jnp.concatenate([leg[i] for i in members], axis=1)
            )
            for j, i in enumerate(members):
                here = slice(j * width, (j + 1) * width)
                out[i] = cot[i].astype(F32) * factor[...] + product[here]
        leave(c).start()
        return carry

    lax.fori_loop(0, own // block, step, 0)
    for c in range(own // block):
        leave(c).wait()


def backward(arrived, cot, legendre, damping, ranks):
    own, width, degrees = cot.shape
    lat = legendre.shape[2]
    near = lat // ranks // 2 // PARTS
    block = block_of(own, 8)
    return pl.pallas_call(
        functools.partial(backward_kernel, ranks, near, block, 2),
        grid=(1,),
        in_specs=[HBM] * (PARTS + 3),
        out_specs=HBM,
        out_shape=jax.ShapeDtypeStruct((own, width, degrees), F32),
        scratch_shapes=[pltpu.VMEM(piece.shape, BF16) for piece in arrived]
        + [
            pltpu.VMEM(cot.shape, BF16),
            pltpu.VMEM(legendre.shape, BF16),
            pltpu.VMEM(damping.shape, F32),
            pltpu.VMEM(cot.shape, F32),
            pltpu.VMEM((PARTS * ranks * near * own, 2 * width), F32),
            pltpu.VMEM((width, degrees), F32),
            pltpu.SemaphoreType.DMA((own // block, 2)),
            pltpu.SemaphoreType.DMA((own // block,)),
            pltpu.SemaphoreType.DMA((PARTS + 1,)),
        ],
        compiler_params=params(57),
        name="legendre_backward",
    )(*arrived, cot, legendre, damping)


def collect_kernel(base, arrived, bias, out):
    lanes = arrived.shape[2]
    total = arrived[0, base:, :].astype(F32)
    for s in range(1, arrived.shape[0]):
        total = total + arrived[s, base:, :].astype(F32)
    cuts = range(0, bias.shape[1], lanes)
    total = jnp.concatenate([total] + [bias[:, c : c + lanes] for c in cuts], axis=0).astype(BF16)
    for s in range(out.shape[0]):
        out[s] = total


def collect(arrived, bias, base, copies):
    lanes = arrived.shape[2]
    shape = (copies, arrived.shape[1] - base + bias.shape[1] // lanes, lanes)
    return pl.pallas_call(
        functools.partial(collect_kernel, base),
        grid=(1,),
        in_specs=[whole(*arrived.shape), whole(*bias.shape)],
        out_specs=whole(*shape),
        out_shape=jax.ShapeDtypeStruct(shape, BF16),
        compiler_params=params(8),
        name="collect_gradients",
    )(arrived, bias)


def finish_kernel(groups, scale, parts, grad_in, grad_bias, grad_out):
    ranks = parts.shape[0] // groups
    chans, hid = grad_in.shape
    lanes = parts.shape[2]
    cuts = hid // lanes
    share = 2 * chans // ranks
    for r in range(ranks):
        total = parts[r].astype(F32)
        for g in range(1, groups):
            total = total + parts[g * ranks + r].astype(F32)
        total = total * scale
        row = r * share
        dest, row = (grad_in, row) if row < chans else (grad_out, row - chans)
        for c in range(cuts):
            dest[row : row + share, c * lanes : (c + 1) * lanes] = total[c * share : (c + 1) * share]
    tail = parts[0, cuts * share :].astype(F32)
    for s in range(1, parts.shape[0]):
        tail = tail + parts[s, cuts * share :].astype(F32)
    for c in range(cuts):
        grad_bias[:, c * lanes : (c + 1) * lanes] = tail[c : c + 1] * scale


def finish(parts, hid, chans, groups, scale):
    return pl.pallas_call(
        functools.partial(finish_kernel, groups, scale),
        grid=(1,),
        in_specs=[whole(*parts.shape)],
        out_specs=(whole(chans, hid), whole(1, hid), whole(chans, hid)),
        out_shape=(
            jax.ShapeDtypeStruct((chans, hid), F32),
            jax.ShapeDtypeStruct((1, hid), F32),
            jax.ShapeDtypeStruct((chans, hid), F32),
        ),
        compiler_params=params(8),
        name="weight_gradients",
    )(parts)


def body(
    spectral_state, cotangent, legendre, quadrature, damping, physics_in, physics_bias, physics_out
):
    spectral = spectral_state[0]
    cot = cotangent[0]
    own, width, degrees = spectral.shape
    chans = width // 2
    hid = physics_in.shape[0]
    ranks = lax.axis_size("lat")
    groups = lax.axis_size("grp")
    lat = legendre.shape[2]
    lat_rows = lat // ranks
    table = jnp.asarray(longitude_table(own * ranks, NLON))
    damping = damping[None, :]
    exchange = functools.partial(
        lax.all_to_all, axis_name="lat", split_axis=0, concat_axis=0, tiled=True
    )

    weights = column_weights(physics_in.T, physics_bias[None, :], physics_out)
    arrived = []
    for part in range(PARTS):
        sent = forward(spectral, cot, legendre, damping, quadrature[None, :], ranks, part)
        if arrived:
            sent, weights, arrived[-1] = lax.optimization_barrier((sent, weights, arrived[-1]))
        arrived.append(exchange(sent))
    sums = []
    returned = []
    for part in range(PARTS):
        back, sums = columns(
            arrived[part],
            table,
            physics_in.T,
            weights,
            sums,
            ranks,
            own,
            part == PARTS - 1,
        )
        if returned:
            back, returned[-1] = lax.optimization_barrier((back, returned[-1]))
        returned.append(exchange(back))

    base = lat_rows // 2 // PARTS * own
    spread = collect(returned[-1], sums[0], base, groups * ranks)
    parts = lax.all_to_all(spread, ("grp", "lat"), split_axis=0, concat_axis=0, tiled=True)
    grad_state = backward(returned, cot, legendre, damping, ranks)
    scale = 1.0 / math.sqrt(groups * lat * NLON)
    grad_in, grad_bias, grad_out = finish(parts, hid, chans, groups, scale)
    return (grad_state[None], grad_in.T, grad_bias[0], grad_out)


def solution(mesh):
    in_specs = (
        P("grp", "lat", None, None),
        P("grp", "lat", None, None),
        P("lat", None, None),
        P(),
        P(),
        P(),
        P(),
        P(),
    )
    out_specs = (P("grp", "lat", None, None), P(), P(), P())
    return jax.shard_map(body, mesh=mesh, in_specs=in_specs, out_specs=out_specs, check_vma=False)
```

```python
import functools
import math

import jax
import jax.numpy as jnp
import numpy as np
import ml_dtypes
from jax import lax
from jax.experimental import pallas as pl
from jax.experimental.pallas import tpu as pltpu
from jax.sharding import PartitionSpec as P

NLON = 2560
MIB = 1024 * 1024
F32 = jnp.float32
BF16 = jnp.bfloat16
PARTS = 2
SLOTS = 256
UNIT = 128
HBM = pl.BlockSpec(memory_space=pl.ANY)


def longitude_table(waves, points):
    slots = points // 2
    phase = np.arange(waves)[:, None] * np.arange(slots)[None, :] % points
    angle = phase * (2.0 * math.pi / points)
    scale = math.sqrt(2.0 / points)
    both = np.concatenate([np.cos(angle) * scale, -np.sin(angle) * scale])
    return both.astype(np.float32).astype(ml_dtypes.bfloat16)


def dot(a, b):
    return jnp.dot(a, b, preferred_element_type=F32)


def dot_nt(a, b):
    return lax.dot_general(a, b, (((1,), (1,)), ((), ())), preferred_element_type=F32)


def params(mib):
    return pltpu.CompilerParams(vmem_limit_bytes=mib * MIB, dimension_semantics=("arbitrary",))


def whole(*shape):
    return pl.BlockSpec(shape, lambda i: (0,) * len(shape))


def block_of(waves, most):
    return max(size for size in range(1, most + 1) if waves % size == 0)


def set_factor(factor, damping):
    width, degrees = factor.shape
    chans = width // 2
    lanes = 128
    spread = jnp.broadcast_to(damping[...], (lanes, chans)).T
    for start in range(0, degrees, lanes):
        degree = (lax.broadcasted_iota(jnp.int32, (chans, lanes), 1) + start).astype(F32)
        ratio = degree * (degree + 1.0) / (degrees * (degrees + 1.0))
        piece = 1.0 / (1.0 + spread * ratio)
        factor[:chans, start : start + lanes] = piece
        factor[chans:, start : start + lanes] = piece


def copies_of(pairs, sems):
    copies = [pltpu.make_async_copy(src, dst, sems.at[k]) for k, (src, dst) in enumerate(pairs)]
    for copy in copies:
        copy.start()
    return copies


def forward_kernel(ranks, block, part, *refs):
    spec_h, cot_h, leg_h, damping, quad, out = refs[:6]
    spec, cot, leg, rows, factor, sems = refs[6:]
    own, width, _ = spec.shape
    chans = width // 2
    lat = leg.shape[2]
    near = lat // ranks // 2 // PARTS
    span = ranks * near

    def moves(c):
        here = pl.ds(c * block, block)
        return [
            pltpu.make_async_copy(src.at[here], dst.at[here], sems.at[c, k])
            for k, (src, dst) in enumerate(((spec_h, spec), (cot_h, cot), (leg_h, leg)))
        ]

    for c in range(own // block):
        for move in moves(c):
            move.start()
    set_factor(factor, damping)

    def step(c, carry):
        for move in moves(c):
            move.wait()
        weight = quad[...]
        for k in range(block):
            i = c * block + k
            tend = (cot[i].astype(F32) * factor[...]).astype(BF16)
            state = spec[i]
            stacked = jnp.concatenate(
                [state[:chans], tend[:chans], state[chans:], tend[chans:]], axis=0
            )
            res = dot(stacked, leg[i])
            res = jnp.concatenate(
                [
                    res[:chans],
                    res[chans : 2 * chans] * weight,
                    res[2 * chans : 3 * chans],
                    res[3 * chans :] * weight,
                ],
                axis=0,
            )
            res = res.astype(BF16).T.astype(F32)
            for side in range(2):
                start = (side * PARTS + part) * span
                rows[pl.ds(side * span * own + i, span, stride=own), :] = res[start : start + span]
        return carry

    lax.fori_loop(0, own // block, step, 0)
    size = near * own
    for d in range(ranks):
        for side in range(2):
            start = (side * ranks + d) * size
            out[d, side * size : (side + 1) * size, :] = rows[start : start + size, :].astype(BF16)


def forward(spectral, cot, legendre, damping, quad, ranks, part):
    own, width, degrees = spectral.shape
    lat = legendre.shape[2]
    block = block_of(own, 8)
    shape = (ranks, lat // ranks // PARTS * own, 2 * width)
    return pl.pallas_call(
        functools.partial(forward_kernel, ranks, block, part),
        grid=(1,),
        in_specs=[HBM] * 3 + [whole(*damping.shape), whole(1, lat)],
        out_specs=whole(*shape),
        out_shape=jax.ShapeDtypeStruct(shape, BF16),
        scratch_shapes=[
            pltpu.VMEM(spectral.shape, BF16),
            pltpu.VMEM(cot.shape, BF16),
            pltpu.VMEM(legendre.shape, BF16),
            pltpu.VMEM((lat // PARTS * own, 2 * width), F32),
            pltpu.VMEM((width, degrees), F32),
            pltpu.SemaphoreType.DMA((own // block, 3)),
        ],
        compiler_params=params(60),
        name="legendre_forward",
    )(spectral, cot, legendre, damping, quad)


def weights_kernel(w_in, bias, w_out, weights):
    chans, hid = w_in.shape
    width = 2 * chans
    half_bias = bias[...] * 0.5
    high = half_bias.astype(BF16).astype(F32)
    left = half_bias - high
    mid = left.astype(BF16).astype(F32)
    low = left - mid
    stack = jnp.concatenate(
        [
            w_in[...].astype(F32) * 0.5,
            w_out[...].astype(F32) * 0.5,
            high,
            mid,
            low,
            jnp.zeros((13, hid), F32),
        ],
        axis=0,
    ).T.astype(BF16)
    lane = lax.broadcasted_iota(jnp.int32, stack.shape, 1)
    is_out = (lane >= chans) & (lane < width)
    nothing = jnp.zeros_like(stack)
    inward = jnp.where(is_out, nothing, stack)
    outward = jnp.where(is_out, stack, nothing)
    for k in range(0, hid, UNIT):
        weights[2 * k : 2 * k + UNIT, :] = inward[k : k + UNIT]
        weights[2 * k + UNIT : 2 * k + 2 * UNIT, :] = outward[k : k + UNIT]


def column_weights(w_in, bias, w_out):
    chans, hid = w_in.shape
    shape = (2 * hid, 2 * chans + 16)
    return pl.pallas_call(
        weights_kernel,
        grid=(1,),
        in_specs=[whole(*w_in.shape), whole(*bias.shape), whole(*w_out.shape)],
        out_specs=whole(*shape),
        out_shape=jax.ShapeDtypeStruct(shape, BF16),
        compiler_params=params(60),
        name="column_weights",
    )(w_in, bias, w_out)


def column_kernel(ranks, own, first, last, *refs):
    given = 4 if first else 5
    sources, out = refs[:given], refs[given]
    refs = refs[given + 1 :]
    after, refs = refs[0], refs[1:]
    arrived, table, w_in, weights, sums = refs[:5]
    fourier, cols, acts, evens, odds, edge, sems = refs[5:]
    chans, hid = w_in.shape
    waves = ranks * own
    lat_rows = arrived.shape[1] // own
    near = lat_rows // 2
    slots = table.shape[1]
    points = 2 * slots
    scale = math.sqrt(2.0 / points)
    width = 2 * chans
    arrived_h, table_h, w_in_h, weights_h = sources[:4]
    pairs = [(arrived_h, arrived), (w_in_h, w_in), (weights_h, weights)]
    if not first:
        pairs.append((sources[4], sums))
    small = copies_of(pairs, sems)
    moves = []
    for c in range(slots // SLOTS):
        here = pl.ds(c * SLOTS, SLOTS)
        moves.append(
            pltpu.make_async_copy(table_h.at[:, here], table.at[:, here], sems.at[4 + c])
        )
        moves[c].start()
    for p in range(lat_rows):
        cols[p, width:, :] = jnp.ones((16, points), BF16)
    for copy in small:
        copy.wait()
    if first:
        sums[...] = jnp.zeros_like(sums)
    for p in range(lat_rows):
        piece = jnp.concatenate(
            [arrived[s, p * own : (p + 1) * own, :] for s in range(ranks)], axis=0
        ).T
        row = width * p
        fourier[row : row + width, :waves] = piece[:width]
        fourier[row : row + width, waves:] = piece[width:]
    wave = lax.broadcasted_iota(jnp.int32, (waves, 128), 0)
    lane = lax.broadcasted_iota(jnp.int32, (waves, 128), 1)
    alternate = jnp.where(lane == 0, jnp.where(wave % 2 == 0, scale, -scale), 0.0).astype(BF16)
    for c, move in enumerate(moves):
        move.wait()
        here = slice(c * SLOTS, (c + 1) * SLOTS)
        even = dot(fourier[:, :waves], table[:waves, here])
        odd = dot(fourier[:, waves:], table[waves:, here])
        front = (even + odd).astype(BF16)
        rear = even - odd
        if c == 0:
            middle = dot(fourier[:, :waves], alternate)
            lane = lax.broadcasted_iota(jnp.int32, middle.shape, 1)
            rear = jnp.concatenate(
                [jnp.where(lane == 0, middle, rear[:, :128]), rear[:, 128:]], axis=1
            )
        rear = rear.astype(BF16)
        there = slice(slots + c * SLOTS, slots + (c + 1) * SLOTS)
        for p in range(lat_rows):
            cols[p, :width, here] = front[width * p : width * (p + 1)]
            cols[p, :width, there] = rear[width * p : width * (p + 1)]

    together = acts.shape[0]
    span = 512

    def rows_step(g, carry):
        for r in range(together):
            p = g * together + r
            for n in range(0, points, span):
                here = slice(n, n + span)
                columns_here = cols[p, :, here]
                for k in range(0, hid, UNIT):
                    both = dot(weights[2 * k : 2 * k + 2 * UNIT, :], columns_here).astype(BF16)
                    arg = both[:UNIT]
                    th = jnp.tanh(arg)
                    rise = 1 + th
                    act = arg * rise
                    acts[r, k : k + UNIT, here] = act
                    acts[r, hid + k : hid + k + UNIT, here] = both[UNIT:] * (
                        rise + act * (1 - th)
                    )
            grad = dot(w_in[...], acts[r, hid:, :])
            front, rear = grad[:, :slots], grad[:, slots:]
            edge[p] = rear[:, :128].astype(BF16)
            slot = lax.broadcasted_iota(jnp.int32, rear.shape, 1)
            evens[p] = (front + jnp.where(slot == 0, 0.0, rear)).astype(BF16)
            odds[p] = (front - rear).astype(BF16)
            sums[...] += dot_nt(acts[r], cols[p])
        return carry

    lax.fori_loop(0, lat_rows // together, rows_step, 0)

    def joined(ref):
        return ref[...].reshape(chans * lat_rows, ref.shape[2])

    real = dot_nt(table[:waves, :], joined(evens)) + dot_nt(alternate, joined(edge))
    real = real.astype(BF16)
    imag = dot_nt(table[waves:, :], joined(odds)).astype(BF16)
    span = near * chans
    for q in range(near):
        a, b = q * chans, (q + 1) * chans
        piece = jnp.concatenate(
            [real[:, a:b], imag[:, a:b], real[:, span + a : span + b], imag[:, span + a : span + b]],
            axis=1,
        )
        for d in range(ranks):
            out[d, q * own : (q + 1) * own, :] = piece[d * own : (d + 1) * own]
    if not last:
        after[...] = sums[...]
        return
    base = near * own
    turned = sums[...].T
    main = jnp.concatenate([turned[:chans, hid:], turned[chans:width, :hid]], axis=0)
    lanes = 4 * chans
    cuts = range(0, hid, lanes)
    after[...] = turned[width : width + 1, hid:]
    share = width // ranks
    for d in range(ranks):
        rows = [main[d * share : (d + 1) * share, c : c + lanes] for c in cuts]
        rows = jnp.concatenate(rows, axis=0).astype(BF16)
        out[d, base : base + rows.shape[0], :] = rows


def columns(arrived, table, w_in, weights, before, ranks, own, last):
    chans, hid = w_in.shape
    lat_rows = arrived.shape[1] // own
    waves = ranks * own
    slots = table.shape[1]
    points = 2 * slots
    together = 4
    rows_out = lat_rows // 2 * own
    lanes = 4 * chans
    if last:
        rows_out += (hid // lanes) * (2 * chans // ranks)
    sums = (2 * hid, 2 * chans + 16)
    after = (1, hid) if last else sums
    out_specs = [whole(ranks, rows_out, lanes), whole(*after)]
    out_shape = [
        jax.ShapeDtypeStruct((ranks, rows_out, lanes), BF16),
        jax.ShapeDtypeStruct(after, F32),
    ]
    sources = [arrived, table, w_in, weights] + before
    result = pl.pallas_call(
        functools.partial(column_kernel, ranks, own, not before, last),
        grid=(1,),
        in_specs=[HBM] * len(sources),
        out_specs=out_specs,
        out_shape=out_shape,
        scratch_shapes=[
            pltpu.VMEM(arrived.shape, BF16),
            pltpu.VMEM(table.shape, BF16),
            pltpu.VMEM(w_in.shape, BF16),
            pltpu.VMEM(weights.shape, BF16),
            pltpu.VMEM(sums, F32),
            pltpu.VMEM((2 * chans * lat_rows, 2 * waves), BF16),
            pltpu.VMEM((lat_rows, 2 * chans + 16, points), BF16),
            pltpu.VMEM((together, 2 * hid, points), BF16),
            pltpu.VMEM((lat_rows, chans, slots), BF16),
            pltpu.VMEM((lat_rows, chans, slots), BF16),
            pltpu.VMEM((lat_rows, chans, 128), BF16),
            pltpu.SemaphoreType.DMA((4 + slots // SLOTS,)),
        ],
        compiler_params=params(57),
        name="column_physics",
    )(*sources)
    return result[0], list(result[1:])


def backward_kernel(ranks, near, block, ahead, *refs):
    arrived_h, refs = refs[:PARTS], refs[PARTS:]
    cot_h, leg_h, damping_h, out_h = refs[:4]
    arrived, refs = refs[4 : 4 + PARTS], refs[4 + PARTS :]
    cot, leg, damping, out, rows, factor, in_sems, out_sems, sems = refs
    own, width, _ = cot.shape
    size = near * own
    early = copies_of([(damping_h, damping), *zip(arrived_h, arrived)], sems)

    def moves(c):
        here = pl.ds(c * block, block)
        return [
            pltpu.make_async_copy(src.at[here], dst.at[here], in_sems.at[c, k])
            for k, (src, dst) in enumerate(((cot_h, cot), (leg_h, leg)))
        ]

    def leave(c):
        here = pl.ds(c * block, block)
        return pltpu.make_async_copy(out.at[here], out_h.at[here], out_sems.at[c])

    for c in range(min(ahead, own // block)):
        for move in moves(c):
            move.start()
    early[0].wait()
    set_factor(factor, damping)
    for part in range(PARTS):
        early[1 + part].wait()
        for s in range(ranks):
            row = (part * ranks + s) * size
            rows[row : row + size, :] = arrived[part][s, :size, :].astype(F32)

    def step(c, carry):
        for move in moves(c):
            move.wait()

        @pl.when(c + ahead < own // block)
        def _():
            for move in moves(c + ahead):
                move.start()

        group = 2 if block % 2 == 0 else 1
        count = PARTS * ranks * near
        for k in range(0, block, group):
            members = [c * block + k + j for j in range(group)]
            mine = [rows[pl.ds(i, count, stride=own), :].astype(BF16) for i in members]
            mine = jnp.concatenate(mine, axis=0).T
            lhs = []
            for j in range(group):
                here = slice(j * count, (j + 1) * count)
                piece = jnp.concatenate([mine[:width, here], mine[width:, here]], axis=1)
                blank = jnp.zeros_like(piece)
                lhs.append(
                    jnp.concatenate([piece if g == j else blank for g in range(group)], axis=1)
                )
            product = dot_nt(
                jnp.concatenate(lhs, axis=0), jnp.concatenate([leg[i] for i in members], axis=1)
            )
            for j, i in enumerate(members):
                here = slice(j * width, (j + 1) * width)
                out[i] = cot[i].astype(F32) * factor[...] + product[here]
        leave(c).start()
        return carry

    lax.fori_loop(0, own // block, step, 0)
    for c in range(own // block):
        leave(c).wait()


def backward(arrived, cot, legendre, damping, ranks):
    own, width, degrees = cot.shape
    lat = legendre.shape[2]
    near = lat // ranks // 2 // PARTS
    block = block_of(own, 8)
    return pl.pallas_call(
        functools.partial(backward_kernel, ranks, near, block, 2),
        grid=(1,),
        in_specs=[HBM] * (PARTS + 3),
        out_specs=HBM,
        out_shape=jax.ShapeDtypeStruct((own, width, degrees), F32),
        scratch_shapes=[pltpu.VMEM(piece.shape, BF16) for piece in arrived]
        + [
            pltpu.VMEM(cot.shape, BF16),
            pltpu.VMEM(legendre.shape, BF16),
            pltpu.VMEM(damping.shape, F32),
            pltpu.VMEM(cot.shape, F32),
            pltpu.VMEM((PARTS * ranks * near * own, 2 * width), F32),
            pltpu.VMEM((width, degrees), F32),
            pltpu.SemaphoreType.DMA((own // block, 2)),
            pltpu.SemaphoreType.DMA((own // block,)),
            pltpu.SemaphoreType.DMA((PARTS + 1,)),
        ],
        compiler_params=params(57),
        name="legendre_backward",
    )(*arrived, cot, legendre, damping)


def collect_kernel(base, arrived, bias, out):
    lanes = arrived.shape[2]
    total = arrived[0, base:, :].astype(F32)
    for s in range(1, arrived.shape[0]):
        total = total + arrived[s, base:, :].astype(F32)
    cuts = range(0, bias.shape[1], lanes)
    total = jnp.concatenate([total] + [bias[:, c : c + lanes] for c in cuts], axis=0).astype(BF16)
    for s in range(out.shape[0]):
        out[s] = total


def collect(arrived, bias, base, copies):
    lanes = arrived.shape[2]
    shape = (copies, arrived.shape[1] - base + bias.shape[1] // lanes, lanes)
    return pl.pallas_call(
        functools.partial(collect_kernel, base),
        grid=(1,),
        in_specs=[whole(*arrived.shape), whole(*bias.shape)],
        out_specs=whole(*shape),
        out_shape=jax.ShapeDtypeStruct(shape, BF16),
        compiler_params=params(8),
        name="collect_gradients",
    )(arrived, bias)


def finish_kernel(groups, scale, parts, grad_in, grad_bias, grad_out):
    ranks = parts.shape[0] // groups
    chans, hid = grad_in.shape
    lanes = parts.shape[2]
    cuts = hid // lanes
    share = 2 * chans // ranks
    for r in range(ranks):
        total = parts[r].astype(F32)
        for g in range(1, groups):
            total = total + parts[g * ranks + r].astype(F32)
        total = total * scale
        row = r * share
        dest, row = (grad_in, row) if row < chans else (grad_out, row - chans)
        for c in range(cuts):
            dest[row : row + share, c * lanes : (c + 1) * lanes] = total[c * share : (c + 1) * share]
    tail = parts[0, cuts * share :].astype(F32)
    for s in range(1, parts.shape[0]):
        tail = tail + parts[s, cuts * share :].astype(F32)
    for c in range(cuts):
        grad_bias[:, c * lanes : (c + 1) * lanes] = tail[c : c + 1] * scale


def finish(parts, hid, chans, groups, scale):
    return pl.pallas_call(
        functools.partial(finish_kernel, groups, scale),
        grid=(1,),
        in_specs=[whole(*parts.shape)],
        out_specs=(whole(chans, hid), whole(1, hid), whole(chans, hid)),
        out_shape=(
            jax.ShapeDtypeStruct((chans, hid), F32),
            jax.ShapeDtypeStruct((1, hid), F32),
            jax.ShapeDtypeStruct((chans, hid), F32),
        ),
        compiler_params=params(8),
        name="weight_gradients",
    )(parts)


def body(
    spectral_state, cotangent, legendre, quadrature, damping, physics_in, physics_bias, physics_out
):
    spectral = spectral_state[0]
    cot = cotangent[0]
    own, width, degrees = spectral.shape
    chans = width // 2
    hid = physics_in.shape[0]
    ranks = lax.axis_size("lat")
    groups = lax.axis_size("grp")
    lat = legendre.shape[2]
    lat_rows = lat // ranks
    table = jnp.asarray(longitude_table(own * ranks, NLON))
    damping = damping[None, :]
    exchange = functools.partial(
        lax.all_to_all, axis_name="lat", split_axis=0, concat_axis=0, tiled=True
    )

    weights = column_weights(physics_in.T, physics_bias[None, :], physics_out)
    arrived = []
    for part in range(PARTS):
        sent = forward(spectral, cot, legendre, damping, quadrature[None, :], ranks, part)
        if arrived:
            sent, weights, arrived[-1] = lax.optimization_barrier((sent, weights, arrived[-1]))
        arrived.append(exchange(sent))
    sums = []
    returned = []
    for part in range(PARTS):
        back, sums = columns(
            arrived[part],
            table,
            physics_in.T,
            weights,
            sums,
            ranks,
            own,
            part == PARTS - 1,
        )
        if returned:
            back, returned[-1] = lax.optimization_barrier((back, returned[-1]))
        returned.append(exchange(back))

    base = lat_rows // 2 // PARTS * own
    spread = collect(returned[-1], sums[0], base, groups * ranks)
    parts = lax.all_to_all(spread, ("grp", "lat"), split_axis=0, concat_axis=0, tiled=True)
    grad_state = backward(returned, cot, legendre, damping, ranks)
    scale = 1.0 / math.sqrt(groups * lat * NLON)
    grad_in, grad_bias, grad_out = finish(parts, hid, chans, groups, scale)
    return (grad_state[None], grad_in.T, grad_bias[0], grad_out)


def solution(mesh):
    in_specs = (
        P("grp", "lat", None, None),
        P("grp", "lat", None, None),
        P("lat", None, None),
        P(),
        P(),
        P(),
        P(),
        P(),
    )
    out_specs = (P("grp", "lat", None, None), P(), P(), P())
    return jax.shard_map(body, mesh=mesh, in_specs=in_specs, out_specs=out_specs, check_vma=False)
```

```python
import functools
import math

import jax
import jax.numpy as jnp
import numpy as np
import ml_dtypes
from jax import lax
from jax.experimental import pallas as pl
from jax.experimental.pallas import tpu as pltpu
from jax.sharding import PartitionSpec as P

NLON = 2560
MIB = 1024 * 1024
F32 = jnp.float32
BF16 = jnp.bfloat16
PARTS = 2
SLOTS = 256
UNIT = 256
HBM = pl.BlockSpec(memory_space=pl.ANY)


def longitude_table(waves, points):
    slots = points // 2
    phase = np.arange(waves)[:, None] * np.arange(slots)[None, :] % points
    angle = phase * (2.0 * math.pi / points)
    scale = math.sqrt(2.0 / points)
    both = np.concatenate([np.cos(angle) * scale, -np.sin(angle) * scale])
    return both.astype(np.float32).astype(ml_dtypes.bfloat16)


def dot(a, b):
    return jnp.dot(a, b, preferred_element_type=F32)


def dot_nt(a, b):
    return lax.dot_general(a, b, (((1,), (1,)), ((), ())), preferred_element_type=F32)


def params(mib):
    return pltpu.CompilerParams(vmem_limit_bytes=mib * MIB, dimension_semantics=("arbitrary",))


def whole(*shape):
    return pl.BlockSpec(shape, lambda i: (0,) * len(shape))


def block_of(waves, most):
    return max(size for size in range(1, most + 1) if waves % size == 0)


def set_factor(factor, damping):
    width, degrees = factor.shape
    chans = width // 2
    lanes = 128
    spread = jnp.broadcast_to(damping[...], (lanes, chans)).T
    for start in range(0, degrees, lanes):
        degree = (lax.broadcasted_iota(jnp.int32, (chans, lanes), 1) + start).astype(F32)
        ratio = degree * (degree + 1.0) / (degrees * (degrees + 1.0))
        piece = 1.0 / (1.0 + spread * ratio)
        factor[:chans, start : start + lanes] = piece
        factor[chans:, start : start + lanes] = piece


def copies_of(pairs, sems):
    copies = [pltpu.make_async_copy(src, dst, sems.at[k]) for k, (src, dst) in enumerate(pairs)]
    for copy in copies:
        copy.start()
    return copies


def forward_kernel(ranks, block, part, *refs):
    spec_h, cot_h, leg_h, damping, quad, out = refs[:6]
    spec, cot, leg, rows, factor, sems = refs[6:]
    own, width, _ = spec.shape
    chans = width // 2
    lat = leg.shape[2]
    near = lat // ranks // 2 // PARTS
    span = ranks * near

    def moves(c):
        here = pl.ds(c * block, block)
        return [
            pltpu.make_async_copy(src.at[here], dst.at[here], sems.at[c, k])
            for k, (src, dst) in enumerate(((spec_h, spec), (cot_h, cot), (leg_h, leg)))
        ]

    for c in range(own // block):
        for move in moves(c):
            move.start()
    set_factor(factor, damping)

    def step(c, carry):
        for move in moves(c):
            move.wait()
        weight = quad[...]
        for k in range(block):
            i = c * block + k
            tend = (cot[i].astype(F32) * factor[...]).astype(BF16)
            state = spec[i]
            stacked = jnp.concatenate(
                [state[:chans], tend[:chans], state[chans:], tend[chans:]], axis=0
            )
            res = dot(stacked, leg[i])
            res = jnp.concatenate(
                [
                    res[:chans],
                    res[chans : 2 * chans] * weight,
                    res[2 * chans : 3 * chans],
                    res[3 * chans :] * weight,
                ],
                axis=0,
            )
            res = res.astype(BF16).T.astype(F32)
            for side in range(2):
                start = (side * PARTS + part) * span
                rows[pl.ds(side * span * own + i, span, stride=own), :] = res[start : start + span]
        return carry

    lax.fori_loop(0, own // block, step, 0)
    size = near * own
    for d in range(ranks):
        for side in range(2):
            start = (side * ranks + d) * size
            out[d, side * size : (side + 1) * size, :] = rows[start : start + size, :].astype(BF16)


def forward(spectral, cot, legendre, damping, quad, ranks, part):
    own, width, degrees = spectral.shape
    lat = legendre.shape[2]
    block = block_of(own, 8)
    shape = (ranks, lat // ranks // PARTS * own, 2 * width)
    return pl.pallas_call(
        functools.partial(forward_kernel, ranks, block, part),
        grid=(1,),
        in_specs=[HBM] * 3 + [whole(*damping.shape), whole(1, lat)],
        out_specs=whole(*shape),
        out_shape=jax.ShapeDtypeStruct(shape, BF16),
        scratch_shapes=[
            pltpu.VMEM(spectral.shape, BF16),
            pltpu.VMEM(cot.shape, BF16),
            pltpu.VMEM(legendre.shape, BF16),
            pltpu.VMEM((lat // PARTS * own, 2 * width), F32),
            pltpu.VMEM((width, degrees), F32),
            pltpu.SemaphoreType.DMA((own // block, 3)),
        ],
        compiler_params=params(60),
        name="legendre_forward",
    )(spectral, cot, legendre, damping, quad)


def weights_kernel(w_in, bias, w_out, weights):
    chans, hid = w_in.shape
    width = 2 * chans
    half_bias = bias[...] * 0.5
    high = half_bias.astype(BF16).astype(F32)
    left = half_bias - high
    mid = left.astype(BF16).astype(F32)
    low = left - mid
    stack = jnp.concatenate(
        [
            w_in[...].astype(F32) * 0.5,
            w_out[...].astype(F32) * 0.5,
            high,
            mid,
            low,
            jnp.zeros((13, hid), F32),
        ],
        axis=0,
    ).T.astype(BF16)
    lane = lax.broadcasted_iota(jnp.int32, stack.shape, 1)
    is_out = (lane >= chans) & (lane < width)
    nothing = jnp.zeros_like(stack)
    inward = jnp.where(is_out, nothing, stack)
    outward = jnp.where(is_out, stack, nothing)
    for k in range(0, hid, UNIT):
        weights[2 * k : 2 * k + UNIT, :] = inward[k : k + UNIT]
        weights[2 * k + UNIT : 2 * k + 2 * UNIT, :] = outward[k : k + UNIT]


def column_weights(w_in, bias, w_out):
    chans, hid = w_in.shape
    shape = (2 * hid, 2 * chans + 16)
    return pl.pallas_call(
        weights_kernel,
        grid=(1,),
        in_specs=[whole(*w_in.shape), whole(*bias.shape), whole(*w_out.shape)],
        out_specs=whole(*shape),
        out_shape=jax.ShapeDtypeStruct(shape, BF16),
        compiler_params=params(60),
        name="column_weights",
    )(w_in, bias, w_out)


def column_kernel(ranks, own, first, last, *refs):
    given = 4 if first else 5
    sources, out = refs[:given], refs[given]
    refs = refs[given + 1 :]
    after, refs = refs[0], refs[1:]
    arrived, table, w_in, weights, sums = refs[:5]
    fourier, cols, acts, evens, odds, edge, sems = refs[5:]
    chans, hid = w_in.shape
    waves = ranks * own
    lat_rows = arrived.shape[1] // own
    near = lat_rows // 2
    slots = table.shape[1]
    points = 2 * slots
    scale = math.sqrt(2.0 / points)
    width = 2 * chans
    arrived_h, table_h, w_in_h, weights_h = sources[:4]
    pairs = [(arrived_h, arrived), (w_in_h, w_in), (weights_h, weights)]
    if not first:
        pairs.append((sources[4], sums))
    small = copies_of(pairs, sems)
    moves = []
    for c in range(slots // SLOTS):
        here = pl.ds(c * SLOTS, SLOTS)
        moves.append(
            pltpu.make_async_copy(table_h.at[:, here], table.at[:, here], sems.at[4 + c])
        )
        moves[c].start()
    for p in range(lat_rows):
        cols[p, width:, :] = jnp.ones((16, points), BF16)
    for copy in small:
        copy.wait()
    if first:
        sums[...] = jnp.zeros_like(sums)
    for p in range(lat_rows):
        piece = jnp.concatenate(
            [arrived[s, p * own : (p + 1) * own, :] for s in range(ranks)], axis=0
        ).T
        row = width * p
        fourier[row : row + width, :waves] = piece[:width]
        fourier[row : row + width, waves:] = piece[width:]
    wave = lax.broadcasted_iota(jnp.int32, (waves, 128), 0)
    lane = lax.broadcasted_iota(jnp.int32, (waves, 128), 1)
    alternate = jnp.where(lane == 0, jnp.where(wave % 2 == 0, scale, -scale), 0.0).astype(BF16)
    for c, move in enumerate(moves):
        move.wait()
        here = slice(c * SLOTS, (c + 1) * SLOTS)
        even = dot(fourier[:, :waves], table[:waves, here])
        odd = dot(fourier[:, waves:], table[waves:, here])
        front = (even + odd).astype(BF16)
        rear = even - odd
        if c == 0:
            middle = dot(fourier[:, :waves], alternate)
            lane = lax.broadcasted_iota(jnp.int32, middle.shape, 1)
            rear = jnp.concatenate(
                [jnp.where(lane == 0, middle, rear[:, :128]), rear[:, 128:]], axis=1
            )
        rear = rear.astype(BF16)
        there = slice(slots + c * SLOTS, slots + (c + 1) * SLOTS)
        for p in range(lat_rows):
            cols[p, :width, here] = front[width * p : width * (p + 1)]
            cols[p, :width, there] = rear[width * p : width * (p + 1)]

    steps = [(p, n) for p in range(lat_rows) for n in range(2)]
    front = None
    for at in range(len(steps) + 1):
        for k in range(0, hid, UNIT):
            if at < len(steps):
                p, n = steps[at]
                here = slice(n * slots, (n + 1) * slots)
                both = dot(weights[2 * k : 2 * k + 2 * UNIT, :], cols[p, :, here]).astype(BF16)
                arg = both[:UNIT]
                th = jnp.tanh(arg)
                rise = 1 + th
                act = arg * rise
                acts[p, k : k + UNIT, here] = act
                acts[p, hid + k : hid + k + UNIT, here] = both[UNIT:] * (rise + act * (1 - th))
            if at > 0:
                p, n = steps[at - 1]
                here = slice(n * slots, (n + 1) * slots)
                some = slice(2 * k, 2 * k + 2 * UNIT)
                sums[some, :] += dot_nt(acts[p, some, here], cols[p, :, here])
        if at > 0:
            grad = dot(w_in[...], acts[p, hid:, here])
            if n == 0:
                front = grad
            else:
                edge[p] = grad[:, :128].astype(BF16)
                slot = lax.broadcasted_iota(jnp.int32, grad.shape, 1)
                evens[p] = (front + jnp.where(slot == 0, 0.0, grad)).astype(BF16)
                odds[p] = (front - grad).astype(BF16)

    def joined(ref):
        return ref[...].reshape(chans * lat_rows, ref.shape[2])

    real = dot_nt(table[:waves, :], joined(evens)) + dot_nt(alternate, joined(edge))
    real = real.astype(BF16)
    imag = dot_nt(table[waves:, :], joined(odds)).astype(BF16)
    span = near * chans
    for q in range(near):
        a, b = q * chans, (q + 1) * chans
        piece = jnp.concatenate(
            [real[:, a:b], imag[:, a:b], real[:, span + a : span + b], imag[:, span + a : span + b]],
            axis=1,
        )
        for d in range(ranks):
            out[d, q * own : (q + 1) * own, :] = piece[d * own : (d + 1) * own]
    if not last:
        after[...] = sums[...]
        return
    base = near * own
    turned = sums[...].T
    main = jnp.concatenate([turned[:chans, hid:], turned[chans:width, :hid]], axis=0)
    lanes = 4 * chans
    cuts = range(0, hid, lanes)
    after[...] = turned[width : width + 1, hid:]
    share = width // ranks
    for d in range(ranks):
        rows = [main[d * share : (d + 1) * share, c : c + lanes] for c in cuts]
        rows = jnp.concatenate(rows, axis=0).astype(BF16)
        out[d, base : base + rows.shape[0], :] = rows


def columns(arrived, table, w_in, weights, before, ranks, own, last):
    chans, hid = w_in.shape
    lat_rows = arrived.shape[1] // own
    waves = ranks * own
    slots = table.shape[1]
    points = 2 * slots
    rows_out = lat_rows // 2 * own
    lanes = 4 * chans
    if last:
        rows_out += (hid // lanes) * (2 * chans // ranks)
    sums = (2 * hid, 2 * chans + 16)
    after = (1, hid) if last else sums
    out_specs = [whole(ranks, rows_out, lanes), whole(*after)]
    out_shape = [
        jax.ShapeDtypeStruct((ranks, rows_out, lanes), BF16),
        jax.ShapeDtypeStruct(after, F32),
    ]
    sources = [arrived, table, w_in, weights] + before
    result = pl.pallas_call(
        functools.partial(column_kernel, ranks, own, not before, last),
        grid=(1,),
        in_specs=[HBM] * len(sources),
        out_specs=out_specs,
        out_shape=out_shape,
        scratch_shapes=[
            pltpu.VMEM(arrived.shape, BF16),
            pltpu.VMEM(table.shape, BF16),
            pltpu.VMEM(w_in.shape, BF16),
            pltpu.VMEM(weights.shape, BF16),
            pltpu.VMEM(sums, F32),
            pltpu.VMEM((2 * chans * lat_rows, 2 * waves), BF16),
            pltpu.VMEM((lat_rows, 2 * chans + 16, points), BF16),
            pltpu.VMEM((lat_rows, 2 * hid, points), BF16),
            pltpu.VMEM((lat_rows, chans, slots), BF16),
            pltpu.VMEM((lat_rows, chans, slots), BF16),
            pltpu.VMEM((lat_rows, chans, 128), BF16),
            pltpu.SemaphoreType.DMA((4 + slots // SLOTS,)),
        ],
        compiler_params=params(57),
        name="column_physics",
    )(*sources)
    return result[0], list(result[1:])


def backward_kernel(ranks, near, block, ahead, *refs):
    arrived_h, refs = refs[:PARTS], refs[PARTS:]
    cot_h, leg_h, damping_h, out_h = refs[:4]
    arrived, refs = refs[4 : 4 + PARTS], refs[4 + PARTS :]
    cot, leg, damping, out, rows, factor, in_sems, out_sems, sems = refs
    own, width, _ = cot.shape
    size = near * own
    early = copies_of([(damping_h, damping), *zip(arrived_h, arrived)], sems)

    def moves(c):
        here = pl.ds(c * block, block)
        return [
            pltpu.make_async_copy(src.at[here], dst.at[here], in_sems.at[c, k])
            for k, (src, dst) in enumerate(((cot_h, cot), (leg_h, leg)))
        ]

    def leave(c):
        here = pl.ds(c * block, block)
        return pltpu.make_async_copy(out.at[here], out_h.at[here], out_sems.at[c])

    for c in range(min(ahead, own // block)):
        for move in moves(c):
            move.start()
    early[0].wait()
    set_factor(factor, damping)
    for part in range(PARTS):
        early[1 + part].wait()
        for s in range(ranks):
            row = (part * ranks + s) * size
            rows[row : row + size, :] = arrived[part][s, :size, :].astype(F32)

    def step(c, carry):
        for move in moves(c):
            move.wait()

        @pl.when(c + ahead < own // block)
        def _():
            for move in moves(c + ahead):
                move.start()

        group = 2 if block % 2 == 0 else 1
        count = PARTS * ranks * near
        for k in range(0, block, group):
            members = [c * block + k + j for j in range(group)]
            mine = [rows[pl.ds(i, count, stride=own), :].astype(BF16) for i in members]
            mine = jnp.concatenate(mine, axis=0).T
            lhs = []
            for j in range(group):
                here = slice(j * count, (j + 1) * count)
                piece = jnp.concatenate([mine[:width, here], mine[width:, here]], axis=1)
                blank = jnp.zeros_like(piece)
                lhs.append(
                    jnp.concatenate([piece if g == j else blank for g in range(group)], axis=1)
                )
            product = dot_nt(
                jnp.concatenate(lhs, axis=0), jnp.concatenate([leg[i] for i in members], axis=1)
            )
            for j, i in enumerate(members):
                here = slice(j * width, (j + 1) * width)
                out[i] = cot[i].astype(F32) * factor[...] + product[here]
        leave(c).start()
        return carry

    lax.fori_loop(0, own // block, step, 0)
    for c in range(own // block):
        leave(c).wait()


def backward(arrived, cot, legendre, damping, ranks):
    own, width, degrees = cot.shape
    lat = legendre.shape[2]
    near = lat // ranks // 2 // PARTS
    block = block_of(own, 8)
    return pl.pallas_call(
        functools.partial(backward_kernel, ranks, near, block, 2),
        grid=(1,),
        in_specs=[HBM] * (PARTS + 3),
        out_specs=HBM,
        out_shape=jax.ShapeDtypeStruct((own, width, degrees), F32),
        scratch_shapes=[pltpu.VMEM(piece.shape, BF16) for piece in arrived]
        + [
            pltpu.VMEM(cot.shape, BF16),
            pltpu.VMEM(legendre.shape, BF16),
            pltpu.VMEM(damping.shape, F32),
            pltpu.VMEM(cot.shape, F32),
            pltpu.VMEM((PARTS * ranks * near * own, 2 * width), F32),
            pltpu.VMEM((width, degrees), F32),
            pltpu.SemaphoreType.DMA((own // block, 2)),
            pltpu.SemaphoreType.DMA((own // block,)),
            pltpu.SemaphoreType.DMA((PARTS + 1,)),
        ],
        compiler_params=params(57),
        name="legendre_backward",
    )(*arrived, cot, legendre, damping)


def collect_kernel(base, arrived, bias, out):
    lanes = arrived.shape[2]
    total = arrived[0, base:, :].astype(F32)
    for s in range(1, arrived.shape[0]):
        total = total + arrived[s, base:, :].astype(F32)
    cuts = range(0, bias.shape[1], lanes)
    total = jnp.concatenate([total] + [bias[:, c : c + lanes] for c in cuts], axis=0).astype(BF16)
    for s in range(out.shape[0]):
        out[s] = total


def collect(arrived, bias, base, copies):
    lanes = arrived.shape[2]
    shape = (copies, arrived.shape[1] - base + bias.shape[1] // lanes, lanes)
    return pl.pallas_call(
        functools.partial(collect_kernel, base),
        grid=(1,),
        in_specs=[whole(*arrived.shape), whole(*bias.shape)],
        out_specs=whole(*shape),
        out_shape=jax.ShapeDtypeStruct(shape, BF16),
        compiler_params=params(8),
        name="collect_gradients",
    )(arrived, bias)


def finish_kernel(groups, scale, parts, grad_in, grad_bias, grad_out):
    ranks = parts.shape[0] // groups
    chans, hid = grad_in.shape
    lanes = parts.shape[2]
    cuts = hid // lanes
    share = 2 * chans // ranks
    for r in range(ranks):
        total = parts[r].astype(F32)
        for g in range(1, groups):
            total = total + parts[g * ranks + r].astype(F32)
        total = total * scale
        row = r * share
        dest, row = (grad_in, row) if row < chans else (grad_out, row - chans)
        for c in range(cuts):
            dest[row : row + share, c * lanes : (c + 1) * lanes] = total[c * share : (c + 1) * share]
    tail = parts[0, cuts * share :].astype(F32)
    for s in range(1, parts.shape[0]):
        tail = tail + parts[s, cuts * share :].astype(F32)
    for c in range(cuts):
        grad_bias[:, c * lanes : (c + 1) * lanes] = tail[c : c + 1] * scale


def finish(parts, hid, chans, groups, scale):
    return pl.pallas_call(
        functools.partial(finish_kernel, groups, scale),
        grid=(1,),
        in_specs=[whole(*parts.shape)],
        out_specs=(whole(chans, hid), whole(1, hid), whole(chans, hid)),
        out_shape=(
            jax.ShapeDtypeStruct((chans, hid), F32),
            jax.ShapeDtypeStruct((1, hid), F32),
            jax.ShapeDtypeStruct((chans, hid), F32),
        ),
        compiler_params=params(8),
        name="weight_gradients",
    )(parts)


def body(
    spectral_state, cotangent, legendre, quadrature, damping, physics_in, physics_bias, physics_out
):
    spectral = spectral_state[0]
    cot = cotangent[0]
    own, width, degrees = spectral.shape
    chans = width // 2
    hid = physics_in.shape[0]
    ranks = lax.axis_size("lat")
    groups = lax.axis_size("grp")
    lat = legendre.shape[2]
    lat_rows = lat // ranks
    table = jnp.asarray(longitude_table(own * ranks, NLON))
    damping = damping[None, :]
    exchange = functools.partial(
        lax.all_to_all, axis_name="lat", split_axis=0, concat_axis=0, tiled=True
    )

    weights = column_weights(physics_in.T, physics_bias[None, :], physics_out)
    arrived = []
    for part in range(PARTS):
        sent = forward(spectral, cot, legendre, damping, quadrature[None, :], ranks, part)
        if arrived:
            sent, weights, arrived[-1] = lax.optimization_barrier((sent, weights, arrived[-1]))
        arrived.append(exchange(sent))
    sums = []
    returned = []
    for part in range(PARTS):
        back, sums = columns(
            arrived[part],
            table,
            physics_in.T,
            weights,
            sums,
            ranks,
            own,
            part == PARTS - 1,
        )
        if returned:
            back, returned[-1] = lax.optimization_barrier((back, returned[-1]))
        returned.append(exchange(back))

    base = lat_rows // 2 // PARTS * own
    spread = collect(returned[-1], sums[0], base, groups * ranks)
    parts = lax.all_to_all(spread, ("grp", "lat"), split_axis=0, concat_axis=0, tiled=True)
    grad_state = backward(returned, cot, legendre, damping, ranks)
    scale = 1.0 / math.sqrt(groups * lat * NLON)
    grad_in, grad_bias, grad_out = finish(parts, hid, chans, groups, scale)
    return (grad_state[None], grad_in.T, grad_bias[0], grad_out)


def solution(mesh):
    in_specs = (
        P("grp", "lat", None, None),
        P("grp", "lat", None, None),
        P("lat", None, None),
        P(),
        P(),
        P(),
        P(),
        P(),
    )
    out_specs = (P("grp", "lat", None, None), P(), P(), P())
    return jax.shard_map(body, mesh=mesh, in_specs=in_specs, out_specs=out_specs, check_vma=False)
```

```python
import functools
import math

import jax
import jax.numpy as jnp
import numpy as np
import ml_dtypes
from jax import lax
from jax.experimental import pallas as pl
from jax.experimental.pallas import tpu as pltpu
from jax.sharding import PartitionSpec as P

NLON = 2560
MIB = 1024 * 1024
F32 = jnp.float32
BF16 = jnp.bfloat16
PARTS = 2
SLOTS = 256
UNIT = 128
HBM = pl.BlockSpec(memory_space=pl.ANY)


def longitude_table(waves, points):
    slots = points // 2
    phase = np.arange(waves)[:, None] * np.arange(slots)[None, :] % points
    angle = phase * (2.0 * math.pi / points)
    scale = math.sqrt(2.0 / points)
    both = np.concatenate([np.cos(angle) * scale, -np.sin(angle) * scale])
    return both.astype(np.float32).astype(ml_dtypes.bfloat16)


def dot(a, b):
    return jnp.dot(a, b, preferred_element_type=F32)


def dot_nt(a, b):
    return lax.dot_general(a, b, (((1,), (1,)), ((), ())), preferred_element_type=F32)


def params(mib):
    return pltpu.CompilerParams(vmem_limit_bytes=mib * MIB, dimension_semantics=("arbitrary",))


def whole(*shape):
    return pl.BlockSpec(shape, lambda i: (0,) * len(shape))


def block_of(waves, most):
    return max(size for size in range(1, most + 1) if waves % size == 0)


def set_factor(factor, damping):
    width, degrees = factor.shape
    chans = width // 2
    lanes = 128
    spread = jnp.broadcast_to(damping[...], (lanes, chans)).T
    for start in range(0, degrees, lanes):
        degree = (lax.broadcasted_iota(jnp.int32, (chans, lanes), 1) + start).astype(F32)
        ratio = degree * (degree + 1.0) / (degrees * (degrees + 1.0))
        piece = 1.0 / (1.0 + spread * ratio)
        factor[:chans, start : start + lanes] = piece
        factor[chans:, start : start + lanes] = piece


def copies_of(pairs, sems):
    copies = [pltpu.make_async_copy(src, dst, sems.at[k]) for k, (src, dst) in enumerate(pairs)]
    for copy in copies:
        copy.start()
    return copies


def forward_kernel(ranks, block, part, *refs):
    spec_h, cot_h, leg_h, damping, quad, out = refs[:6]
    spec, cot, leg, rows, factor, sems = refs[6:]
    own, width, _ = spec.shape
    chans = width // 2
    lat = leg.shape[2]
    near = lat // ranks // 2 // PARTS
    span = ranks * near

    def moves(c):
        here = pl.ds(c * block, block)
        return [
            pltpu.make_async_copy(src.at[here], dst.at[here], sems.at[c, k])
            for k, (src, dst) in enumerate(((spec_h, spec), (cot_h, cot), (leg_h, leg)))
        ]

    for c in range(own // block):
        for move in moves(c):
            move.start()
    set_factor(factor, damping)

    def step(c, carry):
        for move in moves(c):
            move.wait()
        weight = quad[...]
        for k in range(block):
            i = c * block + k
            tend = (cot[i].astype(F32) * factor[...]).astype(BF16)
            state = spec[i]
            stacked = jnp.concatenate(
                [state[:chans], tend[:chans], state[chans:], tend[chans:]], axis=0
            )
            res = dot(stacked, leg[i])
            res = jnp.concatenate(
                [
                    res[:chans],
                    res[chans : 2 * chans] * weight,
                    res[2 * chans : 3 * chans],
                    res[3 * chans :] * weight,
                ],
                axis=0,
            )
            res = res.astype(BF16).T.astype(F32)
            for side in range(2):
                start = (side * PARTS + part) * span
                rows[pl.ds(side * span * own + i, span, stride=own), :] = res[start : start + span]
        return carry

    lax.fori_loop(0, own // block, step, 0)
    size = near * own
    for d in range(ranks):
        for side in range(2):
            start = (side * ranks + d) * size
            out[d, side * size : (side + 1) * size, :] = rows[start : start + size, :].astype(BF16)


def forward(spectral, cot, legendre, damping, quad, ranks, part):
    own, width, degrees = spectral.shape
    lat = legendre.shape[2]
    block = block_of(own, 8)
    shape = (ranks, lat // ranks // PARTS * own, 2 * width)
    return pl.pallas_call(
        functools.partial(forward_kernel, ranks, block, part),
        grid=(1,),
        in_specs=[HBM] * 3 + [whole(*damping.shape), whole(1, lat)],
        out_specs=whole(*shape),
        out_shape=jax.ShapeDtypeStruct(shape, BF16),
        scratch_shapes=[
            pltpu.VMEM(spectral.shape, BF16),
            pltpu.VMEM(cot.shape, BF16),
            pltpu.VMEM(legendre.shape, BF16),
            pltpu.VMEM(((lat // PARTS + 1) * own, 2 * width), F32),
            pltpu.VMEM((width, degrees), F32),
            pltpu.SemaphoreType.DMA((own // block, 3)),
        ],
        compiler_params=params(60),
        name="legendre_forward",
    )(spectral, cot, legendre, damping, quad)


def weights_kernel(w_in, bias, w_out, weights):
    chans, hid = w_in.shape
    width = 2 * chans
    half_bias = bias[...] * 0.5
    high = half_bias.astype(BF16).astype(F32)
    left = half_bias - high
    mid = left.astype(BF16).astype(F32)
    low = left - mid
    stack = jnp.concatenate(
        [
            w_in[...].astype(F32) * 0.5,
            w_out[...].astype(F32) * 0.5,
            high,
            mid,
            low,
            jnp.zeros((13, hid), F32),
        ],
        axis=0,
    ).T.astype(BF16)
    lane = lax.broadcasted_iota(jnp.int32, stack.shape, 1)
    is_out = (lane >= chans) & (lane < width)
    nothing = jnp.zeros_like(stack)
    inward = jnp.where(is_out, nothing, stack)
    outward = jnp.where(is_out, stack, nothing)
    for k in range(0, hid, UNIT):
        weights[2 * k : 2 * k + UNIT, :] = inward[k : k + UNIT]
        weights[2 * k + UNIT : 2 * k + 2 * UNIT, :] = outward[k : k + UNIT]


def column_weights(w_in, bias, w_out):
    chans, hid = w_in.shape
    shape = (2 * hid, 2 * chans + 16)
    return pl.pallas_call(
        weights_kernel,
        grid=(1,),
        in_specs=[whole(*w_in.shape), whole(*bias.shape), whole(*w_out.shape)],
        out_specs=whole(*shape),
        out_shape=jax.ShapeDtypeStruct(shape, BF16),
        compiler_params=params(60),
        name="column_weights",
    )(w_in, bias, w_out)


def column_kernel(ranks, own, first, last, *refs):
    given = 4 if first else 5
    sources, out = refs[:given], refs[given]
    refs = refs[given + 1 :]
    after, refs = refs[0], refs[1:]
    arrived, table, w_in, weights, sums = refs[:5]
    fourier, cols, acts, evens, odds, edge, sems = refs[5:]
    chans, hid = w_in.shape
    waves = ranks * own
    lat_rows = arrived.shape[1] // own
    near = lat_rows // 2
    slots = table.shape[1]
    points = 2 * slots
    scale = math.sqrt(2.0 / points)
    width = 2 * chans
    arrived_h, table_h, w_in_h, weights_h = sources[:4]
    pairs = [(arrived_h, arrived), (w_in_h, w_in), (weights_h, weights)]
    if not first:
        pairs.append((sources[4], sums))
    small = copies_of(pairs, sems)
    moves = []
    for c in range(slots // SLOTS):
        here = pl.ds(c * SLOTS, SLOTS)
        moves.append(
            pltpu.make_async_copy(table_h.at[:, here], table.at[:, here], sems.at[4 + c])
        )
        moves[c].start()
    for p in range(lat_rows):
        cols[p, width:, :] = jnp.ones((16, points), BF16)
    for copy in small:
        copy.wait()
    if first:
        sums[...] = jnp.zeros_like(sums)
    for p in range(lat_rows):
        piece = jnp.concatenate(
            [arrived[s, p * own : (p + 1) * own, :] for s in range(ranks)], axis=0
        ).T
        row = width * p
        fourier[row : row + width, :waves] = piece[:width]
        fourier[row : row + width, waves:] = piece[width:]
    wave = lax.broadcasted_iota(jnp.int32, (waves, 128), 0)
    lane = lax.broadcasted_iota(jnp.int32, (waves, 128), 1)
    alternate = jnp.where(lane == 0, jnp.where(wave % 2 == 0, scale, -scale), 0.0).astype(BF16)
    for c, move in enumerate(moves):
        move.wait()
        here = slice(c * SLOTS, (c + 1) * SLOTS)
        even = dot(fourier[:, :waves], table[:waves, here])
        odd = dot(fourier[:, waves:], table[waves:, here])
        front = (even + odd).astype(BF16)
        rear = even - odd
        if c == 0:
            middle = dot(fourier[:, :waves], alternate)
            lane = lax.broadcasted_iota(jnp.int32, middle.shape, 1)
            rear = jnp.concatenate(
                [jnp.where(lane == 0, middle, rear[:, :128]), rear[:, 128:]], axis=1
            )
        rear = rear.astype(BF16)
        there = slice(slots + c * SLOTS, slots + (c + 1) * SLOTS)
        for p in range(lat_rows):
            cols[p, :width, here] = front[width * p : width * (p + 1)]
            cols[p, :width, there] = rear[width * p : width * (p + 1)]

    together = acts.shape[0]
    span = 512

    def rows_step(g, carry):
        for r in range(together):
            p = g * together + r
            for n in range(0, points, span):
                here = slice(n, n + span)
                columns_here = cols[p, :, here]
                for k in range(0, hid, UNIT):
                    both = dot(weights[2 * k : 2 * k + 2 * UNIT, :], columns_here).astype(BF16)
                    arg = both[:UNIT]
                    th = jnp.tanh(arg)
                    rise = 1 + th
                    act = arg * rise
                    acts[r, k : k + UNIT, here] = act
                    acts[r, hid + k : hid + k + UNIT, here] = both[UNIT:] * (
                        rise + act * (1 - th)
                    )
            grad = dot(w_in[...], acts[r, hid:, :])
            front, rear = grad[:, :slots], grad[:, slots:]
            edge[p] = rear[:, :128].astype(BF16)
            slot = lax.broadcasted_iota(jnp.int32, rear.shape, 1)
            evens[p] = (front + jnp.where(slot == 0, 0.0, rear)).astype(BF16)
            odds[p] = (front - rear).astype(BF16)
            sums[...] += dot_nt(acts[r], cols[p])
        return carry

    lax.fori_loop(0, lat_rows // together, rows_step, 0)

    def joined(ref):
        return ref[...].reshape(chans * lat_rows, ref.shape[2])

    real = dot_nt(table[:waves, :], joined(evens)) + dot_nt(alternate, joined(edge))
    real = real.astype(BF16)
    imag = dot_nt(table[waves:, :], joined(odds)).astype(BF16)
    span = near * chans
    for q in range(near):
        a, b = q * chans, (q + 1) * chans
        piece = jnp.concatenate(
            [real[:, a:b], imag[:, a:b], real[:, span + a : span + b], imag[:, span + a : span + b]],
            axis=1,
        )
        for d in range(ranks):
            out[d, q * own : (q + 1) * own, :] = piece[d * own : (d + 1) * own]
    if not last:
        after[...] = sums[...]
        return
    base = near * own
    turned = sums[...].T
    main = jnp.concatenate([turned[:chans, hid:], turned[chans:width, :hid]], axis=0)
    lanes = 4 * chans
    cuts = range(0, hid, lanes)
    after[...] = turned[width : width + 1, hid:]
    share = width // ranks
    for d in range(ranks):
        rows = [main[d * share : (d + 1) * share, c : c + lanes] for c in cuts]
        rows = jnp.concatenate(rows, axis=0).astype(BF16)
        out[d, base : base + rows.shape[0], :] = rows


def columns(arrived, table, w_in, weights, before, ranks, own, last):
    chans, hid = w_in.shape
    lat_rows = arrived.shape[1] // own
    waves = ranks * own
    slots = table.shape[1]
    points = 2 * slots
    together = 4
    rows_out = lat_rows // 2 * own
    lanes = 4 * chans
    if last:
        rows_out += (hid // lanes) * (2 * chans // ranks)
    sums = (2 * hid, 2 * chans + 16)
    after = (1, hid) if last else sums
    out_specs = [whole(ranks, rows_out, lanes), whole(*after)]
    out_shape = [
        jax.ShapeDtypeStruct((ranks, rows_out, lanes), BF16),
        jax.ShapeDtypeStruct(after, F32),
    ]
    sources = [arrived, table, w_in, weights] + before
    result = pl.pallas_call(
        functools.partial(column_kernel, ranks, own, not before, last),
        grid=(1,),
        in_specs=[HBM] * len(sources),
        out_specs=out_specs,
        out_shape=out_shape,
        scratch_shapes=[
            pltpu.VMEM(arrived.shape, BF16),
            pltpu.VMEM(table.shape, BF16),
            pltpu.VMEM(w_in.shape, BF16),
            pltpu.VMEM(weights.shape, BF16),
            pltpu.VMEM(sums, F32),
            pltpu.VMEM((2 * chans * lat_rows, 2 * waves), BF16),
            pltpu.VMEM((lat_rows, 2 * chans + 16, points), BF16),
            pltpu.VMEM((together, 2 * hid, points), BF16),
            pltpu.VMEM((lat_rows, chans, slots), BF16),
            pltpu.VMEM((lat_rows, chans, slots), BF16),
            pltpu.VMEM((lat_rows, chans, 128), BF16),
            pltpu.SemaphoreType.DMA((4 + slots // SLOTS,)),
        ],
        compiler_params=params(57),
        name="column_physics",
    )(*sources)
    return result[0], list(result[1:])


def backward_kernel(ranks, near, block, ahead, *refs):
    arrived_h, refs = refs[:PARTS], refs[PARTS:]
    cot_h, leg_h, damping_h, out_h = refs[:4]
    arrived, refs = refs[4 : 4 + PARTS], refs[4 + PARTS :]
    cot, leg, damping, out, rows, factor, in_sems, out_sems, sems = refs
    own, width, _ = cot.shape
    size = near * own
    early = copies_of([(damping_h, damping), *zip(arrived_h, arrived)], sems)

    def moves(c):
        here = pl.ds(c * block, block)
        return [
            pltpu.make_async_copy(src.at[here], dst.at[here], in_sems.at[c, k])
            for k, (src, dst) in enumerate(((cot_h, cot), (leg_h, leg)))
        ]

    def leave(c):
        here = pl.ds(c * block, block)
        return pltpu.make_async_copy(out.at[here], out_h.at[here], out_sems.at[c])

    for c in range(min(ahead, own // block)):
        for move in moves(c):
            move.start()
    early[0].wait()
    set_factor(factor, damping)
    for part in range(PARTS):
        early[1 + part].wait()
        for s in range(ranks):
            row = (part * ranks + s) * size
            rows[row : row + size, :] = arrived[part][s, :size, :].astype(F32)

    def step(c, carry):
        for move in moves(c):
            move.wait()

        @pl.when(c + ahead < own // block)
        def _():
            for move in moves(c + ahead):
                move.start()

        group = 2 if block % 2 == 0 else 1
        count = PARTS * ranks * near
        for k in range(0, block, group):
            members = [c * block + k + j for j in range(group)]
            mine = [rows[pl.ds(i, count, stride=own), :].astype(BF16) for i in members]
            mine = jnp.concatenate(mine, axis=0).T
            lhs = []
            for j in range(group):
                here = slice(j * count, (j + 1) * count)
                piece = jnp.concatenate([mine[:width, here], mine[width:, here]], axis=1)
                blank = jnp.zeros_like(piece)
                lhs.append(
                    jnp.concatenate([piece if g == j else blank for g in range(group)], axis=1)
                )
            product = dot_nt(
                jnp.concatenate(lhs, axis=0), jnp.concatenate([leg[i] for i in members], axis=1)
            )
            for j, i in enumerate(members):
                here = slice(j * width, (j + 1) * width)
                out[i] = cot[i].astype(F32) * factor[...] + product[here]
        leave(c).start()
        return carry

    lax.fori_loop(0, own // block, step, 0)
    for c in range(own // block):
        leave(c).wait()


def backward(arrived, cot, legendre, damping, ranks):
    own, width, degrees = cot.shape
    lat = legendre.shape[2]
    near = lat // ranks // 2 // PARTS
    block = block_of(own, 8)
    return pl.pallas_call(
        functools.partial(backward_kernel, ranks, near, block, 2),
        grid=(1,),
        in_specs=[HBM] * (PARTS + 3),
        out_specs=HBM,
        out_shape=jax.ShapeDtypeStruct((own, width, degrees), F32),
        scratch_shapes=[pltpu.VMEM(piece.shape, BF16) for piece in arrived]
        + [
            pltpu.VMEM(cot.shape, BF16),
            pltpu.VMEM(legendre.shape, BF16),
            pltpu.VMEM(damping.shape, F32),
            pltpu.VMEM(cot.shape, F32),
            pltpu.VMEM(((PARTS * ranks * near + 1) * own, 2 * width), F32),
            pltpu.VMEM((width, degrees), F32),
            pltpu.SemaphoreType.DMA((own // block, 2)),
            pltpu.SemaphoreType.DMA((own // block,)),
            pltpu.SemaphoreType.DMA((PARTS + 1,)),
        ],
        compiler_params=params(57),
        name="legendre_backward",
    )(*arrived, cot, legendre, damping)


def collect_kernel(base, arrived, bias, out):
    lanes = arrived.shape[2]
    total = arrived[0, base:, :].astype(F32)
    for s in range(1, arrived.shape[0]):
        total = total + arrived[s, base:, :].astype(F32)
    cuts = range(0, bias.shape[1], lanes)
    total = jnp.concatenate([total] + [bias[:, c : c + lanes] for c in cuts], axis=0).astype(BF16)
    for s in range(out.shape[0]):
        out[s] = total


def collect(arrived, bias, base, copies):
    lanes = arrived.shape[2]
    shape = (copies, arrived.shape[1] - base + bias.shape[1] // lanes, lanes)
    return pl.pallas_call(
        functools.partial(collect_kernel, base),
        grid=(1,),
        in_specs=[whole(*arrived.shape), whole(*bias.shape)],
        out_specs=whole(*shape),
        out_shape=jax.ShapeDtypeStruct(shape, BF16),
        compiler_params=params(8),
        name="collect_gradients",
    )(arrived, bias)


def finish_kernel(groups, scale, parts, grad_in, grad_bias, grad_out):
    ranks = parts.shape[0] // groups
    chans, hid = grad_in.shape
    lanes = parts.shape[2]
    cuts = hid // lanes
    share = 2 * chans // ranks
    for r in range(ranks):
        total = parts[r].astype(F32)
        for g in range(1, groups):
            total = total + parts[g * ranks + r].astype(F32)
        total = total * scale
        row = r * share
        dest, row = (grad_in, row) if row < chans else (grad_out, row - chans)
        for c in range(cuts):
            dest[row : row + share, c * lanes : (c + 1) * lanes] = total[c * share : (c + 1) * share]
    tail = parts[0, cuts * share :].astype(F32)
    for s in range(1, parts.shape[0]):
        tail = tail + parts[s, cuts * share :].astype(F32)
    for c in range(cuts):
        grad_bias[:, c * lanes : (c + 1) * lanes] = tail[c : c + 1] * scale


def finish(parts, hid, chans, groups, scale):
    return pl.pallas_call(
        functools.partial(finish_kernel, groups, scale),
        grid=(1,),
        in_specs=[whole(*parts.shape)],
        out_specs=(whole(chans, hid), whole(1, hid), whole(chans, hid)),
        out_shape=(
            jax.ShapeDtypeStruct((chans, hid), F32),
            jax.ShapeDtypeStruct((1, hid), F32),
            jax.ShapeDtypeStruct((chans, hid), F32),
        ),
        compiler_params=params(8),
        name="weight_gradients",
    )(parts)


def body(
    spectral_state, cotangent, legendre, quadrature, damping, physics_in, physics_bias, physics_out
):
    spectral = spectral_state[0]
    cot = cotangent[0]
    own, width, degrees = spectral.shape
    chans = width // 2
    hid = physics_in.shape[0]
    ranks = lax.axis_size("lat")
    groups = lax.axis_size("grp")
    lat = legendre.shape[2]
    lat_rows = lat // ranks
    table = jnp.asarray(longitude_table(own * ranks, NLON))
    damping = damping[None, :]
    exchange = functools.partial(
        lax.all_to_all, axis_name="lat", split_axis=0, concat_axis=0, tiled=True
    )

    weights = column_weights(physics_in.T, physics_bias[None, :], physics_out)
    arrived = []
    for part in range(PARTS):
        sent = forward(spectral, cot, legendre, damping, quadrature[None, :], ranks, part)
        if arrived:
            sent, weights, arrived[-1] = lax.optimization_barrier((sent, weights, arrived[-1]))
        arrived.append(exchange(sent))
    sums = []
    returned = []
    for part in range(PARTS):
        back, sums = columns(
            arrived[part],
            table,
            physics_in.T,
            weights,
            sums,
            ranks,
            own,
            part == PARTS - 1,
        )
        if returned:
            back, returned[-1] = lax.optimization_barrier((back, returned[-1]))
        returned.append(exchange(back))

    base = lat_rows // 2 // PARTS * own
    spread = collect(returned[-1], sums[0], base, groups * ranks)
    parts = lax.all_to_all(spread, ("grp", "lat"), split_axis=0, concat_axis=0, tiled=True)
    grad_state = backward(returned, cot, legendre, damping, ranks)
    scale = 1.0 / math.sqrt(groups * lat * NLON)
    grad_in, grad_bias, grad_out = finish(parts, hid, chans, groups, scale)
    return (grad_state[None], grad_in.T, grad_bias[0], grad_out)


def solution(mesh):
    in_specs = (
        P("grp", "lat", None, None),
        P("grp", "lat", None, None),
        P("lat", None, None),
        P(),
        P(),
        P(),
        P(),
        P(),
    )
    out_specs = (P("grp", "lat", None, None), P(), P(), P())
    return jax.shard_map(body, mesh=mesh, in_specs=in_specs, out_specs=out_specs, check_vma=False)
```
